32 devices in a mesh: segment: 2 (over x), dp: 16 (over z, y, core).
Axes of the slice: x: 2, y: 2, z: 4, core: 2. Of those that a mesh axis runs over, the one named last changes fastest.
Arguments:
- patches: bfloat16 [32, 1024, 768], P(('segment', 'dp')), may hold values from -6 to 6
- lengths: int32 [32], replicated, may hold values from 576 to 1024, as said below
- keep_order: int32 [32, 1024], replicated, may hold values from 0 to 1023, as said below
- e_vectors: float32 [8, 768], P(None, ('segment', 'dp')), may hold values from -1.75 to 1.75
- e_qkv: float32 [768, 2304], P(('segment', 'dp')), may hold values from -0.21875 to 0.21875
- e_proj: float32 [768, 768], P(('segment', 'dp')), may hold values from -1.75 to 1.75
- e_fc1: float32 [768, 3072], P(('segment', 'dp')), may hold values from -0.21875 to 0.21875
- e_fc1_bias: float32 [3072], P(('segment', 'dp')), may hold values from -1.75 to 1.75
- e_fc2: float32 [3072, 768], P(('segment', 'dp')), may hold values from -0.109375 to 0.109375
- embed: float32 [768, 512], P(('segment', 'dp')), may hold values from -0.21875 to 0.21875
- d_vectors: float32 [10, 512], P(None, ('segment', 'dp')), may hold values from -1.75 to 1.75
- dec_pos: float32 [1024, 512], P(None, ('segment', 'dp')), may hold values from -6 to 6
- d_qkv: float32 [512, 1536], P(('segment', 'dp')), may hold values from -0.25 to 0.25
- d_proj: float32 [512, 512], P(('segment', 'dp')), may hold values from -6 to 6
- d_fc1: float32 [512, 2048], P(('segment', 'dp')), may hold values from -0.25 to 0.25
- d_fc1_bias: float32 [2048], P(('segment', 'dp')), may hold values from -1.75 to 1.75
- d_fc2: float32 [2048, 512], P(('segment', 'dp')), may hold values from -0.125 to 0.125
- cotangent: bfloat16 [32, 1024, 512], P(('segment', 'dp')), may hold values from -12 to 12
Outputs:
- decoded: bfloat16 [32, 1024, 512], P(('segment', 'dp'))
- patches_grad: float32 [32, 1024, 768], P(('segment', 'dp'))
- e_vectors_grad: float32 [8, 768], P(None, ('segment', 'dp'))
- e_qkv_grad: float32 [768, 2304], P(('segment', 'dp'))
- e_proj_grad: float32 [768, 768], P(('segment', 'dp'))
- e_fc1_grad: float32 [768, 3072], P(('segment', 'dp'))
- e_fc1_bias_grad: float32 [3072], P(('segment', 'dp'))
- e_fc2_grad: float32 [3072, 768], P(('segment', 'dp'))
- embed_grad: float32 [768, 512], P(('segment', 'dp'))
- d_vectors_grad: float32 [10, 512], P(None, ('segment', 'dp'))
- dec_pos_grad: float32 [1024, 512], P(None, ('segment', 'dp'))
- d_qkv_grad: float32 [512, 1536], P(('segment', 'dp'))
- d_proj_grad: float32 [512, 512], P(('segment', 'dp'))
- d_fc1_grad: float32 [512, 2048], P(('segment', 'dp'))
- d_fc1_bias_grad: float32 [2048], P(('segment', 'dp'))
- d_fc2_grad: float32 [2048, 512], P(('segment', 'dp'))
The draws below stay inside these ranges and needn't reach their ends.
Inputs may be any that keep to these rules, and one draw needn't show every extreme that they name: Each cube holds either 576 or 1024 tokens; both lengths occur. `keep_order`: for a cube of n tokens the first n entries are a permutation of 0 to n - 1 and the others are n to 1023 in order; the visible tokens are the first n // 10 entries.
All inputs are finite; a program needn't handle non-finite values.
Results may differ from the reference program's by a relative error of at most 0.017.
Values may be sent and summed in bfloat16 or wider, within the bound.
A program may use at most 384 MiB of HBM per device.

```python
import jax
import jax.numpy as jnp
from jax import lax

HEADS_E = 12
DE = 768
FE = 3072
HEADS_D = 16
DD = 512
FD = 2048
LMAX = 1024
SHORT = 576
VIS = 104
CUBES = 32


def cube_lengths(key):
    chosen = jax.random.randint(key, (CUBES,), 0, 2)
    sizes = jnp.where(chosen == 1, LMAX, SHORT).astype(jnp.int32)
    return sizes.at[0].set(LMAX).at[1].set(SHORT)


def draw_lengths(key, part):
    return cube_lengths(key)


def draw_keep_order(key, part):
    sizes = cube_lengths(key)
    key = jax.random.fold_in(key, 7)
    cube_keys = jax.random.split(key, CUBES)
    shuffled = jax.vmap(lambda sub_key: jax.random.permutation(sub_key, LMAX))(cube_keys).astype(jnp.int32)
    slots = jnp.arange(LMAX, dtype=jnp.int32)
    ranks = jnp.where(slots[None, :] < sizes[:, None], shuffled, LMAX + slots[None, :])
    return jnp.argsort(ranks, axis=1, stable=True).astype(jnp.int32)


def strengthened(drawn, rng, source, target, parts, factor):
    owner, partner = [(jnp.arange(drawn.shape[position]) // (drawn.shape[position] // parts)).reshape([-1 if axis == position else 1 for axis in range(drawn.ndim)]) for position in (source, target)]
    chosen = jax.random.permutation(rng, parts)[partner]
    strong = (owner == chosen) | (owner == (partner + parts // 2) % parts)
    return jnp.where(strong, factor * drawn, drawn)


def block_levels(own_key, shape, cuts, least, high):
    level, own = 1.0, jax.random.fold_in(own_key, 6)
    for position, parts in cuts:
        steps = jnp.exp(jax.random.uniform(jax.random.fold_in(own, position), (parts,), jnp.float32, least / len(cuts), high / len(cuts)))
        level = level * jnp.repeat(steps, shape[position] // parts).reshape([-1 if axis == position else 1 for axis in range(len(shape))])
    return level


def scatter_about(own_key, shape, deviation, most, shards=(), kind=jnp.bfloat16):
    level = block_levels(own_key, shape, shards, -0.22, 0.18) if shards else 1.0
    drawn = jax.random.normal(own_key, shape, jnp.float32) * deviation * level
    return jnp.minimum(jnp.maximum(drawn, -most), most).astype(kind)


def bell_draw_with(key, shape, scale, limit, shards, heavy, kind=jnp.bfloat16):
    drawn = scale * jax.random.normal(key, shape, jnp.float32)
    if shards:
        drawn = drawn * block_levels(key, shape, shards, -0.22, 0.18)
    return jnp.clip(strengthened(drawn, jax.random.fold_in(key, 3), *heavy), -limit, limit).astype(kind)


def setup_inputs(seed: int = 0) -> dict:
    keys = jax.random.split(jax.random.key(seed), 19)
    patches = scatter_about(keys[0], (CUBES, LMAX, DE), 1.0, 6.0, ((0, 32),))
    lengths = draw_lengths(jax.random.fold_in(keys[18], 71), 0)
    keep_order = draw_keep_order(jax.random.fold_in(keys[18], 71), 0)
    e_vectors = scatter_about(keys[3], (8, DE), 0.3, 1.75, ((1, 32),), jnp.float32)
    e_qkv = scatter_about(keys[4], (DE, 3 * DE), DE ** -0.5, 0.21875, ((0, 32),), jnp.float32)
    e_proj = scatter_about(keys[5], (DE, DE), (max(DE // 64, 1)) ** -0.5, 1.75, ((0, 32),), jnp.float32)
    e_fc1 = scatter_about(keys[6], (DE, FE), DE ** -0.5, 0.21875, ((0, 32),), jnp.float32)
    e_fc1_bias = scatter_about(keys[7], (FE,), 0.3, 1.75, ((0, 32),), jnp.float32)
    e_fc2 = scatter_about(keys[8], (FE, DE), FE ** -0.5, 0.109375, ((0, 32),), jnp.float32)
    embed = scatter_about(keys[9], (DE, DD), DE ** -0.5, 0.21875, ((0, 32),), jnp.float32)
    d_vectors = scatter_about(keys[10], (10, DD), 0.3, 1.75, ((1, 32),), jnp.float32)
    dec_pos = scatter_about(keys[11], (LMAX, DD), 1.0, 6.0, ((1, 32),), jnp.float32)
    d_qkv = scatter_about(keys[12], (DD, 3 * DD), DD ** -0.5, 0.25, ((0, 32),), jnp.float32)
    d_proj = scatter_about(keys[13], (DD, DD), (max(DD // 512, 1)) ** -0.5, 6.0, ((0, 32),), jnp.float32)
    d_fc1 = scatter_about(keys[14], (DD, FD), DD ** -0.5, 0.25, ((0, 32),), jnp.float32)
    d_fc1_bias = scatter_about(keys[15], (FD,), 0.3, 1.75, ((0, 32),), jnp.float32)
    d_fc2 = scatter_about(keys[16], (FD, DD), FD ** -0.5, 0.125, ((0, 32),), jnp.float32)
    cotangent = bell_draw_with(keys[17], (CUBES, LMAX, DD), 1.0, 12.0, ((0, 32),), (0, 2, 32, 2.75))
    return dict(patches=patches, lengths=lengths, keep_order=keep_order, e_vectors=e_vectors, e_qkv=e_qkv, e_proj=e_proj, e_fc1=e_fc1, e_fc1_bias=e_fc1_bias, e_fc2=e_fc2, embed=embed, d_vectors=d_vectors, dec_pos=dec_pos, d_qkv=d_qkv, d_proj=d_proj, d_fc1=d_fc1, d_fc1_bias=d_fc1_bias, d_fc2=d_fc2, cotangent=cotangent)


@jax.custom_vjp
def low(v):
    return lax.optimization_barrier(v.astype(jnp.bfloat16)).astype(jnp.float32)

@jax.custom_vjp
def low_back(v):
    return v

def low_keep(v):
    return (low(v), None)

def low_pass(kept, grad):
    return (grad,)

def back_keep(v):
    return (v, None)

def back_low(kept, grad):
    return (low(grad),)
low.defvjp(low_keep, low_pass)
low_back.defvjp(back_keep, back_low)
norm_eps = 1e-06
far_below = -1e+30

def round_both(values):
    return low(low_back(values))

def norm_rows(values, gain, shift):
    center = values - lax.optimization_barrier(jnp.mean(values, axis=-1, keepdims=True))
    spread = lax.optimization_barrier(jnp.mean(center * center, axis=-1, keepdims=True))
    return center * lax.rsqrt(spread + norm_eps) * (1.0 + gain) + shift

def attend(queries, key_rows, value_rows, live, heads):
    total_rows, width = queries.shape
    head_size = width // heads
    block_rows = min(512, total_rows)
    scale = head_size ** (-0.5)
    q_heads = queries.reshape(total_rows, heads, head_size)
    k_heads = key_rows.reshape(total_rows, heads, head_size)
    v_heads = value_rows.reshape(total_rows, heads, head_size)
    starts = jnp.arange(total_rows // block_rows, dtype=jnp.int32) * block_rows

    def one_block(start):
        q_block = lax.dynamic_slice_in_dim(q_heads, start, block_rows, 0)
        scores = jnp.einsum('qhd,khd->hqk', q_block, k_heads, precision=lax.Precision.HIGHEST) * scale
        scores = low_back(scores)
        scores = jnp.where(live[None, None, :], scores, far_below)
        probs = low(jax.nn.softmax(scores, axis=-1))
        return jnp.einsum('hqk,khd->qhd', probs, v_heads, precision=lax.Precision.HIGHEST)
    mixed = lax.map(jax.checkpoint(one_block), starts)
    return mixed.reshape(total_rows, width)

def block(inputs, live, weights, heads):
    vectors, qkv_weight, out_weight, up_weight, up_bias, down_weight = weights
    width = inputs.shape[1]
    normed = low(norm_rows(inputs, vectors[0], vectors[1]))
    joined = jnp.dot(normed, qkv_weight, precision=lax.Precision.HIGHEST)
    queries = round_both(joined[:, :width] + vectors[4])
    key_rows = round_both(joined[:, width:2 * width])
    value_rows = round_both(joined[:, 2 * width:] + vectors[5])
    attended = round_both(attend(queries, key_rows, value_rows, live, heads))
    branch = low_back(jnp.dot(attended, out_weight, precision=lax.Precision.HIGHEST) + vectors[6])
    middle = inputs + branch
    normed_two = low(norm_rows(middle, vectors[2], vectors[3]))
    hidden = low_back(jnp.dot(normed_two, up_weight, precision=lax.Precision.HIGHEST) + up_bias)
    active = low(jax.nn.gelu(hidden, approximate=False))
    second = low_back(jnp.dot(active, down_weight, precision=lax.Precision.HIGHEST) + vectors[7])
    return middle + second

def one_cube(weights, patch, length, order):
    enc_weights = weights[:6]
    embed_weight = weights[6]
    dec_vectors = weights[7]
    positions = weights[8]
    dec_block = (weights[7],) + tuple(weights[9:])
    visible = length // 10
    keep = jnp.arange(VIS) < visible
    places = order[:VIS].astype(jnp.int32)
    inputs = jnp.where(keep[:, None], patch[places], 0.0)
    encoded = round_both(block(inputs, keep, enc_weights, HEADS_E))
    embedded = low_back(jnp.dot(encoded, embed_weight, precision=lax.Precision.HIGHEST) + dec_vectors[8])
    target = jnp.where(keep, places, LMAX).astype(jnp.int32)
    filled = jnp.broadcast_to(dec_vectors[9], (LMAX, dec_vectors.shape[1]))
    filled = filled.at[target].set(embedded, mode='drop')
    live = jnp.arange(LMAX) < length
    result = block(filled + positions, live, dec_block, HEADS_D)
    return jnp.where(live[:, None], result, 0.0)

def reference(patches, lengths, keep_order, e_vectors, e_qkv, e_proj, e_fc1, e_fc1_bias, e_fc2, embed, d_vectors, dec_pos, d_qkv, d_proj, d_fc1, d_fc1_bias, d_fc2, cotangent):
    masters = (e_vectors, e_qkv, e_proj, e_fc1, e_fc1_bias, e_fc2, embed, d_vectors, dec_pos, d_qkv, d_proj, d_fc1, d_fc1_bias, d_fc2)

    def forward(patch_values, weights):
        lowered = tuple((low(weight) for weight in weights))

        def step(carry, item):
            patch, length, order = item
            return (carry, jax.checkpoint(one_cube)(lowered, patch, length, order))
        unused, results = lax.scan(step, jnp.zeros((), jnp.float32), (patch_values, lengths, keep_order))
        return results
    decoded, pull = jax.vjp(forward, patches.astype(jnp.float32), masters)
    patch_grad, grads = pull(cotangent.astype(jnp.float32))
    return (decoded.astype(jnp.bfloat16), patch_grad, grads[0], grads[1], grads[2], grads[3], grads[4], grads[5], grads[6], grads[7], grads[8], grads[9], grads[10], grads[11], grads[12], grads[13])
```

```python
import functools
import math

import jax
import jax.numpy as jnp
from jax import lax
from jax.experimental import pallas as pl
from jax.experimental.pallas import tpu as pltpu
from jax.sharding import PartitionSpec as P

HEADS_E = 12
HEADS_D = 16
VIS = 104
SHORT = 576
HD = 32
GROUP = 128
F32 = jnp.float32
BF16 = jnp.bfloat16
AXES = ("segment", "dp")
MESH = pl.DeviceIdType.MESH
NORM_EPS = 1e-06
FAR_BELOW = -1e30


def place():
    s = lax.axis_index("segment")
    dp = lax.axis_index("dp")
    return s, dp // 4, (dp // 2) % 2, dp % 2


def device(s, z, y, c):
    return (s, (z * 2 + y) * 2 + c)


def halves(columns):
    return (columns // 2, columns // 2) if columns % 256 == 0 else (columns, 0)


def greet(peers):
    barrier = pltpu.get_barrier_semaphore()
    for peer in peers:
        pl.semaphore_signal(barrier, inc=1, device_id=peer, device_id_type=MESH)
    pl.semaphore_wait(barrier, len(peers))


def send(src, dst, send_sem, recv_sem, target):
    copy = pltpu.make_async_remote_copy(
        src_ref=src,
        dst_ref=dst,
        send_sem=send_sem,
        recv_sem=recv_sem,
        device_id=target,
        device_id_type=MESH,
    )
    copy.start()
    return copy


def gather_kernel(n, Z, *refs):
    ins, outs = refs[:n], refs[n : 2 * n]
    loc, zs, zr, ms, mr, cs, cr = refs[2 * n :]
    s, z, y, c = place()
    X, Y, C = device(1 - s, z, y, c), device(s, z, 1 - y, c), device(s, z, y, 1 - c)
    z_peers = [device(s, lax.rem(z + d, Z), y, c) for d in range(1, Z)]
    greet(z_peers + [X, Y, C])
    state = {}
    sends = []

    def both(ref, i, sems, k, target):
        copy = send(ref, ref, sems[0].at[i, k], sems[1].at[i, k], target)
        sends.append(copy)
        return copy

    def stage0(i):
        own = pltpu.make_async_copy(ins[i], outs[i].at[s, z, y, c], loc.at[i])
        own.start()
        copies = [
            send(ins[i], outs[i].at[s, z, y, c], zs.at[i, d], zr.at[i, d], z_peers[d])
            for d in range(Z - 1)
        ]
        sends.extend(copies)
        state[i, 0] = (own, copies)

    def stage1(i):
        own, copies = state[i, 0]
        own.wait()
        for copy in copies:
            copy.wait_recv()
        o = outs[i]
        ka, kb = halves(o.shape[-1])
        A, B = pl.ds(0, ka), pl.ds(ka, kb)
        state[i, 1] = [both(o.at[s, :, y, c, :, A], i, (ms, mr), 0, X)]
        if kb:
            state[i, 1].append(both(o.at[s, :, y, c, :, B], i, (ms, mr), 1, Y))
        state[i, 9] = [both(o.at[s, :, y, c], i, (cs, cr), 0, C)]

    def stage2(i):
        for copy in state[i, 1]:
            copy.wait_recv()
        o = outs[i]
        ka, kb = halves(o.shape[-1])
        A, B = pl.ds(0, ka), pl.ds(ka, kb)
        state[i, 2] = [both(o.at[:, :, y, c, :, A], i, (ms, mr), 2, Y)]
        state[i, 9].append(both(o.at[1 - s, :, y, c, :, A], i, (cs, cr), 1, C))
        if kb:
            state[i, 2].append(both(o.at[s, :, :, c, :, B], i, (ms, mr), 3, X))
            state[i, 9].append(both(o.at[s, :, 1 - y, c, :, B], i, (cs, cr), 2, C))

    def stage3(i):
        for copy in state[i, 2]:
            copy.wait_recv()
        o = outs[i]
        ka, kb = halves(o.shape[-1])
        A, B = pl.ds(0, ka), pl.ds(ka, kb)
        state[i, 9].append(both(o.at[:, :, 1 - y, c, :, A], i, (cs, cr), 3, C))
        if kb:
            state[i, 9].append(both(o.at[1 - s, :, :, c, :, B], i, (cs, cr), 4, C))

    stages = (stage0, stage1, stage2, stage3)
    for t in range(n + 3):
        for k in range(4):
            if 0 <= t - k < n:
                stages[k](t - k)
    for i in range(n):
        for copy in state[i, 9]:
            copy.wait_recv()
    for copy in sends:
        copy.wait_send()


def gather_all(arrays, Z):
    n = len(arrays)
    D = pltpu.SemaphoreType.DMA
    return pl.pallas_call(
        functools.partial(gather_kernel, n, Z),
        out_shape=[jax.ShapeDtypeStruct((2, Z, 2, 2) + a.shape, a.dtype) for a in arrays],
        in_specs=[pl.BlockSpec(memory_space=pl.ANY)] * n,
        out_specs=[pl.BlockSpec(memory_space=pl.ANY)] * n,
        scratch_shapes=[
            D((n,)),
            D((n, Z - 1)),
            D((n, Z - 1)),
            D((n, 4)),
            D((n, 4)),
            D((n, 5)),
            D((n, 5)),
        ],
        compiler_params=pltpu.CompilerParams(collective_id=0, has_side_effects=True),
    )(*arrays)


def scatter_kernel(n, Z, *refs):
    ins, outs = refs[:n], refs[n : 2 * n]
    L0, R0, R1A, R1B, R2A, R2B, R3 = [refs[(2 + i) * n : (3 + i) * n] for i in range(7)]
    loc, cs, cr, ms, mr, zs, zr = refs[9 * n :]
    s, z, y, c = place()
    X, Y, C = device(1 - s, z, y, c), device(s, z, 1 - y, c), device(s, z, y, 1 - c)
    z_peers = [device(s, lax.rem(z + d, Z), y, c) for d in range(1, Z)]
    greet(z_peers + [X, Y, C])
    state = {}
    sends = []

    def ship(src, dst, ss, rs, target):
        copy = send(src, dst, ss, rs, target)
        sends.append(copy)
        return copy

    def total(a, b):
        return (a.astype(F32) + b.astype(F32)).astype(BF16)

    def stage0(i):
        own = pltpu.make_async_copy(ins[i].at[:, :, :, c], L0[i], loc.at[i])
        own.start()
        state[i, 0] = (own, ship(ins[i].at[:, :, :, 1 - c], R0[i], cs.at[i], cr.at[i], C))

    def stage1(i):
        own, copy = state[i, 0]
        own.wait()
        copy.wait_recv()
        ka, kb = halves(ins[i].shape[-1])

        def add(t, _):
            at = (t // (Z * 2), (t // 2) % Z, t % 2)
            L0[i][at] = total(L0[i][at], R0[i][at])
            return 0

        lax.fori_loop(0, 4 * Z, add, 0)
        A, B = pl.ds(0, ka), pl.ds(ka, kb)
        state[i, 1] = [ship(L0[i].at[:, :, 1 - y, :, A], R1A[i], ms.at[i, 0], mr.at[i, 0], Y)]
        if kb:
            state[i, 1].append(
                ship(L0[i].at[1 - s, :, :, :, B], R1B[i], ms.at[i, 1], mr.at[i, 1], X)
            )

    def stage2(i):
        for copy in state[i, 1]:
            copy.wait_recv()
        ka, kb = halves(ins[i].shape[-1])
        A, B = slice(0, ka), slice(ka, ka + kb)

        def add(t, _):
            u, zz = t // Z, t % Z
            L0[i][u, zz, y, :, A] = total(L0[i][u, zz, y, :, A], R1A[i][u, zz])
            if kb:
                L0[i][s, zz, u, :, B] = total(L0[i][s, zz, u, :, B], R1B[i][zz, u])
            return 0

        lax.fori_loop(0, 2 * Z, add, 0)
        A, B = pl.ds(0, ka), pl.ds(ka, kb)
        state[i, 2] = [ship(L0[i].at[1 - s, :, y, :, A], R2A[i], ms.at[i, 2], mr.at[i, 2], X)]
        if kb:
            state[i, 2].append(
                ship(L0[i].at[s, :, 1 - y, :, B], R2B[i], ms.at[i, 3], mr.at[i, 3], Y)
            )

    def stage3(i):
        for copy in state[i, 2]:
            copy.wait_recv()
        ka, kb = halves(ins[i].shape[-1])
        A, B = slice(0, ka), slice(ka, ka + kb)

        def add(zz, _):
            L0[i][s, zz, y, :, A] = total(L0[i][s, zz, y, :, A], R2A[i][zz])
            if kb:
                L0[i][s, zz, y, :, B] = total(L0[i][s, zz, y, :, B], R2B[i][zz])
            return 0

        lax.fori_loop(0, Z, add, 0)
        state[i, 3] = [
            ship(
                L0[i].at[s, lax.rem(z + d, Z), y],
                R3[i].at[d - 1],
                zs.at[i, d - 1],
                zr.at[i, d - 1],
                z_peers[d - 1],
            )
            for d in range(1, Z)
        ]

    def stage4(i):
        for copy in state[i, 3]:
            copy.wait_recv()
        acc = L0[i][s, z, y].astype(F32)
        for d in range(1, Z):
            acc = acc + R3[i][d - 1].astype(F32)
        outs[i][...] = acc

    stages = (stage0, stage1, stage2, stage3, stage4)
    for t in range(n + 4):
        for k in range(5):
            if 0 <= t - k < n:
                stages[k](t - k)
    for copy in sends:
        copy.wait_send()


def scatter_all(arrays, Z):
    n = len(arrays)
    D = pltpu.SemaphoreType.DMA

    def buffers(shape_of):
        return [pltpu.VMEM(shape_of(*a.shape[4:]), BF16) for a in arrays]

    def half(columns, k):
        return max(halves(columns)[k], 128)

    return pl.pallas_call(
        functools.partial(scatter_kernel, n, Z),
        out_shape=[jax.ShapeDtypeStruct(a.shape[4:], F32) for a in arrays],
        in_specs=[pl.BlockSpec(memory_space=pl.ANY)] * n,
        out_specs=[pl.BlockSpec(memory_space=pltpu.VMEM)] * n,
        scratch_shapes=buffers(lambda r, k: (2, Z, 2, r, k))
        + buffers(lambda r, k: (2, Z, 2, r, k))
        + buffers(lambda r, k: (2, Z, r, half(k, 0)))
        + buffers(lambda r, k: (Z, 2, r, half(k, 1)))
        + buffers(lambda r, k: (Z, r, half(k, 0)))
        + buffers(lambda r, k: (Z, r, half(k, 1)))
        + buffers(lambda r, k: (Z - 1, r, k))
        + [D((n,)), D((n,)), D((n,)), D((n, 4)), D((n, 4)), D((n, Z - 1)), D((n, Z - 1))],
        compiler_params=pltpu.CompilerParams(
            collective_id=1, has_side_effects=True, vmem_limit_bytes=60 * 2**20
        ),
    )(*arrays)


def head_rows(block, j):
    parts = []
    if j > 0:
        parts.append(jnp.zeros((HD * j, block.shape[1]), block.dtype))
    parts.append(block[HD * j : HD * (j + 1)])
    if j < 3:
        parts.append(jnp.zeros((HD * (3 - j), block.shape[1]), block.dtype))
    return jnp.concatenate(parts, 0)


def head_lanes(block, j):
    lane = lax.broadcasted_iota(jnp.int32, block.shape, 1)
    return jnp.where((lane >= HD * j) & (lane < HD * (j + 1)), block, jnp.zeros_like(block))


def attend_kernel(bias_ref, k_ref, vT_ref, qT_ref, oT_ref, L_ref):
    k = k_ref[...]
    for j in range(4):
        rows = slice(HD * j, HD * (j + 1))
        s = jnp.dot(k, head_rows(qT_ref[...], j), preferred_element_type=F32)
        s = jnp.concatenate([s[:SHORT], s[SHORT:] + bias_ref[...]], 0)
        m = jnp.max(s, axis=0, keepdims=True)
        p = jnp.exp2(s - m)
        total = jnp.sum(p, axis=0, keepdims=True)
        o = jnp.dot(vT_ref[rows, :], p.astype(BF16), preferred_element_type=F32)
        oT_ref[rows, :] = (o * (1.0 / total)).astype(BF16)
        L_ref[0, j : j + 1, :] = m + jnp.log2(total)


def attend(bias, k, vT, qT):
    n, width = k.shape
    tq = n
    groups = width // GROUP
    return pl.pallas_call(
        attend_kernel,
        out_shape=(
            jax.ShapeDtypeStruct((width, n), BF16),
            jax.ShapeDtypeStruct((groups, 4, n), F32),
        ),
        grid=(groups, n // tq),
        in_specs=[
            pl.BlockSpec((n - SHORT, 1), lambda g, i: (0, 0)),
            pl.BlockSpec((n, GROUP), lambda g, i: (0, g)),
            pl.BlockSpec((GROUP, n), lambda g, i: (g, 0)),
            pl.BlockSpec((GROUP, tq), lambda g, i: (g, i)),
        ],
        out_specs=(
            pl.BlockSpec((GROUP, tq), lambda g, i: (g, i)),
            pl.BlockSpec((1, 4, tq), lambda g, i: (g, 0, i)),
        ),
        compiler_params=pltpu.CompilerParams(vmem_limit_bytes=48 * 2**20),
    )(bias, k, vT, qT)


def attend_back_kernel(
    steps,
    bias_ref,
    k_ref,
    kT_ref,
    v_ref,
    qT_ref,
    q_ref,
    goT_ref,
    go_ref,
    oT_ref,
    L_ref,
    gqT_ref,
    gk_ref,
    gv_ref,
    ak,
    av,
):
    i = pl.program_id(1)

    @pl.when(i == 0)
    def _():
        ak[...] = jnp.zeros_like(ak)
        av[...] = jnp.zeros_like(av)

    k = k_ref[...]
    v = v_ref[...]
    for j in range(4):
        rows = slice(HD * j, HD * (j + 1))
        s = jnp.dot(k, head_rows(qT_ref[...], j), preferred_element_type=F32)
        s = jnp.concatenate([s[:SHORT], s[SHORT:] + bias_ref[...]], 0)
        p = jnp.exp2(s - L_ref[0, j : j + 1, :])
        gp = jnp.dot(v, head_rows(goT_ref[...], j), preferred_element_type=F32)
        inner = jnp.sum(
            goT_ref[rows, :].astype(F32) * oT_ref[rows, :].astype(F32), axis=0, keepdims=True
        )
        gs = (p * (gp - inner)).astype(BF16)
        av[...] += jnp.dot(
            p.astype(BF16), head_lanes(go_ref[...], j), preferred_element_type=F32
        )
        ak[...] += jnp.dot(gs, head_lanes(q_ref[...], j), preferred_element_type=F32)
        gq = jnp.dot(kT_ref[rows, :], gs, preferred_element_type=F32)
        gqT_ref[rows, :] = (gq * math.log(2.0)).astype(BF16)

    @pl.when(i == steps - 1)
    def _():
        gk_ref[...] = (ak[...] * HD**-0.5).astype(BF16)
        gv_ref[...] = av[...].astype(BF16)


def attend_back(bias, k, kT, v, qT, q, goT, go, oT, L):
    n, width = k.shape
    tq = n
    groups = width // GROUP
    by_rows = pl.BlockSpec((n, GROUP), lambda g, i: (0, g))
    by_columns = pl.BlockSpec((GROUP, n), lambda g, i: (g, 0))
    query_rows = pl.BlockSpec((tq, GROUP), lambda g, i: (i, g))
    query_columns = pl.BlockSpec((GROUP, tq), lambda g, i: (g, i))
    return pl.pallas_call(
        functools.partial(attend_back_kernel, n // tq),
        out_shape=(
            jax.ShapeDtypeStruct((width, n), BF16),
            jax.ShapeDtypeStruct((n, width), BF16),
            jax.ShapeDtypeStruct((n, width), BF16),
        ),
        grid=(groups, n // tq),
        in_specs=[
            pl.BlockSpec((n - SHORT, 1), lambda g, i: (0, 0)),
            by_rows,
            by_columns,
            by_rows,
            query_columns,
            query_rows,
            query_columns,
            query_rows,
            query_columns,
            pl.BlockSpec((1, 4, tq), lambda g, i: (g, 0, i)),
        ],
        out_specs=(query_columns, by_rows, by_rows),
        scratch_shapes=[pltpu.VMEM((n, GROUP), F32), pltpu.VMEM((n, GROUP), F32)],
        compiler_params=pltpu.CompilerParams(vmem_limit_bytes=48 * 2**20),
    )(bias, k, kT, v, qT, q, goT, go, oT, L)


def mm(spec, a, b):
    return jnp.einsum(spec, a, b, preferred_element_type=F32)


def norm_rows(values, gain, shift):
    center = values - jnp.mean(values, axis=-1, keepdims=True)
    spread = jnp.mean(center * center, axis=-1, keepdims=True)
    return center * lax.rsqrt(spread + NORM_EPS) * (1.0 + gain) + shift


def exact_gelu(values):
    return jax.nn.gelu(values, approximate=False)


def encoder_attend(q, k, v, live):
    heads = lambda m: m.reshape(m.shape[0], HEADS_E, m.shape[1] // HEADS_E)
    scale = (q.shape[1] // HEADS_E) ** -0.5
    s = mm("qhd,khd->hqk", heads(q), heads(k)) * scale
    s = jnp.where(live[None, None, :], s, FAR_BELOW)
    high = jnp.max(s, axis=-1, keepdims=True)
    raised = jnp.exp(s - high)
    p = raised / jnp.sum(raised, axis=-1, keepdims=True)
    o = mm("hqk,khd->qhd", p.astype(BF16), heads(v))
    return o.reshape(q.shape).astype(BF16), p


def encoder_attend_back(kept, go, width):
    q, k, v, p = kept
    heads = lambda m: m.reshape(m.shape[0], HEADS_E, m.shape[1] // HEADS_E)
    scale = (width // HEADS_E) ** -0.5
    g = heads(go)
    gv = mm("hqk,qhd->khd", p.astype(BF16), g)
    gp = mm("qhd,khd->hqk", g, heads(v))
    gs = (p * (gp - jnp.sum(gp * p, axis=-1, keepdims=True))).astype(BF16)
    gq = mm("hqk,khd->qhd", gs, heads(k)) * scale
    gk = mm("hqk,qhd->khd", gs, heads(q)) * scale
    return tuple(m.reshape(q.shape).astype(BF16) for m in (gq, gk, gv))


def decoder_attend(q, k, v, bias):
    scaled = (k * (HD**-0.5 * math.log2(math.e))).astype(BF16)
    q, v = q.astype(BF16), v.astype(BF16)
    oT, L = attend(bias, scaled, v.T, q.T)
    return oT.T, (q, scaled, v, oT, L)


def decoder_attend_back(kept, go, bias):
    q, k, v, oT, L = kept
    gqT, gk, gv = attend_back(bias, k, k.T, v, q.T, q, go.T, go, oT, L)
    return gqT.T, gk, gv


def block_forward(inputs, live, weights, encoder):
    gains, qkv, proj, fc1, fc1_bias, fc2 = weights
    width = inputs.shape[1]
    normed = norm_rows(inputs, gains[0], gains[1]).astype(BF16)
    joined = mm("rd,de->re", normed, qkv)
    q = joined[:, :width] + gains[4]
    k = joined[:, width : 2 * width]
    v = joined[:, 2 * width :] + gains[5]
    if encoder:
        q, k, v = (m.astype(BF16) for m in (q, k, v))
        attended, p = encoder_attend(q, k, v, live)
        kept_attend = (q, k, v, p)
    else:
        attended, kept_attend = decoder_attend(q, k, v, live)
    middle = inputs + (mm("rd,de->re", attended, proj) + gains[6])
    normed_two = norm_rows(middle, gains[2], gains[3]).astype(BF16)
    hidden = mm("rd,df->rf", normed_two, fc1) + fc1_bias
    active = exact_gelu(hidden).astype(BF16)
    result = middle + (mm("rf,fd->rd", active, fc2) + gains[7])
    return result, (inputs, normed, kept_attend, attended, middle, normed_two, hidden, active)


def block_backward(grad_out, kept, weights, bias, encoder):
    gains, qkv, proj, fc1, fc1_bias, fc2 = weights
    inputs, normed, kept_attend, attended, middle, normed_two, hidden, active = kept
    gy = grad_out.astype(BF16)
    g_fc2 = mm("rf,rd->fd", active, gy).astype(BF16)
    unused, gelu_pull = jax.vjp(exact_gelu, hidden)
    gz = gelu_pull(mm("rd,fd->rf", gy, fc2))[0].astype(BF16)
    g_fc1 = mm("rd,rf->df", normed_two, gz).astype(BF16)
    unused, second_pull = jax.vjp(norm_rows, middle, gains[2], gains[3])
    g_middle, g2, g3 = second_pull(mm("rf,df->rd", gz, fc1))
    g_middle = g_middle + grad_out
    ga = g_middle.astype(BF16)
    g_proj = mm("rd,re->de", attended, ga).astype(BF16)
    go = mm("re,de->rd", ga, proj).astype(BF16)
    if encoder:
        gq, gk, gv = encoder_attend_back(kept_attend, go, inputs.shape[1])
    else:
        gq, gk, gv = decoder_attend_back(kept_attend, go, bias)
    joined = jnp.concatenate([gq, gk, gv], axis=1)
    g_qkv = mm("rd,re->de", normed, joined).astype(BF16)
    unused, first_pull = jax.vjp(norm_rows, inputs, gains[0], gains[1])
    g_inputs, g0, g1 = first_pull(mm("re,de->rd", joined, qkv))
    g_inputs = g_inputs + g_middle
    rows = [jnp.sum(m.astype(F32), 0) for m in (gq, gv, ga, gy)]
    g_vectors = jnp.stack([g0, g1, g2, g3] + rows)
    return g_inputs, (g_vectors, g_qkv, g_proj, g_fc1, jnp.sum(gz.astype(F32), 0), g_fc2)


SMALL = 2048


def body(
    patches,
    lengths,
    keep_order,
    e_vectors,
    e_qkv,
    e_proj,
    e_fc1,
    e_fc1_bias,
    e_fc2,
    embed,
    d_vectors,
    dec_pos,
    d_qkv,
    d_proj,
    d_fc1,
    d_fc1_bias,
    d_fc2,
    cotangent,
):
    count = lax.axis_size("segment") * lax.axis_size("dp")
    Z = lax.axis_size("dp") // 4
    device_index = lax.axis_index(AXES)
    small_shards = (e_vectors, e_fc1_bias, d_vectors, d_fc1_bias)
    sizes = [m.size for m in small_shards]
    small = jnp.concatenate([m.reshape(-1) for m in small_shards])
    small = jnp.pad(small, (0, SMALL - small.size)).reshape(SMALL // 128, 128)
    sent = (small, e_qkv, e_proj, e_fc1, e_fc2, embed, dec_pos.T, d_qkv, d_proj, d_fc1, d_fc2)
    full = gather_all([m.astype(BF16) for m in sent], Z)
    small_all = full[0].reshape(count, SMALL).astype(F32)
    parts, start = [], 0
    for size in sizes:
        parts.append(small_all[:, start : start + size])
        start += size

    def by_columns(part, rows):
        return part.reshape(count, rows, -1).transpose(1, 0, 2).reshape(rows, -1)

    e_gains, d_gains = by_columns(parts[0], 8), by_columns(parts[2], 10)
    mats = [m.reshape(-1, m.shape[-1]) for m in full[1:]]
    w_qkv, w_proj, w_fc1, w_fc2, w_embed, posT, dw_qkv, dw_proj, dw_fc1, dw_fc2 = mats
    enc = (e_gains, w_qkv, w_proj, w_fc1, parts[1].reshape(-1), w_fc2)
    dec = (d_gains, dw_qkv, dw_proj, dw_fc1, parts[3].reshape(-1), dw_fc2)

    def run_cube(patch, cotan, length, order):
        slots = patch.shape[0]
        keep = jnp.arange(VIS) < length // 10
        places = order[:VIS]
        spots = jnp.where(keep, places, slots)
        rows_in = jnp.where(keep[:, None], jnp.take(patch, places, axis=0).astype(F32), 0.0)
        encoded, kept_e = block_forward(rows_in, keep, enc, True)
        encoded = encoded.astype(BF16)
        embedded = mm("rd,de->re", encoded, w_embed) + d_gains[8]
        filled = jnp.broadcast_to(d_gains[9], (slots, d_gains.shape[1]))
        filled = filled.at[spots].set(embedded, mode="drop")
        inputs = filled + posT.T.astype(F32)
        live = (jnp.arange(slots) < length)[:, None]
        bias = jnp.where(live[SHORT:], 0.0, FAR_BELOW).astype(F32)
        result, kept_d = block_forward(inputs, bias, dec, False)
        decoded = jnp.where(live, result, 0.0).astype(BF16)
        G = jnp.where(live, cotan.astype(F32), 0.0)
        gxd, dg = block_backward(G, kept_d, dec, bias, False)
        picked = jnp.where(keep[:, None], jnp.take(gxd, places, axis=0), 0.0)
        gemb = picked.astype(BF16)
        g_embed = mm("rd,re->de", encoded, gemb).astype(BF16)
        gencoded = mm("re,de->rd", gemb, w_embed).astype(BF16)
        g_token = jnp.sum(gxd, 0) - jnp.sum(picked, 0)
        d_vec = jnp.concatenate(
            [dg[0], jnp.stack([jnp.sum(gemb.astype(F32), 0), g_token])], 0
        )
        g_rows, eg = block_backward(gencoded.astype(F32), kept_e, enc, None, True)
        g_patch = jnp.zeros((slots, patch.shape[1]), F32).at[spots].set(g_rows, mode="drop")
        return decoded, g_patch, eg, g_embed, d_vec, gxd.T.astype(BF16), dg

    own = patches.shape[0]
    base = device_index * own
    runs = [
        run_cube(patches[i], cotangent[i], lengths[base + i], keep_order[base + i])
        for i in range(own)
    ]
    decoded = jnp.stack([r[0] for r in runs])
    patches_grad = jnp.stack([r[1] for r in runs])
    eg, g_embed, d_vec, g_pos, dg = jax.tree.map(
        lambda *m: functools.reduce(lambda a, b: a + b, m), *[r[2:] for r in runs]
    )

    def to_devices(vector, rows):
        return vector.reshape(rows, count, -1).transpose(1, 0, 2).reshape(count, -1)

    g_small = jnp.concatenate(
        [
            to_devices(eg[0], 8),
            eg[4].reshape(count, -1),
            to_devices(d_vec, 10),
            dg[4].reshape(count, -1),
        ],
        axis=1,
    )
    g_small = jnp.pad(g_small, ((0, 0), (0, SMALL - g_small.shape[1])))
    g_small = g_small.reshape(count, SMALL // 128, 128).astype(BF16)

    def blocks(m):
        return m.reshape((2, Z, 2, 2, -1, m.shape[-1]))

    order = (dg[5], dg[3], dg[2], dg[1], g_pos, g_embed, eg[5], eg[3], eg[2], eg[1], g_small)
    out = scatter_all([blocks(m) for m in order], Z)
    dr_fc2, dr_fc1, dr_proj, dr_qkv, r_pos, r_embed, r_fc2, r_fc1, r_proj, r_qkv, r_small = out
    flat = r_small.reshape(-1)
    parts, start = [], 0
    for shard in small_shards:
        parts.append(flat[start : start + shard.size].reshape(shard.shape))
        start += shard.size
    return (
        decoded,
        patches_grad,
        parts[0],
        r_qkv,
        r_proj,
        r_fc1,
        parts[1],
        r_fc2,
        r_embed,
        parts[2],
        r_pos.T,
        dr_qkv,
        dr_proj,
        dr_fc1,
        parts[3],
        dr_fc2,
    )


def solution(mesh):
    rows, columns, cubes = P(AXES, None), P(None, AXES), P(AXES, None, None)
    weights = (columns, rows, rows, rows, P(AXES), rows, rows, columns, columns)
    weights = weights + (rows, rows, rows, P(AXES), rows)
    return jax.shard_map(
        body,
        mesh=mesh,
        in_specs=(cubes, P(), P()) + weights + (cubes,),
        out_specs=(cubes, cubes) + weights,
        check_vma=False,
    )
```

```python
import functools
import math

import jax
import jax.numpy as jnp
from jax import lax
from jax.experimental import pallas as pl
from jax.experimental.pallas import tpu as pltpu
from jax.sharding import PartitionSpec as P

HEADS_E = 12
HEADS_D = 16
VIS = 104
SHORT = 576
HD = 32
GROUP = 128
F32 = jnp.float32
BF16 = jnp.bfloat16
AXES = ("segment", "dp")
MESH = pl.DeviceIdType.MESH
ROWS_E = 128
NORM_EPS = 1e-06
FAR_BELOW = -1e30


SMALL_ROWS = 32
POS_AT = 5


def place():
    s = lax.axis_index("segment")
    dp = lax.axis_index("dp")
    return s, dp // 4, (dp // 2) % 2, dp % 2


def device(s, z, y, c):
    return (s, (z * 2 + y) * 2 + c)


def halves(columns):
    return (columns // 2, columns // 2) if columns % 256 == 0 else (columns, 0)


def greet(peers):
    barrier = pltpu.get_barrier_semaphore()
    for peer in peers:
        pl.semaphore_signal(barrier, inc=1, device_id=peer, device_id_type=MESH)
    pl.semaphore_wait(barrier, len(peers))


def send(src, dst, send_sem, recv_sem, target):
    copy = pltpu.make_async_remote_copy(
        src_ref=src,
        dst_ref=dst,
        send_sem=send_sem,
        recv_sem=recv_sem,
        device_id=target,
        device_id_type=MESH,
    )
    copy.start()
    return copy


def gather_kernel(n, Z, *refs):
    m = n + 3
    given, outs, ins, shards = refs[:m], refs[m : m + n], refs[m + n : m + 2 * n], refs[m + 2 * n : 2 * m + 2 * n]
    get, loc, zs, zr, ms, mr, cs, cr = refs[2 * m + 2 * n :]
    loads = [pltpu.make_async_copy(given[i], shards[i], get.at[i]) for i in range(m)]
    for load in loads:
        load.start()

    def cast(i):
        if i == 0:
            small = ins[0]
            small[...] = jnp.zeros_like(small)
            for row, k in zip((0, 8, 24, 25), range(4)):
                loads[k].wait()
                ref = shards[k]
                small[row : row + ref.shape[0], : ref.shape[1]] = ref[...].astype(BF16)
        else:
            loads[i + 3].wait()
            ref = shards[i + 3]
            ins[i][...] = (ref[...].T if i == 1 + POS_AT else ref[...]).astype(BF16)

    s, z, y, c = place()
    X, Y, C = device(1 - s, z, y, c), device(s, z, 1 - y, c), device(s, z, y, 1 - c)
    z_peers = [device(s, lax.rem(z + d, Z), y, c) for d in range(1, Z)]
    greet(z_peers + [X, Y, C])
    state = {}
    sends = []

    def both(ref, i, sems, k, target):
        copy = send(ref, ref, sems[0].at[i, k], sems[1].at[i, k], target)
        sends.append(copy)
        return copy

    def stage0(i):
        cast(i)
        own = pltpu.make_async_copy(ins[i], outs[i].at[s, z, y, c], loc.at[i])
        own.start()
        copies = [
            send(ins[i], outs[i].at[s, z, y, c], zs.at[i, d], zr.at[i, d], z_peers[d])
            for d in range(Z - 1)
        ]
        sends.extend(copies)
        state[i, 0] = (own, copies)

    def stage1(i):
        own, copies = state[i, 0]
        own.wait()
        for copy in copies:
            copy.wait_recv()
        o = outs[i]
        ka, kb = halves(o.shape[-1])
        A, B = pl.ds(0, ka), pl.ds(ka, kb)
        state[i, 1] = [both(o.at[s, :, y, c, :, A], i, (ms, mr), 0, X)]
        if kb:
            state[i, 1].append(both(o.at[s, :, y, c, :, B], i, (ms, mr), 1, Y))
        state[i, 9] = [both(o.at[s, :, y, c], i, (cs, cr), 0, C)]

    def stage2(i):
        for copy in state[i, 1]:
            copy.wait_recv()
        o = outs[i]
        ka, kb = halves(o.shape[-1])
        A, B = pl.ds(0, ka), pl.ds(ka, kb)
        state[i, 2] = [both(o.at[:, :, y, c, :, A], i, (ms, mr), 2, Y)]
        state[i, 9].append(both(o.at[1 - s, :, y, c, :, A], i, (cs, cr), 1, C))
        if kb:
            state[i, 2].append(both(o.at[s, :, :, c, :, B], i, (ms, mr), 3, X))
            state[i, 9].append(both(o.at[s, :, 1 - y, c, :, B], i, (cs, cr), 2, C))

    def stage3(i):
        for copy in state[i, 2]:
            copy.wait_recv()
        o = outs[i]
        ka, kb = halves(o.shape[-1])
        A, B = pl.ds(0, ka), pl.ds(ka, kb)
        state[i, 9].append(both(o.at[:, :, 1 - y, c, :, A], i, (cs, cr), 3, C))
        if kb:
            state[i, 9].append(both(o.at[1 - s, :, :, c, :, B], i, (cs, cr), 4, C))

    stages = (stage0, stage1, stage2, stage3)
    for t in range(n + 3):
        for k in range(4):
            if 0 <= t - k < n:
                stages[k](t - k)
    for i in range(n):
        for copy in state[i, 9]:
            copy.wait_recv()
    for copy in sends:
        copy.wait_send()


def gather_all(small_shards, arrays, Z):
    shapes = [(SMALL_ROWS, 128)] + [a.shape for a in arrays]
    shapes[1 + POS_AT] = shapes[1 + POS_AT][::-1]
    n = len(shapes)
    D = pltpu.SemaphoreType.DMA
    return pl.pallas_call(
        functools.partial(gather_kernel, n, Z),
        out_shape=[jax.ShapeDtypeStruct((2, Z, 2, 2) + s, BF16) for s in shapes],
        in_specs=[pl.BlockSpec(memory_space=pl.ANY)] * (n + 3),
        out_specs=[pl.BlockSpec(memory_space=pl.ANY)] * n,
        scratch_shapes=[pltpu.VMEM(s, BF16) for s in shapes]
        + [pltpu.VMEM(a.shape, F32) for a in (*small_shards, *arrays)]
        + [
            D((n + 3,)),
            D((n,)),
            D((n, Z - 1)),
            D((n, Z - 1)),
            D((n, 4)),
            D((n, 4)),
            D((n, 5)),
            D((n, 5)),
        ],
        compiler_params=pltpu.CompilerParams(
            collective_id=0, has_side_effects=True, vmem_limit_bytes=60 * 2**20
        ),
    )(*small_shards, *arrays)


def scatter_kernel(n, Z, *refs):
    ins, outs = refs[:n], refs[n : 2 * n]
    L0, R0, R1A, R1B, R2A, R2B = [refs[(2 + i) * n : (3 + i) * n] for i in range(6)]
    loc, cs, cr, ms, mr, zs, zr = refs[8 * n :]
    s, z, y, c = place()
    X, Y, C = device(1 - s, z, y, c), device(s, z, 1 - y, c), device(s, z, y, 1 - c)
    z_peers = [device(s, lax.rem(z + d, Z), y, c) for d in range(1, Z)]
    greet(z_peers + [X, Y, C])
    state = {}
    sends = []

    def ship(src, dst, ss, rs, target):
        copy = send(src, dst, ss, rs, target)
        sends.append(copy)
        return copy

    def total(a, b):
        return (a.astype(F32) + b.astype(F32)).astype(BF16)

    def stage0(i):
        own = pltpu.make_async_copy(ins[i].at[:, :, :, c], L0[i], loc.at[i])
        own.start()
        state[i, 0] = (own, ship(ins[i].at[:, :, :, 1 - c], R0[i], cs.at[i], cr.at[i], C))

    def stage1(i):
        own, copy = state[i, 0]
        own.wait()
        copy.wait_recv()
        ka, kb = halves(ins[i].shape[-1])

        def add(t, _):
            at = (t // (Z * 2), (t // 2) % Z, t % 2)
            L0[i][at] = total(L0[i][at], R0[i][at])
            return 0

        lax.fori_loop(0, 4 * Z, add, 0)
        A, B = pl.ds(0, ka), pl.ds(ka, kb)
        state[i, 1] = [ship(L0[i].at[:, :, 1 - y, :, A], R1A[i], ms.at[i, 0], mr.at[i, 0], Y)]
        if kb:
            state[i, 1].append(
                ship(L0[i].at[1 - s, :, :, :, B], R1B[i], ms.at[i, 1], mr.at[i, 1], X)
            )

    def stage2(i):
        for copy in state[i, 1]:
            copy.wait_recv()
        ka, kb = halves(ins[i].shape[-1])
        A, B = slice(0, ka), slice(ka, ka + kb)

        def add(t, _):
            u, zz = t // Z, t % Z
            L0[i][u, zz, y, :, A] = total(L0[i][u, zz, y, :, A], R1A[i][u, zz])
            if kb:
                L0[i][s, zz, u, :, B] = total(L0[i][s, zz, u, :, B], R1B[i][zz, u])
            return 0

        lax.fori_loop(0, 2 * Z, add, 0)
        A, B = pl.ds(0, ka), pl.ds(ka, kb)
        state[i, 2] = [ship(L0[i].at[1 - s, :, y, :, A], R2A[i], ms.at[i, 2], mr.at[i, 2], X)]
        if kb:
            state[i, 2].append(
                ship(L0[i].at[s, :, 1 - y, :, B], R2B[i], ms.at[i, 3], mr.at[i, 3], Y)
            )

    def stage3(i):
        for copy in state[i, 2]:
            copy.wait_recv()
        ka, kb = halves(ins[i].shape[-1])
        A, B = slice(0, ka), slice(ka, ka + kb)

        def add(zz, _):
            L0[i][s, zz, y, :, A] = total(L0[i][s, zz, y, :, A], R2A[i][zz])
            if kb:
                L0[i][s, zz, y, :, B] = total(L0[i][s, zz, y, :, B], R2B[i][zz])
            return 0

        lax.fori_loop(0, Z, add, 0)
        state[i, 3] = [
            ship(
                L0[i].at[s, lax.rem(z + d, Z), y],
                outs[i].at[d],
                zs.at[i, d - 1],
                zr.at[i, d - 1],
                z_peers[d - 1],
            )
            for d in range(1, Z)
        ]

    def stage4(i):
        for copy in state[i, 3]:
            copy.wait_recv()
        outs[i][0] = L0[i][s, z, y]

    stages = (stage0, stage1, stage2, stage3, stage4)
    for t in range(n + 4):
        for k in range(5):
            if 0 <= t - k < n:
                stages[k](t - k)
    for copy in sends:
        copy.wait_send()


def scatter_all(arrays, Z):
    n = len(arrays)
    D = pltpu.SemaphoreType.DMA

    def buffers(shape_of):
        return [pltpu.VMEM(shape_of(*a.shape[4:]), BF16) for a in arrays]

    def half(columns, k):
        return max(halves(columns)[k], 128)

    return pl.pallas_call(
        functools.partial(scatter_kernel, n, Z),
        out_shape=[jax.ShapeDtypeStruct((Z,) + a.shape[4:], BF16) for a in arrays],
        in_specs=[pl.BlockSpec(memory_space=pl.ANY)] * n,
        out_specs=[pl.BlockSpec(memory_space=pltpu.VMEM)] * n,
        scratch_shapes=buffers(lambda r, k: (2, Z, 2, r, k))
        + buffers(lambda r, k: (2, Z, 2, r, k))
        + buffers(lambda r, k: (2, Z, r, half(k, 0)))
        + buffers(lambda r, k: (Z, 2, r, half(k, 1)))
        + buffers(lambda r, k: (Z, r, half(k, 0)))
        + buffers(lambda r, k: (Z, r, half(k, 1)))
        + [D((n,)), D((n,)), D((n,)), D((n, 4)), D((n, 4)), D((n, Z - 1)), D((n, Z - 1))],
        compiler_params=pltpu.CompilerParams(
            collective_id=1, has_side_effects=True, vmem_limit_bytes=60 * 2**20
        ),
    )(*arrays)


def nn(a, b): return jnp.dot(a, b, preferred_element_type=F32)
def nt(a, b): return lax.dot_general(a, b, (((1,), (1,)), ((), ())), preferred_element_type=F32)
def tn(a, b): return lax.dot_general(a, b, (((0,), (0,)), ((), ())), preferred_element_type=F32)

def norm_parts(x):
    center = x - jnp.mean(x, axis=-1, keepdims=True)
    r = lax.rsqrt(jnp.mean(center * center, axis=-1, keepdims=True) + NORM_EPS)
    return center * r, r

def norm_back(g, hat, r, gain):
    w = g * (1.0 + gain)
    return r * (w - jnp.mean(w, axis=-1, keepdims=True) - hat * jnp.mean(w * hat, axis=-1, keepdims=True))

def gelu_parts(z):
    x = jnp.abs(z) * math.sqrt(0.5)
    t = 1.0 / (1.0 + 0.3275911 * x)
    e = jnp.exp(-(x * x))
    poly = t * (0.254829592 + t * (-0.284496736 + t * (1.421413741 + t * (-1.453152027 + t * 1.061405429))))
    half = 0.5 * poly * e
    cdf = jnp.where(z > 0, 1.0 - half, half)
    return z * cdf, cdf + z * e * (1.0 / math.sqrt(2.0 * math.pi))

def col_sum(m): return jnp.sum(m, axis=0, keepdims=True)

def pick_matrix(places_row, keep_count, slots):
    pos = lax.broadcasted_iota(jnp.int32, (slots, ROWS_E), 0)
    r = lax.broadcasted_iota(jnp.int32, (slots, ROWS_E), 1)
    return ((pos == places_row) & (r < keep_count)).astype(BF16)

def enc_fwd_kernel(info, places, patches, gains, bias, qkv_h, proj_h, fc1_h, fc2_h,
                   enc_o, x_o, m_o, o_o, x1_o, u_o, dg_o, p_o, qkv, proj, fc1, fc2, sem):
    copies = [pltpu.make_async_copy(h, v, sem.at[i]) for i, (h, v) in enumerate(((qkv_h, qkv), (proj_h, proj), (fc1_h, fc1), (fc2_h, fc2)))]
    for cp in copies: cp.start()
    v = info[0] // 10
    pick = pick_matrix(places[...], v, patches.shape[0])
    x = tn(pick, patches[...])
    x_o[...] = x
    hat, _ = norm_parts(x)
    h = (hat * (1.0 + gains[0:1]) + gains[1:2]).astype(BF16)
    copies[0].wait()
    W = x.shape[1]
    m = nn(h, qkv[...])
    q = (m[:, :W] + gains[4:5]).astype(BF16)
    k = m[:, W:2*W].astype(BF16)
    val = (m[:, 2*W:] + gains[5:6]).astype(BF16)
    m_o[...] = jnp.concatenate([q, k, val], 1)
    live = lax.broadcasted_iota(jnp.int32, (ROWS_E, ROWS_E), 1) < v
    hs = W // HEADS_E
    outs = []
    for j in range(HEADS_E):
        sl = slice(hs*j, hs*(j+1))
        s = jnp.where(live, nt(q[:, sl], k[:, sl]) * hs**-0.5, FAR_BELOW)
        e = jnp.exp(s - jnp.max(s, axis=-1, keepdims=True))
        p = e / jnp.sum(e, axis=-1, keepdims=True)
        p_o[j] = p
        outs.append(nn(p.astype(BF16), val[:, sl]).astype(BF16))
    o = jnp.concatenate(outs, 1)
    o_o[...] = o
    copies[1].wait()
    x1 = x + (nn(o, proj[...]) + gains[6:7])
    x1_o[...] = x1
    hat2, _ = norm_parts(x1)
    h2 = (hat2 * (1.0 + gains[2:3]) + gains[3:4]).astype(BF16)
    copies[2].wait()
    u, dg = gelu_parts(nn(h2, fc1[...]) + bias[...])
    u = u.astype(BF16)
    u_o[...] = u; dg_o[...] = dg
    copies[3].wait()
    enc_o[...] = (x1 + (nn(u, fc2[...]) + gains[7:8])).astype(BF16)

V = pl.BlockSpec(memory_space=pltpu.VMEM); A = pl.BlockSpec(memory_space=pl.ANY); S = pl.BlockSpec(memory_space=pltpu.SMEM)
D = pltpu.SemaphoreType.DMA
def params(mb=56): return pltpu.CompilerParams(vmem_limit_bytes=mb*2**20)

def enc_fwd(info, places, patches, gains, bias, qkv, proj, fc1, fc2):
    W, Fw = fc1.shape
    sd = jax.ShapeDtypeStruct
    return pl.pallas_call(enc_fwd_kernel,
        out_shape=(sd((ROWS_E, W), BF16), sd((ROWS_E, W), F32), sd((ROWS_E, 3*W), BF16), sd((ROWS_E, W), BF16), sd((ROWS_E, W), F32),
                   sd((ROWS_E, Fw), BF16), sd((ROWS_E, Fw), F32), sd((HEADS_E, ROWS_E, ROWS_E), F32)),
        in_specs=[S, V, V, V, V, A, A, A, A], out_specs=(V,)*8,
        scratch_shapes=[pltpu.VMEM(w.shape, BF16) for w in (qkv, proj, fc1, fc2)] + [D((4,))],
        compiler_params=params())(info, places, patches, gains, bias, qkv, proj, fc1, fc2)

def enc_bwd_kernel(info, places, encoded, gemb, embed, gains, x_r, m_r, o_r, x1_r, u_r, dg_r, p_r, qkv_h, proj_h, fc1_h, fc2_h,
                   gp_o, gembed_o, gqkv_o, gproj_o, gfc1_o, gfc2_o, gvec_o, gbias_o,
                   qkv, proj, fc1, fc2, sfc2, sfc1, sproj, sqkv, sem):
    copies = [pltpu.make_async_copy(h, v, sem.at[i]) for i, (h, v) in enumerate(((fc2_h, fc2), (fc1_h, fc1), (proj_h, proj), (qkv_h, qkv)))]
    for cp in copies: cp.start()
    ge = gemb[...]
    gembed_o[...] = tn(encoded[...], ge).astype(BF16)
    gy = nt(ge, embed[...]).astype(BF16)
    G = gy.astype(F32)
    u = u_r[...]
    sfc2[...] = tn(u, gy).astype(BF16)
    w2 = pltpu.make_async_copy(sfc2, gfc2_o, sem.at[4]); w2.start()
    copies[0].wait()
    gz = (nt(gy, fc2[...]) * dg_r[...]).astype(BF16)
    gbias_o[...] = col_sum(gz.astype(F32))
    x1 = x1_r[...]
    hat2, r2 = norm_parts(x1)
    h2 = (hat2 * (1.0 + gains[2:3]) + gains[3:4]).astype(BF16)
    sfc1[...] = tn(h2, gz).astype(BF16)
    w1 = pltpu.make_async_copy(sfc1, gfc1_o, sem.at[5]); w1.start()
    copies[1].wait()
    gh2 = nt(gz, fc1[...])
    gvec_o[2:3, :] = col_sum(gh2 * hat2)
    gvec_o[3:4, :] = col_sum(gh2)
    gx1 = G + norm_back(gh2, hat2, r2, gains[2:3])
    ga = gx1.astype(BF16)
    gvec_o[6:7, :] = col_sum(ga.astype(F32))
    gvec_o[7:8, :] = col_sum(G)
    o = o_r[...]
    sproj[...] = tn(o, ga).astype(BF16)
    wp = pltpu.make_async_copy(sproj, gproj_o, sem.at[6]); wp.start()
    copies[2].wait()
    go = nt(ga, proj[...]).astype(BF16)
    W = x1.shape[1]
    hs = W // HEADS_E
    gq, gk, gv = [], [], []
    for j in range(HEADS_E):
        q = m_r[:, hs*j:hs*(j+1)]; k = m_r[:, W+hs*j:W+hs*(j+1)]; val = m_r[:, 2*W+hs*j:2*W+hs*(j+1)]
        g = go[:, hs*j:hs*(j+1)]
        p = p_r[j]
        gv.append(tn(p.astype(BF16), g).astype(BF16))
        gp = nt(g, val)
        gs = (p * (gp - jnp.sum(gp * p, axis=-1, keepdims=True))).astype(BF16)
        gq.append((nn(gs, k) * hs**-0.5).astype(BF16))
        gk.append((tn(gs, q) * hs**-0.5).astype(BF16))
    gm = jnp.concatenate(gq + gk + gv, 1)
    gvec_o[4:5, :] = col_sum(gm[:, :W].astype(F32))
    gvec_o[5:6, :] = col_sum(gm[:, 2*W:].astype(F32))
    x = x_r[...]
    hat, r = norm_parts(x)
    h = (hat * (1.0 + gains[0:1]) + gains[1:2]).astype(BF16)
    sqkv[...] = tn(h, gm).astype(BF16)
    wq = pltpu.make_async_copy(sqkv, gqkv_o, sem.at[7]); wq.start()
    copies[3].wait()
    gh = nt(gm, qkv[...])
    gvec_o[0:1, :] = col_sum(gh * hat)
    gvec_o[1:2, :] = col_sum(gh)
    gx = gx1 + norm_back(gh, hat, r, gains[0:1])
    pick = pick_matrix(places[...], info[0] // 10, gp_o.shape[0]).astype(F32)
    gp_o[...] = jnp.dot(pick, gx, preferred_element_type=F32, precision=lax.Precision.HIGHEST)
    for cp in (w2, w1, wp, wq): cp.wait()

def enc_bwd(info, places, encoded, gemb, embed, gains, x, m, o, x1, u, dg, p, qkv, proj, fc1, fc2, slots):
    W, Fw = fc1.shape
    sd = jax.ShapeDtypeStruct
    return pl.pallas_call(enc_bwd_kernel,
        out_shape=(sd((slots, W), F32), sd(embed.shape, BF16), sd(qkv.shape, BF16), sd(proj.shape, BF16), sd(fc1.shape, BF16), sd(fc2.shape, BF16), sd((8, W), F32), sd((1, Fw), F32)),
        in_specs=[S] + [V]*12 + [A]*4, out_specs=(V, V, A, A, A, A, V, V),
        scratch_shapes=[pltpu.VMEM(w.shape, BF16) for w in (qkv, proj, fc1, fc2, fc2, fc1, proj, qkv)] + [D((8,))],
        compiler_params=params())(info, places, encoded, gemb, embed, gains, x, m, o, x1, u, dg, p, qkv, proj, fc1, fc2)

def dec_pre_kernel(info, places, encoded, embed, gains, posT, qkv, x_o, q_o, k_o, v_o):
    n = x_o.shape[0]
    i = pl.program_id(0)
    emb = nn(encoded[...], embed[...]) + gains[8:9]
    pos_i = lax.broadcasted_iota(jnp.int32, (n, ROWS_E), 0) + i * n
    r = lax.broadcasted_iota(jnp.int32, (n, ROWS_E), 1)
    pick = ((pos_i == places[...]) & (r < info[0] // 10)).astype(F32)
    seen = jnp.sum(pick, axis=1, keepdims=True)
    placed = jnp.dot(pick, emb, preferred_element_type=F32, precision=lax.Precision.HIGHEST)
    x = placed + (1.0 - seen) * gains[9:10] + posT[...].T.astype(F32)
    x_o[...] = x
    hat, _ = norm_parts(x)
    h = (hat * (1.0 + gains[0:1]) + gains[1:2]).astype(BF16)
    m = nn(h, qkv[...])
    W = x.shape[1]
    q_o[...] = (m[:, :W] + gains[4:5]).astype(BF16)
    k_o[...] = (m[:, W:2*W] * (HD**-0.5 * math.log2(math.e))).astype(BF16)
    v_o[...] = (m[:, 2*W:] + gains[5:6]).astype(BF16)

def dec_pre(info, places, encoded, embed, gains, posT, qkv, tile=512):
    W, n = posT.shape
    sd = jax.ShapeDtypeStruct
    full = lambda a: pl.BlockSpec(a.shape, lambda i: (0,)*a.ndim)
    row = pl.BlockSpec((tile, W), lambda i: (i, 0))
    return pl.pallas_call(dec_pre_kernel, grid=(n//tile,),
        out_shape=(sd((n, W), F32),) + (sd((n, W), BF16),)*3,
        in_specs=[S, full(places), full(encoded), full(embed), full(gains), pl.BlockSpec((W, tile), lambda i: (0, i)), full(qkv)],
        out_specs=(row,)*4, compiler_params=params())(info, places, encoded, embed, gains, posT, qkv)

def head_rows(block, j):
    parts = []
    if j > 0: parts.append(jnp.zeros((HD*j, block.shape[1]), block.dtype))
    parts.append(block[HD*j:HD*(j+1)])
    if j < 3: parts.append(jnp.zeros((HD*(3-j), block.shape[1]), block.dtype))
    return jnp.concatenate(parts, 0)

def head_lanes(block, j):
    lane = lax.broadcasted_iota(jnp.int32, block.shape, 1)
    return jnp.where((lane >= HD*j) & (lane < HD*(j+1)), block, jnp.zeros_like(block))

def dead_bias(count, n):
    return jnp.where(lax.broadcasted_iota(jnp.int32, (n - SHORT, 1), 0) + SHORT < count, 0.0, FAR_BELOW)

def attend_kernel(info, q_ref, k_ref, v_ref, o_ref, L_ref):
    k = k_ref[...]
    bias = dead_bias(info[0], k.shape[0])
    qT = q_ref[...].T
    vT = v_ref[...].T
    outs = []
    for j in range(4):
        rows = slice(HD*j, HD*(j+1))
        s = nn(k, head_rows(qT, j))
        s = jnp.concatenate([s[:SHORT], s[SHORT:] + bias], 0)
        m = jnp.max(s, axis=0, keepdims=True)
        p = jnp.exp2(s - m)
        total = jnp.sum(p, axis=0, keepdims=True)
        o = nn(vT[rows], p.astype(BF16))
        outs.append((o * (1.0 / total)).astype(BF16))
        L_ref[0, j:j+1, :] = m + jnp.log2(total)
    o_ref[...] = jnp.concatenate(outs, 0).T

def attend(info, q, k, v):
    n, W = k.shape
    blk = pl.BlockSpec((n, GROUP), lambda g: (0, g))
    return pl.pallas_call(attend_kernel, grid=(W//GROUP,),
        out_shape=(jax.ShapeDtypeStruct((n, W), BF16), jax.ShapeDtypeStruct((W//GROUP, 4, n), F32)),
        in_specs=[S, blk, blk, blk], out_specs=(blk, pl.BlockSpec((1, 4, n), lambda g: (g, 0, 0))),
        compiler_params=params())(info, q, k, v)

def attend_back_kernel(info, q_ref, k_ref, v_ref, go_ref, o_ref, L_ref, gq_ref, gk_ref, gv_ref):
    q = q_ref[...]; k = k_ref[...]; v = v_ref[...]; go = go_ref[...]
    bias = dead_bias(info[0], k.shape[0])
    qT = q.T; kT = k.T; goT = go.T; oT = o_ref[...].T
    inner_all = goT.astype(F32) * oT.astype(F32)
    ak = av = None
    gqs = []
    for j in range(4):
        rows = slice(HD*j, HD*(j+1))
        s = nn(k, head_rows(qT, j))
        s = jnp.concatenate([s[:SHORT], s[SHORT:] + bias], 0)
        p = jnp.exp2(s - L_ref[0, j:j+1, :])
        gp = nn(v, head_rows(goT, j))
        inner = jnp.sum(inner_all[rows], axis=0, keepdims=True)
        gs = (p * (gp - inner)).astype(BF16)
        a = nn(p.astype(BF16), head_lanes(go, j))
        b = nn(gs, head_lanes(q, j))
        av = a if av is None else av + a
        ak = b if ak is None else ak + b
        gqs.append((nn(kT[rows], gs) * math.log(2.0)).astype(BF16))
    gq_ref[...] = jnp.concatenate(gqs, 0).T
    gk_ref[...] = (ak * HD**-0.5).astype(BF16)
    gv_ref[...] = av.astype(BF16)

def attend_back(info, q, k, v, go, o, L):
    n, W = k.shape
    blk = pl.BlockSpec((n, GROUP), lambda g: (0, g))
    return pl.pallas_call(attend_back_kernel, grid=(W//GROUP,),
        out_shape=(jax.ShapeDtypeStruct((n, W), BF16),)*3,
        in_specs=[S, blk, blk, blk, blk, blk, pl.BlockSpec((1, 4, n), lambda g: (g, 0, 0))], out_specs=(blk,)*3,
        compiler_params=params())(info, q, k, v, go, o, L)

def dec_mid_kernel(steps, info, x_r, o_r, cot_r, gains, bias, proj, fc1, fc2,
                   dec_o, gx1_o, go_o, gfc2_o, gfc1_o, gproj_o, gvec_o, gbias_o, afc2, afc1, aproj):
    i = pl.program_id(0)
    @pl.when(i == 0)
    def _():
        for ref in (afc2, afc1, aproj, gvec_o, gbias_o): ref[...] = jnp.zeros_like(ref)
    n = x_r.shape[0]
    live = lax.broadcasted_iota(jnp.int32, (n, 1), 0) + i * n < info[0]
    o = o_r[...]
    x1 = x_r[...] + (nn(o, proj[...]) + gains[6:7])
    hat, r = norm_parts(x1)
    h2 = (hat * (1.0 + gains[2:3]) + gains[3:4]).astype(BF16)
    u, dg = gelu_parts(nn(h2, fc1[...]) + bias[...])
    u = u.astype(BF16)
    y = x1 + (nn(u, fc2[...]) + gains[7:8])
    dec_o[...] = jnp.where(live, y, 0.0).astype(BF16)
    G = jnp.where(live, cot_r[...].astype(F32), 0.0)
    gy = G.astype(BF16)
    afc2[...] += tn(u, gy)
    gz = (nt(gy, fc2[...]) * dg).astype(BF16)
    gbias_o[...] += col_sum(gz.astype(F32))
    afc1[...] += tn(h2, gz)
    gh2 = nt(gz, fc1[...])
    gvec_o[0:1, :] += col_sum(gh2 * hat)
    gvec_o[1:2, :] += col_sum(gh2)
    gx1 = G + norm_back(gh2, hat, r, gains[2:3])
    gx1_o[...] = gx1
    ga = gx1.astype(BF16)
    gvec_o[2:3, :] += col_sum(ga.astype(F32))
    gvec_o[3:4, :] += col_sum(G)
    aproj[...] += tn(o, ga)
    go_o[...] = nt(ga, proj[...]).astype(BF16)
    @pl.when(i == steps - 1)
    def _():
        gfc2_o[...] = afc2[...].astype(BF16)
        gfc1_o[...] = afc1[...].astype(BF16)
        gproj_o[...] = aproj[...].astype(BF16)

def dec_mid(info, x, o, cot, gains, bias, proj, fc1, fc2, tile=256):
    n, W = x.shape
    sd = jax.ShapeDtypeStruct
    full = lambda a: pl.BlockSpec(a.shape, lambda i: (0,)*a.ndim)
    row = pl.BlockSpec((tile, W), lambda i: (i, 0))
    Fw = fc1.shape[1]
    outs = (sd((n, W), BF16), sd((n, W), F32), sd((n, W), BF16), sd(fc2.shape, BF16), sd(fc1.shape, BF16), sd(proj.shape, BF16), sd((8, W), F32), sd((1, Fw), F32))
    return pl.pallas_call(functools.partial(dec_mid_kernel, n//tile), grid=(n//tile,), out_shape=outs,
        in_specs=[S, row, row, row, full(gains), full(bias), full(proj), full(fc1), full(fc2)],
        out_specs=(row, row, row) + tuple(full(a) for a in outs[3:]),
        scratch_shapes=[pltpu.VMEM(w.shape, F32) for w in (fc2, fc1, proj)],
        compiler_params=params())(info, x, o, cot, gains, bias, proj, fc1, fc2)

def dec_post_kernel(steps, info, places, x_r, gx1_r, gq_r, gk_r, gv_r, gains, qkv, gqkv_o, gposT_o, gemb_o, gvec_o, aqkv, aemb):
    i = pl.program_id(0)
    @pl.when(i == 0)
    def _():
        for ref in (aqkv, aemb, gvec_o): ref[...] = jnp.zeros_like(ref)
    n = x_r.shape[0]
    x = x_r[...]
    hat, r = norm_parts(x)
    h = (hat * (1.0 + gains[0:1]) + gains[1:2]).astype(BF16)
    gm = jnp.concatenate([gq_r[...], gk_r[...], gv_r[...]], 1)
    W = x.shape[1]
    aqkv[...] += tn(h, gm)
    gh = nt(gm, qkv[...])
    gvec_o[0:1, :] += col_sum(gh * hat)
    gvec_o[1:2, :] += col_sum(gh)
    gvec_o[4:5, :] += col_sum(gq_r[...].astype(F32))
    gvec_o[5:6, :] += col_sum(gv_r[...].astype(F32))
    gx = gx1_r[...] + norm_back(gh, hat, r, gains[0:1])
    gxb = gx.astype(BF16)
    gposT_o[...] = gxb.T
    pos_i = lax.broadcasted_iota(jnp.int32, (n, ROWS_E), 0) + i * n
    rr = lax.broadcasted_iota(jnp.int32, (n, ROWS_E), 1)
    pick = ((pos_i == places[...]) & (rr < info[0] // 10)).astype(BF16)
    seen = jnp.sum(pick.astype(F32), axis=1, keepdims=True)
    aemb[...] += tn(pick, gxb)
    gvec_o[9:10, :] += col_sum(gx * (1.0 - seen))
    @pl.when(i == steps - 1)
    def _():
        gqkv_o[...] = aqkv[...].astype(BF16)
        gemb_o[...] = aemb[...].astype(BF16)
        gvec_o[8:9, :] = col_sum(aemb[...])

def dec_post(info, places, x, gx1, gq, gk, gv, gains, qkv, tile=256):
    n, W = x.shape
    sd = jax.ShapeDtypeStruct
    full = lambda a: pl.BlockSpec(a.shape, lambda i: (0,)*a.ndim)
    row = pl.BlockSpec((tile, W), lambda i: (i, 0))
    outs = (sd(qkv.shape, BF16), sd((W, n), BF16), sd((ROWS_E, W), BF16), sd((16, W), F32))
    return pl.pallas_call(functools.partial(dec_post_kernel, n//tile), grid=(n//tile,), out_shape=outs,
        in_specs=[S, full(places), row, row, row, row, row, full(gains), full(qkv)],
        out_specs=(full(outs[0]), pl.BlockSpec((W, tile), lambda i: (0, i)), full(outs[2]), full(outs[3])),
        scratch_shapes=[pltpu.VMEM(qkv.shape, F32), pltpu.VMEM((ROWS_E, W), F32)],
        compiler_params=params())(info, places, x, gx1, gq, gk, gv, gains, qkv)


def unpack_kernel(small, e_gains, e_bias, d_gains, d_bias):
    count = small.shape[0]
    values = small[...].astype(F32)
    for out, row, rows in ((e_gains, 0, 8), (d_gains, 8, 16), (e_bias, 24, 1), (d_bias, 25, 1)):
        w = out.shape[1] // count
        out[...] = jnp.concatenate([values[i, row : row + rows, :w] for i in range(count)], 1)


def unpack(small, shapes):
    return pl.pallas_call(
        unpack_kernel, out_shape=[jax.ShapeDtypeStruct(s, F32) for s in shapes]
    )(small)


def pack_kernel(e_vec, e_bias, mid_vec, post_vec, d_bias, out, whole):
    count = out.shape[0]
    whole[...] = jnp.zeros_like(whole)
    whole[0:2] = post_vec[0:2]
    whole[2:4] = mid_vec[0:2]
    whole[4:6] = post_vec[4:6]
    whole[6:8] = mid_vec[2:4]
    whole[8:10] = post_vec[8:10]
    out[...] = jnp.zeros_like(out)
    for ref, row, rows in ((e_vec, 0, 8), (whole, 8, 16), (e_bias, 24, 1), (d_bias, 25, 1)):
        w = ref.shape[1] // count
        values = ref[...].astype(BF16)
        for i in range(count):
            out[i, row : row + rows, :w] = values[:, w * i : w * i + w]


def pack(e_vec, e_bias, mid_vec, post_vec, d_bias, count):
    return pl.pallas_call(
        pack_kernel,
        out_shape=jax.ShapeDtypeStruct((count, SMALL_ROWS, 128), BF16),
        scratch_shapes=[pltpu.VMEM((16, mid_vec.shape[1]), F32)],
    )(e_vec, e_bias, mid_vec, post_vec, d_bias)


def last_kernel(n, *refs):
    ins, outs = refs[:n], refs[n:]

    def total(ref):
        acc = ref[0].astype(F32)
        for d in range(1, ref.shape[0]):
            acc = acc + ref[d].astype(F32)
        return acc

    small = total(ins[0])
    for out, row in zip(outs[:4], (0, 8, 24, 25)):
        out[...] = small[row : row + out.shape[0], : out.shape[1]]
    for i, ref in enumerate(ins[1:]):
        outs[4 + i][...] = total(ref).T if i == POS_AT else total(ref)


def last_sums(arrays, shapes):
    return pl.pallas_call(
        functools.partial(last_kernel, len(arrays)),
        out_shape=[jax.ShapeDtypeStruct(s, F32) for s in shapes],
        compiler_params=params(),
    )(*arrays)


def body(
    patches,
    lengths,
    keep_order,
    e_vectors,
    e_qkv,
    e_proj,
    e_fc1,
    e_fc1_bias,
    e_fc2,
    embed,
    d_vectors,
    dec_pos,
    d_qkv,
    d_proj,
    d_fc1,
    d_fc1_bias,
    d_fc2,
    cotangent,
):
    count = lax.axis_size("segment") * lax.axis_size("dp")
    Z = lax.axis_size("dp") // 4
    cube = lax.axis_index(AXES)
    slots = patches.shape[1]
    smalls = (e_vectors, d_vectors, e_fc1_bias.reshape(1, -1), d_fc1_bias.reshape(1, -1))
    shards = (e_qkv, e_proj, e_fc1, e_fc2, embed, dec_pos, d_qkv, d_proj, d_fc1, d_fc2)
    full = gather_all(smalls, shards, Z)
    e_gains, e_bias, d_gains, d_bias = unpack(
        full[0].reshape(count, SMALL_ROWS, 128),
        [
            (8, e_vectors.shape[1] * count),
            (1, e_fc1_bias.shape[0] * count),
            (16, d_vectors.shape[1] * count),
            (1, d_fc1_bias.shape[0] * count),
        ],
    )
    mats = [m.reshape(-1, m.shape[-1]) for m in full[1:]]
    w_qkv, w_proj, w_fc1, w_fc2, w_embed, posT, dw_qkv, dw_proj, dw_fc1, dw_fc2 = mats

    info = lax.dynamic_slice_in_dim(lengths, cube, 1, 0)
    places = lax.dynamic_slice_in_dim(keep_order, cube, 1, 0)[:, :ROWS_E]
    encoded, *kept = enc_fwd(
        info, places, patches[0], e_gains, e_bias, w_qkv, w_proj, w_fc1, w_fc2
    )
    x, q, k, v = dec_pre(info, places, encoded, w_embed, d_gains, posT, dw_qkv)
    o, L = attend(info, q, k, v)
    decoded, gx1, go, gd_fc2, gd_fc1, gd_proj, mid_vec, gd_bias = dec_mid(
        info, x, o, cotangent[0], d_gains, d_bias, dw_proj, dw_fc1, dw_fc2
    )
    gq, gk, gv = attend_back(info, q, k, v, go, o, L)
    gd_qkv, g_posT, gemb, post_vec = dec_post(
        info, places, x, gx1, gq, gk, gv, d_gains, dw_qkv
    )
    g_patch, g_embed, ge_qkv, ge_proj, ge_fc1, ge_fc2, e_vec, ge_bias = enc_bwd(
        info, places, encoded, gemb, w_embed, e_gains, *kept, w_qkv, w_proj, w_fc1, w_fc2, slots
    )
    g_small = pack(e_vec, ge_bias, mid_vec, post_vec, gd_bias, count)

    def blocks(m):
        return m.reshape((2, Z, 2, 2, -1, m.shape[-1]))

    order = (gd_fc2, gd_fc1, gd_proj, gd_qkv, g_posT, g_embed, ge_fc2, ge_fc1, ge_proj, ge_qkv)
    parts = scatter_all([blocks(m) for m in order + (g_small.reshape(-1, 128),)], Z)
    shapes = [m.shape for m in smalls + shards]
    out = last_sums(parts[::-1], shapes)
    re_vec, rd_vec, re_bias, rd_bias = out[:4]
    re_qkv, re_proj, re_fc1, re_fc2, r_embed, r_pos, rd_qkv, rd_proj, rd_fc1, rd_fc2 = out[4:]
    return (
        decoded[None],
        g_patch[None],
        re_vec,
        re_qkv,
        re_proj,
        re_fc1,
        re_bias.reshape(-1),
        re_fc2,
        r_embed,
        rd_vec,
        r_pos,
        rd_qkv,
        rd_proj,
        rd_fc1,
        rd_bias.reshape(-1),
        rd_fc2,
    )


def solution(mesh):
    rows, columns, cubes = P(AXES, None), P(None, AXES), P(AXES, None, None)
    weights = (columns, rows, rows, rows, P(AXES), rows, rows, columns, columns)
    weights = weights + (rows, rows, rows, P(AXES), rows)
    return jax.shard_map(
        body,
        mesh=mesh,
        in_specs=(cubes, P(), P()) + weights + (cubes,),
        out_specs=(cubes, cubes) + weights,
        check_vma=False,
    )
```

```python
import functools
import math

import jax
import jax.numpy as jnp
from jax import lax
from jax.experimental import pallas as pl
from jax.experimental.pallas import tpu as pltpu
from jax.sharding import PartitionSpec as P

HEADS_E = 12
HEADS_D = 16
VIS = 104
SHORT = 576
HD = 32
GROUP = 128
F32 = jnp.float32
BF16 = jnp.bfloat16
AXES = ("segment", "dp")
MESH = pl.DeviceIdType.MESH
ROWS_E = 128
NORM_EPS = 1e-06
FAR_BELOW = -1e30


SMALL_ROWS = 32
POS_AT = 5


def place():
    s = lax.axis_index("segment")
    dp = lax.axis_index("dp")
    return s, dp // 4, (dp // 2) % 2, dp % 2


def device(s, z, y, c):
    return (s, (z * 2 + y) * 2 + c)


def halves(columns):
    return (columns // 2, columns // 2) if columns % 256 == 0 else (columns, 0)


def greet(peers):
    barrier = pltpu.get_barrier_semaphore()
    for peer in peers:
        pl.semaphore_signal(barrier, inc=1, device_id=peer, device_id_type=MESH)
    pl.semaphore_wait(barrier, len(peers))


def send(src, dst, send_sem, recv_sem, target):
    copy = pltpu.make_async_remote_copy(
        src_ref=src,
        dst_ref=dst,
        send_sem=send_sem,
        recv_sem=recv_sem,
        device_id=target,
        device_id_type=MESH,
    )
    copy.start()
    return copy


def gather_kernel(n, Z, *refs):
    m = n + 3
    given, outs, ins, shards = refs[:m], refs[m : m + n], refs[m + n : m + 2 * n], refs[m + 2 * n : 2 * m + 2 * n]
    get, loc, zs, zr, ms, mr, cs, cr = refs[2 * m + 2 * n :]
    loads = [pltpu.make_async_copy(given[i], shards[i], get.at[i]) for i in range(m)]
    for load in loads:
        load.start()

    def cast(i):
        if i == 0:
            small = ins[0]
            small[...] = jnp.zeros_like(small)
            for row, k in zip((0, 8, 24, 25), range(4)):
                loads[k].wait()
                ref = shards[k]
                small[row : row + ref.shape[0], : ref.shape[1]] = ref[...].astype(BF16)
        else:
            loads[i + 3].wait()
            ref = shards[i + 3]
            ins[i][...] = (ref[...].T if i == 1 + POS_AT else ref[...]).astype(BF16)

    s, z, y, c = place()
    X, Y, C = device(1 - s, z, y, c), device(s, z, 1 - y, c), device(s, z, y, 1 - c)
    z_peers = [device(s, lax.rem(z + d, Z), y, c) for d in range(1, Z)]
    greet(z_peers + [X, Y, C])
    state = {}
    sends = []

    def both(ref, i, sems, k, target):
        copy = send(ref, ref, sems[0].at[i, k], sems[1].at[i, k], target)
        sends.append(copy)
        return copy

    def stage0(i):
        cast(i)
        own = pltpu.make_async_copy(ins[i], outs[i].at[s, z, y, c], loc.at[i])
        own.start()
        copies = [
            send(ins[i], outs[i].at[s, z, y, c], zs.at[i, d], zr.at[i, d], z_peers[d])
            for d in range(Z - 1)
        ]
        sends.extend(copies)
        state[i, 0] = (own, copies)

    def stage1(i):
        own, copies = state[i, 0]
        own.wait()
        for copy in copies:
            copy.wait_recv()
        o = outs[i]
        ka, kb = halves(o.shape[-1])
        A, B = pl.ds(0, ka), pl.ds(ka, kb)
        state[i, 1] = [both(o.at[s, :, y, c, :, A], i, (ms, mr), 0, X)]
        if kb:
            state[i, 1].append(both(o.at[s, :, y, c, :, B], i, (ms, mr), 1, Y))
        state[i, 9] = [both(o.at[s, :, y, c], i, (cs, cr), 0, C)]

    def stage2(i):
        for copy in state[i, 1]:
            copy.wait_recv()
        o = outs[i]
        ka, kb = halves(o.shape[-1])
        A, B = pl.ds(0, ka), pl.ds(ka, kb)
        state[i, 2] = [both(o.at[:, :, y, c, :, A], i, (ms, mr), 2, Y)]
        state[i, 9].append(both(o.at[1 - s, :, y, c, :, A], i, (cs, cr), 1, C))
        if kb:
            state[i, 2].append(both(o.at[s, :, :, c, :, B], i, (ms, mr), 3, X))
            state[i, 9].append(both(o.at[s, :, 1 - y, c, :, B], i, (cs, cr), 2, C))

    def stage3(i):
        for copy in state[i, 2]:
            copy.wait_recv()
        o = outs[i]
        ka, kb = halves(o.shape[-1])
        A, B = pl.ds(0, ka), pl.ds(ka, kb)
        state[i, 9].append(both(o.at[:, :, 1 - y, c, :, A], i, (cs, cr), 3, C))
        if kb:
            state[i, 9].append(both(o.at[1 - s, :, :, c, :, B], i, (cs, cr), 4, C))

    stages = (stage0, stage1, stage2, stage3)
    for t in range(n + 3):
        for k in range(4):
            if 0 <= t - k < n:
                stages[k](t - k)
    for i in range(n):
        for copy in state[i, 9]:
            copy.wait_recv()
    for copy in sends:
        copy.wait_send()


def gather_all(small_shards, arrays, Z):
    shapes = [(SMALL_ROWS, 128)] + [a.shape for a in arrays]
    shapes[1 + POS_AT] = shapes[1 + POS_AT][::-1]
    n = len(shapes)
    D = pltpu.SemaphoreType.DMA
    return pl.pallas_call(
        functools.partial(gather_kernel, n, Z),
        out_shape=[jax.ShapeDtypeStruct((2, Z, 2, 2) + s, BF16) for s in shapes],
        in_specs=[pl.BlockSpec(memory_space=pl.ANY)] * (n + 3),
        out_specs=[pl.BlockSpec(memory_space=pl.ANY)] * n,
        scratch_shapes=[pltpu.VMEM(s, BF16) for s in shapes]
        + [pltpu.VMEM(a.shape, F32) for a in (*small_shards, *arrays)]
        + [
            D((n + 3,)),
            D((n,)),
            D((n, Z - 1)),
            D((n, Z - 1)),
            D((n, 4)),
            D((n, 4)),
            D((n, 5)),
            D((n, 5)),
        ],
        compiler_params=pltpu.CompilerParams(
            collective_id=0, has_side_effects=True, vmem_limit_bytes=60 * 2**20
        ),
    )(*small_shards, *arrays)


class Scatter:
    def __init__(self, Z, arrays, chunks, sems):
        self.Z, self.arrays, self.chunks = Z, arrays, chunks
        self.loc, self.cs, self.cr, self.ms, self.mr, self.zs, self.zr = sems
        self.s, self.z, self.y, self.c = s, z, y, c = place()
        self.X, self.Y = device(1 - s, z, y, c), device(s, z, 1 - y, c)
        self.C = device(s, z, y, 1 - c)
        self.z_peers = [device(s, lax.rem(z + d, Z), y, c) for d in range(1, Z)]

    def greet(self):
        greet(self.z_peers + [self.X, self.Y, self.C])

    def parts(self, m):
        i, start, width = self.chunks[m]
        ka, kb = halves(width)
        return i, start, width, ka, kb, (start // 2 if kb else start)

    def held(self, i, index, columns):
        blocks, held = self.arrays[i][:2]
        if held is None:
            ss, zz, yy = index
            return blocks.at[ss, zz, yy, self.c, :, columns]
        return held.at[(*index, slice(None), columns)]

    def copy(self, src, dst, ss, rs, target):
        return pltpu.make_async_remote_copy(
            src_ref=src,
            dst_ref=dst,
            send_sem=ss,
            recv_sem=rs,
            device_id=target,
            device_id_type=MESH,
        )

    def own(self, m):
        i, start, width, *_ = self.parts(m)
        blocks, held = self.arrays[i][:2]
        if held is None:
            return None
        cols = pl.ds(start, width)
        return pltpu.make_async_copy(
            blocks.at[:, :, :, self.c, :, cols], held.at[:, :, :, :, cols], self.loc.at[m]
        )

    def copies(self, m, stage):
        i, start, width, ka, kb, at = self.parts(m)
        s, z, y, c, Z = self.s, self.z, self.y, self.c, self.Z
        blocks, held, R0, R1A, R1B, R2A, R2B, out = self.arrays[i]
        cols, A, B = pl.ds(start, width), pl.ds(start, ka), pl.ds(start + ka, kb)
        half = pl.ds(at, ka)
        full = slice(None)
        if stage == 0:
            return [
                self.copy(
                    blocks.at[:, :, :, 1 - c, :, cols],
                    R0.at[:, :, :, :, cols],
                    self.cs.at[m],
                    self.cr.at[m],
                    self.C,
                )
            ]
        if stage == 1:
            made = [(self.held(i, (full, full, 1 - y), A), R1A.at[:, :, :, half], self.Y)]
            if kb:
                made.append((self.held(i, (1 - s, full, full), B), R1B.at[:, :, :, half], self.X))
        elif stage == 2:
            made = [(self.held(i, (1 - s, full, y), A), R2A.at[:, :, half], self.X)]
            if kb:
                made.append((self.held(i, (s, full, 1 - y), B), R2B.at[:, :, half], self.Y))
        else:
            return [
                self.copy(
                    self.held(i, (s, lax.rem(z + d, Z), y), cols),
                    out.at[d, :, cols],
                    self.zs.at[m, d - 1],
                    self.zr.at[m, d - 1],
                    self.z_peers[d - 1],
                )
                for d in range(1, Z)
            ]
        k = 2 * (stage - 1)
        return [
            self.copy(src, dst, self.ms.at[m, k + j], self.mr.at[m, k + j], target)
            for j, (src, dst, target) in enumerate(made)
        ]

    def add(self, i, index, columns, other):
        ref = self.held(i, index, columns)
        ref[...] = (ref[...].astype(F32) + other[...].astype(F32)).astype(BF16)

    def stage(self, m, stage):
        i, start, width, ka, kb, at = self.parts(m)
        s, z, y, Z = self.s, self.z, self.y, self.Z
        blocks, held, R0, R1A, R1B, R2A, R2B, out = self.arrays[i]
        cols, A, B = pl.ds(start, width), pl.ds(start, ka), pl.ds(start + ka, kb)
        half = pl.ds(at, ka)
        if stage == 0:
            own = self.own(m)
            if own is not None:
                own.start()
        else:
            if stage == 1 and held is not None:
                self.own(m).wait()
            for copy in self.copies(m, stage - 1):
                copy.wait_recv()
        if stage == 1:

            @pl.loop(0, 4 * Z)
            def _(t):
                index = (t // (Z * 2), (t // 2) % Z, t % 2)
                self.add(i, index, cols, R0.at[(*index, slice(None), cols)])

        elif stage == 2:

            @pl.loop(0, 2 * Z)
            def _(t):
                u, zz = t // Z, t % Z
                self.add(i, (u, zz, y), A, R1A.at[u, zz, :, half])
                if kb:
                    self.add(i, (s, zz, u), B, R1B.at[zz, u, :, half])

        elif stage == 3:

            @pl.loop(0, Z)
            def _(zz):
                self.add(i, (s, zz, y), A, R2A.at[zz, :, half])
                if kb:
                    self.add(i, (s, zz, y), B, R2B.at[zz, :, half])

        elif stage == 4:
            out[0, :, cols] = self.held(i, (s, z, y), cols)[...]
            return
        for copy in self.copies(m, stage):
            copy.start()

    @property
    def ticks(self):
        return len(self.chunks) + 4

    def tick(self, t):
        for k in range(5):
            if 0 <= t - k < len(self.chunks):
                self.stage(t - k, k)

    def finish(self):
        for m in range(len(self.chunks)):
            for stage in range(4):
                for copy in self.copies(m, stage):
                    copy.wait_send()


def scatter_buffers(shapes, loaded, Z, chunks):
    refs = []
    for (r, k), load in zip(shapes, loaded):
        ka, kb = halves(k)
        kb = max(kb, 128)
        if load:
            refs.append((2, Z, 2, r, k))
        refs += [(2, Z, 2, r, k), (2, Z, r, ka), (Z, 2, r, kb), (Z, r, ka), (Z, r, kb)]
    n = len(chunks)
    D = pltpu.SemaphoreType.DMA
    return [pltpu.VMEM(s, BF16) for s in refs], [
        D((n,)),
        D((n,)),
        D((n,)),
        D((n, 4)),
        D((n, 4)),
        D((n, Z - 1)),
        D((n, Z - 1)),
    ]


def take_buffers(refs, blocks, loaded, outs):
    refs = list(refs)
    arrays = []
    for block, load, out in zip(blocks, loaded, outs):
        held = refs.pop(0) if load else None
        arrays.append((block, held, *(refs.pop(0) for _ in range(5)), out))
    return arrays


def nn(a, b): return jnp.dot(a, b, preferred_element_type=F32)
def nt(a, b): return lax.dot_general(a, b, (((1,), (1,)), ((), ())), preferred_element_type=F32)
def tn(a, b): return lax.dot_general(a, b, (((0,), (0,)), ((), ())), preferred_element_type=F32)

def norm_parts(x):
    center = x - jnp.mean(x, axis=-1, keepdims=True)
    r = lax.rsqrt(jnp.mean(center * center, axis=-1, keepdims=True) + NORM_EPS)
    return center * r, r

def norm_back(g, hat, r, gain):
    w = g * (1.0 + gain)
    return r * (w - jnp.mean(w, axis=-1, keepdims=True) - hat * jnp.mean(w * hat, axis=-1, keepdims=True))

def gelu_parts(z):
    x = jnp.abs(z) * math.sqrt(0.5)
    t = 1.0 / (1.0 + 0.3275911 * x)
    e = jnp.exp(-(x * x))
    poly = t * (0.254829592 + t * (-0.284496736 + t * (1.421413741 + t * (-1.453152027 + t * 1.061405429))))
    half = 0.5 * poly * e
    cdf = jnp.where(z > 0, 1.0 - half, half)
    return z * cdf, cdf + z * e * (1.0 / math.sqrt(2.0 * math.pi))

def col_sum(m): return jnp.sum(m, axis=0, keepdims=True)

def pick_matrix(places_row, keep_count, slots):
    pos = lax.broadcasted_iota(jnp.int32, (slots, ROWS_E), 0)
    r = lax.broadcasted_iota(jnp.int32, (slots, ROWS_E), 1)
    return ((pos == places_row) & (r < keep_count)).astype(BF16)

def enc_fwd_kernel(info, places, patches, gains, bias, qkv_h, proj_h, fc1_h, fc2_h,
                   enc_o, x_o, m_o, o_o, x1_o, u_o, dg_o, p_o, qkv, proj, fc1, fc2, sem):
    copies = [pltpu.make_async_copy(h, v, sem.at[i]) for i, (h, v) in enumerate(((qkv_h, qkv), (proj_h, proj), (fc1_h, fc1), (fc2_h, fc2)))]
    for cp in copies: cp.start()
    v = info[0] // 10
    pick = pick_matrix(places[...], v, patches.shape[0])
    x = tn(pick, patches[...])
    x_o[...] = x
    hat, _ = norm_parts(x)
    h = (hat * (1.0 + gains[0:1]) + gains[1:2]).astype(BF16)
    copies[0].wait()
    W = x.shape[1]
    m = nn(h, qkv[...])
    q = (m[:, :W] + gains[4:5]).astype(BF16)
    k = m[:, W:2*W].astype(BF16)
    val = (m[:, 2*W:] + gains[5:6]).astype(BF16)
    m_o[...] = jnp.concatenate([q, k, val], 1)
    live = lax.broadcasted_iota(jnp.int32, (ROWS_E, ROWS_E), 1) < v
    hs = W // HEADS_E
    outs = []
    for j in range(HEADS_E):
        sl = slice(hs*j, hs*(j+1))
        s = jnp.where(live, nt(q[:, sl], k[:, sl]) * hs**-0.5, FAR_BELOW)
        e = jnp.exp(s - jnp.max(s, axis=-1, keepdims=True))
        p = e / jnp.sum(e, axis=-1, keepdims=True)
        p_o[j] = p
        outs.append(nn(p.astype(BF16), val[:, sl]).astype(BF16))
    o = jnp.concatenate(outs, 1)
    o_o[...] = o
    copies[1].wait()
    x1 = x + (nn(o, proj[...]) + gains[6:7])
    x1_o[...] = x1
    hat2, _ = norm_parts(x1)
    h2 = (hat2 * (1.0 + gains[2:3]) + gains[3:4]).astype(BF16)
    copies[2].wait()
    u, dg = gelu_parts(nn(h2, fc1[...]) + bias[...])
    u = u.astype(BF16)
    u_o[...] = u; dg_o[...] = dg
    copies[3].wait()
    enc_o[...] = (x1 + (nn(u, fc2[...]) + gains[7:8])).astype(BF16)

V = pl.BlockSpec(memory_space=pltpu.VMEM); A = pl.BlockSpec(memory_space=pl.ANY); S = pl.BlockSpec(memory_space=pltpu.SMEM)
D = pltpu.SemaphoreType.DMA
def params(mb=56): return pltpu.CompilerParams(vmem_limit_bytes=mb*2**20)

def enc_fwd(info, places, patches, gains, bias, qkv, proj, fc1, fc2):
    W, Fw = fc1.shape
    sd = jax.ShapeDtypeStruct
    return pl.pallas_call(enc_fwd_kernel,
        out_shape=(sd((ROWS_E, W), BF16), sd((ROWS_E, W), F32), sd((ROWS_E, 3*W), BF16), sd((ROWS_E, W), BF16), sd((ROWS_E, W), F32),
                   sd((ROWS_E, Fw), BF16), sd((ROWS_E, Fw), F32), sd((HEADS_E, ROWS_E, ROWS_E), F32)),
        in_specs=[S, V, V, V, V, A, A, A, A], out_specs=(V,)*8,
        scratch_shapes=[pltpu.VMEM(w.shape, BF16) for w in (qkv, proj, fc1, fc2)] + [D((4,))],
        compiler_params=params())(info, places, patches, gains, bias, qkv, proj, fc1, fc2)

def dec_pre_kernel(info, places, encoded, embed, gains, posT, qkv, x_o, q_o, k_o, v_o):
    n = x_o.shape[0]
    i = pl.program_id(0)
    emb = nn(encoded[...], embed[...]) + gains[8:9]
    pos_i = lax.broadcasted_iota(jnp.int32, (n, ROWS_E), 0) + i * n
    r = lax.broadcasted_iota(jnp.int32, (n, ROWS_E), 1)
    pick = ((pos_i == places[...]) & (r < info[0] // 10)).astype(F32)
    seen = jnp.sum(pick, axis=1, keepdims=True)
    placed = jnp.dot(pick, emb, preferred_element_type=F32, precision=lax.Precision.HIGHEST)
    x = placed + (1.0 - seen) * gains[9:10] + posT[...].T.astype(F32)
    x_o[...] = x
    hat, _ = norm_parts(x)
    h = (hat * (1.0 + gains[0:1]) + gains[1:2]).astype(BF16)
    m = nn(h, qkv[...])
    W = x.shape[1]
    q_o[...] = (m[:, :W] + gains[4:5]).astype(BF16)
    k_o[...] = (m[:, W:2*W] * (HD**-0.5 * math.log2(math.e))).astype(BF16)
    v_o[...] = (m[:, 2*W:] + gains[5:6]).astype(BF16)

def dec_pre(info, places, encoded, embed, gains, posT, qkv, tile=512):
    W, n = posT.shape
    sd = jax.ShapeDtypeStruct
    full = lambda a: pl.BlockSpec(a.shape, lambda i: (0,)*a.ndim)
    row = pl.BlockSpec((tile, W), lambda i: (i, 0))
    return pl.pallas_call(dec_pre_kernel, grid=(n//tile,),
        out_shape=(sd((n, W), F32),) + (sd((n, W), BF16),)*3,
        in_specs=[S, full(places), full(encoded), full(embed), full(gains), pl.BlockSpec((W, tile), lambda i: (0, i)), full(qkv)],
        out_specs=(row,)*4, compiler_params=params())(info, places, encoded, embed, gains, posT, qkv)

def head_rows(block, j):
    parts = []
    if j > 0: parts.append(jnp.zeros((HD*j, block.shape[1]), block.dtype))
    parts.append(block[HD*j:HD*(j+1)])
    if j < 3: parts.append(jnp.zeros((HD*(3-j), block.shape[1]), block.dtype))
    return jnp.concatenate(parts, 0)

def head_lanes(block, j):
    lane = lax.broadcasted_iota(jnp.int32, block.shape, 1)
    return jnp.where((lane >= HD*j) & (lane < HD*(j+1)), block, jnp.zeros_like(block))

def dead_bias(count, n):
    return jnp.where(lax.broadcasted_iota(jnp.int32, (n - SHORT, 1), 0) + SHORT < count, 0.0, FAR_BELOW)

def attend_kernel(info, q_ref, k_ref, v_ref, o_ref, L_ref):
    k = k_ref[...]
    bias = dead_bias(info[0], k.shape[0])
    qT = q_ref[...].T
    vT = v_ref[...].T
    outs = []
    for j in range(4):
        rows = slice(HD*j, HD*(j+1))
        s = nn(k, head_rows(qT, j))
        s = jnp.concatenate([s[:SHORT], s[SHORT:] + bias], 0)
        m = jnp.max(s, axis=0, keepdims=True)
        p = jnp.exp2(s - m)
        total = jnp.sum(p, axis=0, keepdims=True)
        o = nn(vT[rows], p.astype(BF16))
        outs.append((o * (1.0 / total)).astype(BF16))
        L_ref[0, j:j+1, :] = m + jnp.log2(total)
    o_ref[...] = jnp.concatenate(outs, 0).T

def attend(info, q, k, v):
    n, W = k.shape
    blk = pl.BlockSpec((n, GROUP), lambda g: (0, g))
    return pl.pallas_call(attend_kernel, grid=(W//GROUP,),
        out_shape=(jax.ShapeDtypeStruct((n, W), BF16), jax.ShapeDtypeStruct((W//GROUP, 4, n), F32)),
        in_specs=[S, blk, blk, blk], out_specs=(blk, pl.BlockSpec((1, 4, n), lambda g: (g, 0, 0))),
        compiler_params=params())(info, q, k, v)

def dec_mid_kernel(steps, info, x_r, o_r, cot_r, gains, bias, proj, fc1, fc2,
                   dec_o, gx1_o, go_o, gfc2_o, gfc1_o, gproj_o, gvec_o, gbias_o, afc2, afc1, aproj):
    i = pl.program_id(0)
    @pl.when(i == 0)
    def _():
        for ref in (afc2, afc1, aproj, gvec_o, gbias_o): ref[...] = jnp.zeros_like(ref)
    n = x_r.shape[0]
    live = lax.broadcasted_iota(jnp.int32, (n, 1), 0) + i * n < info[0]
    o = o_r[...]
    x1 = x_r[...] + (nn(o, proj[...]) + gains[6:7])
    hat, r = norm_parts(x1)
    h2 = (hat * (1.0 + gains[2:3]) + gains[3:4]).astype(BF16)
    u, dg = gelu_parts(nn(h2, fc1[...]) + bias[...])
    u = u.astype(BF16)
    y = x1 + (nn(u, fc2[...]) + gains[7:8])
    dec_o[...] = jnp.where(live, y, 0.0).astype(BF16)
    G = jnp.where(live, cot_r[...].astype(F32), 0.0)
    gy = G.astype(BF16)
    afc2[...] += tn(u, gy)
    gz = (nt(gy, fc2[...]) * dg).astype(BF16)
    gbias_o[...] += col_sum(gz.astype(F32))
    afc1[...] += tn(h2, gz)
    gh2 = nt(gz, fc1[...])
    gvec_o[0:1, :] += col_sum(gh2 * hat)
    gvec_o[1:2, :] += col_sum(gh2)
    gx1 = G + norm_back(gh2, hat, r, gains[2:3])
    gx1_o[...] = gx1
    ga = gx1.astype(BF16)
    gvec_o[2:3, :] += col_sum(ga.astype(F32))
    gvec_o[3:4, :] += col_sum(G)
    aproj[...] += tn(o, ga)
    go_o[...] = nt(ga, proj[...]).astype(BF16)
    @pl.when(i == steps - 1)
    def _():
        gfc2_o[...] = afc2[...].astype(BF16)
        gfc1_o[...] = afc1[...].astype(BF16)
        gproj_o[...] = aproj[...].astype(BF16)

def dec_mid(info, x, o, cot, gains, bias, proj, fc1, fc2, tile=256):
    n, W = x.shape
    sd = jax.ShapeDtypeStruct
    full = lambda a: pl.BlockSpec(a.shape, lambda i: (0,)*a.ndim)
    row = pl.BlockSpec((tile, W), lambda i: (i, 0))
    Fw = fc1.shape[1]
    outs = (sd((n, W), BF16), sd((n, W), F32), sd((n, W), BF16), sd(fc2.shape, BF16), sd(fc1.shape, BF16), sd(proj.shape, BF16), sd((8, W), F32), sd((1, Fw), F32))
    return pl.pallas_call(functools.partial(dec_mid_kernel, n//tile), grid=(n//tile,), out_shape=outs,
        in_specs=[S, row, row, row, full(gains), full(bias), full(proj), full(fc1), full(fc2)],
        out_specs=(row, row, row) + tuple(full(a) for a in outs[3:]),
        scratch_shapes=[pltpu.VMEM(w.shape, F32) for w in (fc2, fc1, proj)],
        compiler_params=params())(info, x, o, cot, gains, bias, proj, fc1, fc2)

def dec_post_kernel(steps, info, places, x_r, gx1_r, gq_r, gk_r, gv_r, gains, qkv, gqkv_o, gposT_o, gemb_o, gvec_o, aqkv, aemb):
    i = pl.program_id(0)
    @pl.when(i == 0)
    def _():
        for ref in (aqkv, aemb, gvec_o): ref[...] = jnp.zeros_like(ref)
    n = x_r.shape[0]
    x = x_r[...]
    hat, r = norm_parts(x)
    h = (hat * (1.0 + gains[0:1]) + gains[1:2]).astype(BF16)
    gm = jnp.concatenate([gq_r[...], gk_r[...], gv_r[...]], 1)
    W = x.shape[1]
    aqkv[...] += tn(h, gm)
    gh = nt(gm, qkv[...])
    gvec_o[0:1, :] += col_sum(gh * hat)
    gvec_o[1:2, :] += col_sum(gh)
    gvec_o[4:5, :] += col_sum(gq_r[...].astype(F32))
    gvec_o[5:6, :] += col_sum(gv_r[...].astype(F32))
    gx = gx1_r[...] + norm_back(gh, hat, r, gains[0:1])
    gxb = gx.astype(BF16)
    gposT_o[...] = gxb.T
    pos_i = lax.broadcasted_iota(jnp.int32, (n, ROWS_E), 0) + i * n
    rr = lax.broadcasted_iota(jnp.int32, (n, ROWS_E), 1)
    pick = ((pos_i == places[...]) & (rr < info[0] // 10)).astype(BF16)
    seen = jnp.sum(pick.astype(F32), axis=1, keepdims=True)
    aemb[...] += tn(pick, gxb)
    gvec_o[9:10, :] += col_sum(gx * (1.0 - seen))
    @pl.when(i == steps - 1)
    def _():
        gqkv_o[...] = aqkv[...].astype(BF16)
        gemb_o[...] = aemb[...].astype(BF16)
        gvec_o[8:9, :] = col_sum(aemb[...])

def dec_post(info, places, x, gx1, gq, gk, gv, gains, qkv, tile=256):
    n, W = x.shape
    sd = jax.ShapeDtypeStruct
    full = lambda a: pl.BlockSpec(a.shape, lambda i: (0,)*a.ndim)
    row = pl.BlockSpec((tile, W), lambda i: (i, 0))
    outs = (sd(qkv.shape, BF16), sd((W, n), BF16), sd((ROWS_E, W), BF16), sd((16, W), F32))
    return pl.pallas_call(functools.partial(dec_post_kernel, n//tile), grid=(n//tile,), out_shape=outs,
        in_specs=[S, full(places), row, row, row, row, row, full(gains), full(qkv)],
        out_specs=(full(outs[0]), pl.BlockSpec((W, tile), lambda i: (0, i)), full(outs[2]), full(outs[3])),
        scratch_shapes=[pltpu.VMEM(qkv.shape, F32), pltpu.VMEM((ROWS_E, W), F32)],
        compiler_params=params())(info, places, x, gx1, gq, gk, gv, gains, qkv)

SPOTS = (0, 1, 3, 5, 7, 9, 11, 13, 15)


def attend_back_kernel(Z, chunks, info, q_ref, k_ref, v_ref, go_ref, o_ref, L_ref, *refs):
    blocks, (gq_ref, gk_ref, gv_ref), outs, rest = refs[:3], refs[3:6], refs[6:9], refs[9:]
    lands, rest = rest[:3], rest[3:]
    engine = Scatter(Z, take_buffers(rest[:-7], blocks, (True,) * 3, lands), chunks, rest[-7:])
    g = pl.program_id(0)

    @pl.when(g == 0)
    def _():
        engine.greet()

    q = q_ref[...]
    k = k_ref[...]
    v = v_ref[...]
    go = go_ref[...]
    bias = dead_bias(info[0], k.shape[0])
    qT, kT, goT, oT = q.T, k.T, go.T, o_ref[...].T
    inner_all = goT.astype(F32) * oT.astype(F32)
    ak = av = None
    gqs = []
    for j in range(4):
        for step in range(4):
            if 4 * step + j in SPOTS:

                @pl.when(g == step)
                def _():
                    engine.tick(SPOTS.index(4 * step + j))

        rows = slice(HD * j, HD * (j + 1))
        s = nn(k, head_rows(qT, j))
        s = jnp.concatenate([s[:SHORT], s[SHORT:] + bias], 0)
        p = jnp.exp2(s - L_ref[0, j : j + 1, :])
        gp = nn(v, head_rows(goT, j))
        inner = jnp.sum(inner_all[rows], axis=0, keepdims=True)
        gs = (p * (gp - inner)).astype(BF16)
        a = nn(p.astype(BF16), head_lanes(go, j))
        b = nn(gs, head_lanes(q, j))
        av = a if av is None else av + a
        ak = b if ak is None else ak + b
        gqs.append((nn(kT[rows], gs) * math.log(2.0)).astype(BF16))
    gq_ref[...] = jnp.concatenate(gqs, 0).T
    gk_ref[...] = (ak * HD**-0.5).astype(BF16)
    gv_ref[...] = av.astype(BF16)

    @pl.when(g == 3)
    def _():
        engine.finish()
        for out, land in zip(outs, lands):
            out[...] = land[...]


def attend_back(info, q, k, v, go, o, L, grads, Z):
    n, W = k.shape
    blk = pl.BlockSpec((n, GROUP), lambda g: (0, g))
    shapes = [a.shape[4:] for a in grads]
    chunks = []
    for i, (r, c) in enumerate(shapes[:2]):
        chunks += [(i, 0, c // 2), (i, c // 2, c // 2)]
    chunks.append((2, 0, shapes[2][1]))
    buffers, sems = scatter_buffers(shapes, (True,) * 3, Z, chunks)
    outs = [jax.ShapeDtypeStruct((Z, *s), BF16) for s in shapes]
    return pl.pallas_call(
        functools.partial(attend_back_kernel, Z, chunks),
        grid=(W // GROUP,),
        out_shape=[jax.ShapeDtypeStruct((n, W), BF16)] * 3 + outs,
        in_specs=[S, blk, blk, blk, blk, blk, pl.BlockSpec((1, 4, n), lambda g: (g, 0, 0))]
        + [A] * 3,
        out_specs=[blk] * 3 + [V] * 3,
        scratch_shapes=[pltpu.VMEM(a.shape, BF16) for a in outs] + buffers + sems,
        compiler_params=pltpu.CompilerParams(
            collective_id=1, has_side_effects=True, vmem_limit_bytes=60 * 2**20
        ),
    )(info, q, k, v, go, o, L, *grads)


def enc_bwd_kernel(Z, chunks, *refs):
    given, small_in, blocks_in = refs[:14], refs[14:18], refs[18:20]
    gx_o, outs, rest = refs[20], refs[21:29], refs[29:]
    local, made, rest = rest[:13], rest[13:19], rest[19:]
    e_vec, e_bias, whole, sem = rest[-11:-7]
    loaded = (True, True) + (False,) * 6
    engine = Scatter(
        Z, take_buffers(rest[:-11], (*blocks_in, *made), loaded, outs), chunks, rest[-7:]
    )
    g_embed, g_fc2, g_fc1, g_proj, g_qkv, g_small = made
    gains, mid_vec, post_vec, d_bias = small_in
    places = (*local, local[8].at[:, pl.ds(0, given[13].shape[1])])
    loads = [pltpu.make_async_copy(given[i], places[i], sem.at[i]) for i in range(14)]
    for load in loads[:13]:
        load.start()

    def got(i):
        loads[i].wait()
        return places[i][...]

    engine.greet()
    steps = iter(range(engine.ticks))

    def tick():
        engine.tick(next(steps))

    def store(ref, value):
        ref[...] = value.astype(BF16).reshape(ref.shape)

    tick()
    ge = got(0)
    store(g_embed, tn(got(1), ge))
    gy = nt(ge, got(2)).astype(BF16)
    G = gy.astype(F32)
    tick()
    u = got(3)
    store(g_fc2, tn(u, gy))
    tick()
    gz = (nt(gy, got(4)) * got(5)).astype(BF16)
    e_bias[...] = col_sum(gz.astype(F32))
    tick()
    hat2, r2 = norm_parts(got(6))
    h2 = (hat2 * (1.0 + gains[2:3]) + gains[3:4]).astype(BF16)
    store(g_fc1, tn(h2, gz))
    tick()
    gh2 = nt(gz, got(8))
    loads[13].start()
    e_vec[2:3, :] = col_sum(gh2 * hat2)
    e_vec[3:4, :] = col_sum(gh2)
    gx1 = G + norm_back(gh2, hat2, r2, gains[2:3])
    ga = gx1.astype(BF16)
    e_vec[6:7, :] = col_sum(ga.astype(F32))
    e_vec[7:8, :] = col_sum(G)
    store(g_proj, tn(got(7), ga))
    tick()
    go = nt(ga, got(9)).astype(BF16)
    for i in (10, 11, 12):
        loads[i].wait()
    m_r, p_r, x_r = places[10:13]
    W = gx1.shape[1]
    hs = W // HEADS_E
    gq, gk, gv = [], [], []
    for j in range(HEADS_E):
        q = m_r[:, hs * j : hs * (j + 1)]
        k = m_r[:, W + hs * j : W + hs * (j + 1)]
        val = m_r[:, 2 * W + hs * j : 2 * W + hs * (j + 1)]
        g = go[:, hs * j : hs * (j + 1)]
        p = p_r[j]
        gv.append(tn(p.astype(BF16), g).astype(BF16))
        gp = nt(g, val)
        gs = (p * (gp - jnp.sum(gp * p, axis=-1, keepdims=True))).astype(BF16)
        gq.append((nn(gs, k) * hs**-0.5).astype(BF16))
        gk.append((tn(gs, q) * hs**-0.5).astype(BF16))
        if j == HEADS_E // 2:
            tick()
    gm = jnp.concatenate(gq + gk + gv, 1)
    tick()
    e_vec[4:5, :] = col_sum(gm[:, :W].astype(F32))
    e_vec[5:6, :] = col_sum(gm[:, 2 * W :].astype(F32))
    hat, r = norm_parts(x_r[...])
    h = (hat * (1.0 + gains[0:1]) + gains[1:2]).astype(BF16)
    store(g_qkv, tn(h, gm))
    tick()
    gh = nt(gm, got(13))
    e_vec[0:1, :] = col_sum(gh * hat)
    e_vec[1:2, :] = col_sum(gh)
    gx_o[...] = gx1 + norm_back(gh, hat, r, gains[0:1])
    pack(g_small, e_vec, e_bias, mid_vec, post_vec, d_bias, whole)
    for t in steps:
        engine.tick(t)
    engine.finish()


def pack(out, e_vec, e_bias, mid_vec, post_vec, d_bias, whole):
    Z = out.shape[1]
    count = 8 * Z
    whole[...] = jnp.zeros_like(whole)
    whole[0:2] = post_vec[0:2]
    whole[2:4] = mid_vec[0:2]
    whole[4:6] = post_vec[4:6]
    whole[6:8] = mid_vec[2:4]
    whole[8:10] = post_vec[8:10]
    out[...] = jnp.zeros_like(out)
    for ref, row, rows in ((e_vec, 0, 8), (whole, 8, 16), (e_bias, 24, 1), (d_bias, 25, 1)):
        w = ref.shape[1] // count
        values = ref[...].astype(BF16)
        for i in range(count):
            at = (i // (4 * Z), i // 4 % Z, i // 2 % 2, i % 2)
            out[(*at, slice(row, row + rows), slice(0, w))] = values[:, w * i : w * i + w]


def enc_bwd(encoded, gemb, embed, kept, mats, small_in, blocks_in, Z):
    x, m, o, x1, u, dg, p = kept
    qkv, proj, fc1, fc2 = mats
    given = (gemb, encoded, embed, u, fc2, dg, x1, o, fc1, proj, m, p, x, qkv)
    count = 8 * Z

    def block_shape(a):
        return (a.shape[0] // count, a.shape[1])

    shapes = [a.shape[4:] for a in blocks_in]
    shapes += [block_shape(a) for a in (embed, fc2, fc1, proj, qkv)] + [(SMALL_ROWS, 128)]
    W, Fw = fc1.shape
    chunks = [(0, 0, shapes[0][1]), (1, 0, shapes[1][1]), (2, 0, shapes[2][1])]
    chunks += [(3, t * W // 3, W // 3) for t in range(3)]
    chunks += [(4, t * Fw // 3, Fw // 3) for t in range(3)]
    chunks += [(5, 0, W)] + [(6, t * W, W) for t in range(3)] + [(7, 0, 128)]
    loaded = (True, True) + (False,) * 6
    buffers, sems = scatter_buffers(shapes, loaded, Z, chunks)
    sd = jax.ShapeDtypeStruct
    return pl.pallas_call(
        functools.partial(enc_bwd_kernel, Z, chunks),
        out_shape=[sd(x.shape, F32)] + [sd((Z, *s), BF16) for s in shapes],
        in_specs=[A] * 14 + [V] * 4 + [A] * 2,
        out_specs=[V] * 9,
        scratch_shapes=[pltpu.VMEM(a.shape, a.dtype) for a in given[:13]]
        + [pltpu.VMEM((2, Z, 2, 2, *s), BF16) for s in shapes[2:]]
        + buffers
        + [pltpu.VMEM((8, W), F32), pltpu.VMEM((1, Fw), F32), pltpu.VMEM((16, embed.shape[1]), F32)]
        + [D((14,))]
        + sems,
        compiler_params=pltpu.CompilerParams(
            collective_id=2, has_side_effects=True, vmem_limit_bytes=62 * 2**20
        ),
    )(*given, *small_in, *blocks_in)


def unpack_kernel(small, e_gains, e_bias, d_gains, d_bias):
    count = small.shape[0]
    values = small[...].astype(F32)
    for out, row, rows in ((e_gains, 0, 8), (d_gains, 8, 16), (e_bias, 24, 1), (d_bias, 25, 1)):
        w = out.shape[1] // count
        out[...] = jnp.concatenate([values[i, row : row + rows, :w] for i in range(count)], 1)


def unpack(small, shapes):
    return pl.pallas_call(
        unpack_kernel, out_shape=[jax.ShapeDtypeStruct(s, F32) for s in shapes]
    )(small)


def last_kernel(n, info, places, gx, *refs):
    ins, g_patch, outs = refs[:n], refs[n], refs[n + 1 :]
    pick = pick_matrix(places[...], info[0] // 10, g_patch.shape[0]).astype(F32)
    g_patch[...] = jnp.dot(
        pick, gx[...], preferred_element_type=F32, precision=lax.Precision.HIGHEST
    )

    def total(ref):
        acc = ref[0].astype(F32)
        for d in range(1, ref.shape[0]):
            acc = acc + ref[d].astype(F32)
        return acc

    small = total(ins[0])
    for out, row in zip(outs[:4], (0, 8, 24, 25)):
        out[...] = small[row : row + out.shape[0], : out.shape[1]]
    for i, ref in enumerate(ins[1:]):
        outs[4 + i][...] = total(ref).T if i == POS_AT else total(ref)


def last_sums(info, places, gx, arrays, shapes):
    return pl.pallas_call(
        functools.partial(last_kernel, len(arrays)),
        out_shape=[jax.ShapeDtypeStruct(s, F32) for s in shapes],
        in_specs=[S] + [V] * (2 + len(arrays)),
        compiler_params=params(),
    )(info, places, gx, *arrays)


def body(
    patches,
    lengths,
    keep_order,
    e_vectors,
    e_qkv,
    e_proj,
    e_fc1,
    e_fc1_bias,
    e_fc2,
    embed,
    d_vectors,
    dec_pos,
    d_qkv,
    d_proj,
    d_fc1,
    d_fc1_bias,
    d_fc2,
    cotangent,
):
    count = lax.axis_size("segment") * lax.axis_size("dp")
    Z = lax.axis_size("dp") // 4
    cube = lax.axis_index(AXES)
    slots = patches.shape[1]
    smalls = (e_vectors, d_vectors, e_fc1_bias.reshape(1, -1), d_fc1_bias.reshape(1, -1))
    shards = (e_qkv, e_proj, e_fc1, e_fc2, embed, dec_pos, d_qkv, d_proj, d_fc1, d_fc2)
    full = gather_all(smalls, shards, Z)
    e_gains, e_bias, d_gains, d_bias = unpack(
        full[0].reshape(count, SMALL_ROWS, 128),
        [
            (8, e_vectors.shape[1] * count),
            (1, e_fc1_bias.shape[0] * count),
            (16, d_vectors.shape[1] * count),
            (1, d_fc1_bias.shape[0] * count),
        ],
    )
    mats = [m.reshape(-1, m.shape[-1]) for m in full[1:]]
    w_qkv, w_proj, w_fc1, w_fc2, w_embed, posT, dw_qkv, dw_proj, dw_fc1, dw_fc2 = mats

    info = lax.dynamic_slice_in_dim(lengths, cube, 1, 0)
    places = lax.dynamic_slice_in_dim(keep_order, cube, 1, 0)[:, :ROWS_E]
    encoded, *kept = enc_fwd(
        info, places, patches[0], e_gains, e_bias, w_qkv, w_proj, w_fc1, w_fc2
    )
    x, q, k, v = dec_pre(info, places, encoded, w_embed, d_gains, posT, dw_qkv)
    o, L = attend(info, q, k, v)
    decoded, gx1, go, gd_fc2, gd_fc1, gd_proj, mid_vec, gd_bias = dec_mid(
        info, x, o, cotangent[0], d_gains, d_bias, dw_proj, dw_fc1, dw_fc2
    )

    def blocks(m):
        return m.reshape((2, Z, 2, 2, -1, m.shape[-1]))

    gq, gk, gv, *early = attend_back(
        info, q, k, v, go, o, L, [blocks(m) for m in (gd_fc2, gd_fc1, gd_proj)], Z
    )
    gd_qkv, g_posT, gemb, post_vec = dec_post(
        info, places, x, gx1, gq, gk, gv, d_gains, dw_qkv
    )
    gx, *late = enc_bwd(
        encoded,
        gemb,
        w_embed,
        kept,
        (w_qkv, w_proj, w_fc1, w_fc2),
        (e_gains, mid_vec, post_vec, gd_bias),
        (blocks(gd_qkv), blocks(g_posT)),
        Z,
    )
    pd_qkv, p_pos, p_embed, p_fc2, p_fc1, p_proj, p_qkv, p_small = late
    parts = (p_small, p_qkv, p_proj, p_fc1, p_fc2, p_embed, p_pos, pd_qkv, *early[::-1])
    shapes = [(slots, patches.shape[2])] + [m.shape for m in smalls + shards]
    g_patch, *out = last_sums(info, places, gx, parts, shapes)
    re_vec, rd_vec, re_bias, rd_bias = out[:4]
    re_qkv, re_proj, re_fc1, re_fc2, r_embed, r_pos, rd_qkv, rd_proj, rd_fc1, rd_fc2 = out[4:]
    return (
        decoded[None],
        g_patch[None],
        re_vec,
        re_qkv,
        re_proj,
        re_fc1,
        re_bias.reshape(-1),
        re_fc2,
        r_embed,
        rd_vec,
        r_pos,
        rd_qkv,
        rd_proj,
        rd_fc1,
        rd_bias.reshape(-1),
        rd_fc2,
    )


def solution(mesh):
    rows, columns, cubes = P(AXES, None), P(None, AXES), P(AXES, None, None)
    weights = (columns, rows, rows, rows, P(AXES), rows, rows, columns, columns)
    weights = weights + (rows, rows, rows, P(AXES), rows)
    return jax.shard_map(
        body,
        mesh=mesh,
        in_specs=(cubes, P(), P()) + weights + (cubes,),
        out_specs=(cubes, cubes) + weights,
        check_vma=False,
    )
```

```python
import functools
import math

import jax
import jax.numpy as jnp
from jax import lax
from jax.experimental import pallas as pl
from jax.experimental.pallas import tpu as pltpu
from jax.sharding import PartitionSpec as P

HEADS_E = 12
HEADS_D = 16
VIS = 104
SHORT = 576
HD = 32
GROUP = 128
F32 = jnp.float32
BF16 = jnp.bfloat16
AXES = ("segment", "dp")
MESH = pl.DeviceIdType.MESH
ROWS_E = 128
NORM_EPS = 1e-06
FAR_BELOW = -1e30


SMALL_ROWS = 32


def place():
    s = lax.axis_index("segment")
    dp = lax.axis_index("dp")
    return s, dp // 4, (dp // 2) % 2, dp % 2


def device(s, z, y, c):
    return (s, (z * 2 + y) * 2 + c)


def halves(columns):
    return (columns // 2, columns // 2) if columns % 256 == 0 else (columns, 0)


def greet(peers):
    barrier = pltpu.get_barrier_semaphore()
    for peer in peers:
        pl.semaphore_signal(barrier, inc=1, device_id=peer, device_id_type=MESH)
    pl.semaphore_wait(barrier, len(peers))


class Gather:
    def __init__(self, Z, shards, outs, chunks, sems):
        self.Z, self.shards, self.outs, self.chunks = Z, shards, outs, chunks
        self.loc, self.zs, self.zr, self.ms, self.mr, self.cs, self.cr = sems
        self.s, self.z, self.y, self.c = s, z, y, c = place()
        self.X, self.Y = device(1 - s, z, y, c), device(s, z, 1 - y, c)
        self.C = device(s, z, y, 1 - c)
        self.z_peers = [device(s, lax.rem(z + d, Z), y, c) for d in range(1, Z)]

    def greet(self):
        greet(self.z_peers + [self.X, self.Y, self.C])

    def copy(self, src, dst, ss, rs, target):
        return pltpu.make_async_remote_copy(
            src_ref=src,
            dst_ref=dst,
            send_sem=ss,
            recv_sem=rs,
            device_id=target,
            device_id_type=MESH,
        )

    def own(self, m):
        i, start, width = self.chunks[m]
        cols = pl.ds(start, width)
        return pltpu.make_async_copy(
            self.shards[i].at[:, cols],
            self.outs[i].at[self.s, self.z, self.y, self.c, :, cols],
            self.loc.at[m],
        )

    def copies(self, m, stage):
        i, start, width = self.chunks[m]
        ka, kb = halves(width)
        s, z, y, c = self.s, self.z, self.y, self.c
        o = self.outs[i]
        cols, A = pl.ds(start, width), pl.ds(start, ka)
        B = pl.ds(start + ka, kb) if kb else None
        if stage == 0:
            return [
                self.copy(
                    self.shards[i].at[:, cols],
                    o.at[s, z, y, c, :, cols],
                    self.zs.at[m, d],
                    self.zr.at[m, d],
                    self.z_peers[d],
                )
                for d in range(self.Z - 1)
            ]
        if stage == 1:
            made = [(o.at[s, :, y, c, :, A], 0, self.X)]
            if kb:
                made.append((o.at[s, :, y, c, :, B], 1, self.Y))
        elif stage == 2:
            made = [(o.at[:, :, y, c, :, A], 2, self.Y)]
            if kb:
                made.append((o.at[s, :, :, c, :, B], 3, self.X))
        elif stage == 11:
            made = [(o.at[s, :, y, c, :, cols], 0, self.C)]
        elif stage == 12:
            made = [(o.at[1 - s, :, y, c, :, A], 1, self.C)]
            if kb:
                made.append((o.at[s, :, 1 - y, c, :, B], 2, self.C))
        else:
            made = [(o.at[:, :, 1 - y, c, :, A], 3, self.C)]
            if kb:
                made.append((o.at[1 - s, :, :, c, :, B], 4, self.C))
        ss, rs = (self.cs, self.cr) if stage > 10 else (self.ms, self.mr)
        return [self.copy(ref, ref, ss.at[m, k], rs.at[m, k], target) for ref, k, target in made]

    def stage(self, m, stage):
        if stage == 0:
            self.own(m).start()
        else:
            if stage == 1:
                self.own(m).wait()
            for copy in self.copies(m, stage - 1):
                copy.wait_recv()
        if stage < 3:
            for copy in self.copies(m, stage):
                copy.start()
        if stage > 0:
            for copy in self.copies(m, stage + 10):
                copy.start()

    @property
    def ticks(self):
        return len(self.chunks) + 3

    def tick(self, t):
        for k in range(4):
            if 0 <= t - k < len(self.chunks):
                self.stage(t - k, k)

    def arrived(self, i):
        for m, chunk in enumerate(self.chunks):
            if chunk[0] == i:
                for stage in (11, 12, 13):
                    for copy in self.copies(m, stage):
                        copy.wait_recv()

    def finish(self):
        for m in range(len(self.chunks)):
            for stage in (0, 1, 2, 11, 12, 13):
                for copy in self.copies(m, stage):
                    copy.wait_send()


class Scatter:
    def __init__(self, Z, arrays, chunks, sems):
        self.Z, self.arrays, self.chunks = Z, arrays, chunks
        self.loc, self.cs, self.cr, self.ms, self.mr, self.zs, self.zr = sems
        self.s, self.z, self.y, self.c = s, z, y, c = place()
        self.X, self.Y = device(1 - s, z, y, c), device(s, z, 1 - y, c)
        self.C = device(s, z, y, 1 - c)
        self.z_peers = [device(s, lax.rem(z + d, Z), y, c) for d in range(1, Z)]

    def greet(self):
        greet(self.z_peers + [self.X, self.Y, self.C])

    def parts(self, m):
        i, start, width = self.chunks[m]
        ka, kb = halves(width)
        return i, start, width, ka, kb, (start // 2 if kb else start)

    def held(self, i, index, columns):
        blocks, held = self.arrays[i][:2]
        if held is None:
            ss, zz, yy = index
            return blocks.at[ss, zz, yy, self.c, :, columns]
        return held.at[(*index, slice(None), columns)]

    def copy(self, src, dst, ss, rs, target):
        return pltpu.make_async_remote_copy(
            src_ref=src,
            dst_ref=dst,
            send_sem=ss,
            recv_sem=rs,
            device_id=target,
            device_id_type=MESH,
        )

    def own(self, m):
        i, start, width, *_ = self.parts(m)
        blocks, held = self.arrays[i][:2]
        if held is None:
            return None
        cols = pl.ds(start, width)
        return pltpu.make_async_copy(
            blocks.at[:, :, :, self.c, :, cols], held.at[:, :, :, :, cols], self.loc.at[m]
        )

    def copies(self, m, stage):
        i, start, width, ka, kb, at = self.parts(m)
        s, z, y, c, Z = self.s, self.z, self.y, self.c, self.Z
        blocks, held, R0, R1A, R1B, R2A, R2B, out = self.arrays[i]
        cols, A, B = pl.ds(start, width), pl.ds(start, ka), pl.ds(start + ka, kb)
        half = pl.ds(at, ka)
        full = slice(None)
        if stage == 0:
            return [
                self.copy(
                    blocks.at[:, :, :, 1 - c, :, cols],
                    R0.at[:, :, :, :, cols],
                    self.cs.at[m],
                    self.cr.at[m],
                    self.C,
                )
            ]
        if stage == 1:
            made = [(self.held(i, (full, full, 1 - y), A), R1A.at[:, :, :, half], self.Y)]
            if kb:
                made.append((self.held(i, (1 - s, full, full), B), R1B.at[:, :, :, half], self.X))
        elif stage == 2:
            made = [(self.held(i, (1 - s, full, y), A), R2A.at[:, :, half], self.X)]
            if kb:
                made.append((self.held(i, (s, full, 1 - y), B), R2B.at[:, :, half], self.Y))
        else:
            return [
                self.copy(
                    self.held(i, (s, lax.rem(z + d, Z), y), cols),
                    out.at[d, :, cols],
                    self.zs.at[m, d - 1],
                    self.zr.at[m, d - 1],
                    self.z_peers[d - 1],
                )
                for d in range(1, Z)
            ]
        k = 2 * (stage - 1)
        return [
            self.copy(src, dst, self.ms.at[m, k + j], self.mr.at[m, k + j], target)
            for j, (src, dst, target) in enumerate(made)
        ]

    def add(self, i, index, columns, other):
        ref = self.held(i, index, columns)
        ref[...] = (ref[...].astype(F32) + other[...].astype(F32)).astype(BF16)

    def stage(self, m, stage):
        i, start, width, ka, kb, at = self.parts(m)
        s, z, y, Z = self.s, self.z, self.y, self.Z
        blocks, held, R0, R1A, R1B, R2A, R2B, out = self.arrays[i]
        cols, A, B = pl.ds(start, width), pl.ds(start, ka), pl.ds(start + ka, kb)
        half = pl.ds(at, ka)
        if stage == 0:
            own = self.own(m)
            if own is not None:
                own.start()
        else:
            if stage == 1 and held is not None:
                self.own(m).wait()
            for copy in self.copies(m, stage - 1):
                copy.wait_recv()
        if stage == 1:

            @pl.loop(0, 4 * Z)
            def _(t):
                index = (t // (Z * 2), (t // 2) % Z, t % 2)
                self.add(i, index, cols, R0.at[(*index, slice(None), cols)])

        elif stage == 2:

            @pl.loop(0, 2 * Z)
            def _(t):
                u, zz = t // Z, t % Z
                self.add(i, (u, zz, y), A, R1A.at[u, zz, :, half])
                if kb:
                    self.add(i, (s, zz, u), B, R1B.at[zz, u, :, half])

        elif stage == 3:

            @pl.loop(0, Z)
            def _(zz):
                self.add(i, (s, zz, y), A, R2A.at[zz, :, half])
                if kb:
                    self.add(i, (s, zz, y), B, R2B.at[zz, :, half])

        elif stage == 4:
            out[0, :, cols] = self.held(i, (s, z, y), cols)[...]
            return
        for copy in self.copies(m, stage):
            copy.start()

    @property
    def ticks(self):
        return len(self.chunks) + 4

    def tick(self, t):
        for k in range(5):
            if 0 <= t - k < len(self.chunks):
                self.stage(t - k, k)

    def finish(self):
        for m in range(len(self.chunks)):
            for stage in range(4):
                for copy in self.copies(m, stage):
                    copy.wait_send()


def scatter_buffers(shapes, loaded, Z, chunks):
    refs = []
    for (r, k), load in zip(shapes, loaded):
        ka, kb = halves(k)
        kb = max(kb, 128)
        if load:
            refs.append((2, Z, 2, r, k))
        refs += [(2, Z, 2, r, k), (2, Z, r, ka), (Z, 2, r, kb), (Z, r, ka), (Z, r, kb)]
    n = len(chunks)
    D = pltpu.SemaphoreType.DMA
    return [pltpu.VMEM(s, BF16) for s in refs], [
        D((n,)),
        D((n,)),
        D((n,)),
        D((n, 4)),
        D((n, 4)),
        D((n, Z - 1)),
        D((n, Z - 1)),
    ]


def take_buffers(refs, blocks, loaded, outs):
    refs = list(refs)
    arrays = []
    for block, load, out in zip(blocks, loaded, outs):
        held = refs.pop(0) if load else None
        arrays.append((block, held, *(refs.pop(0) for _ in range(5)), out))
    return arrays


def nn(a, b): return jnp.dot(a, b, preferred_element_type=F32)
def nt(a, b): return lax.dot_general(a, b, (((1,), (1,)), ((), ())), preferred_element_type=F32)
def tn(a, b): return lax.dot_general(a, b, (((0,), (0,)), ((), ())), preferred_element_type=F32)

def norm_parts(x):
    center = x - jnp.mean(x, axis=-1, keepdims=True)
    r = lax.rsqrt(jnp.mean(center * center, axis=-1, keepdims=True) + NORM_EPS)
    return center * r, r

def norm_back(g, hat, r, gain):
    w = g * (1.0 + gain)
    return r * (w - jnp.mean(w, axis=-1, keepdims=True) - hat * jnp.mean(w * hat, axis=-1, keepdims=True))

def gelu_parts(z):
    x = jnp.abs(z) * math.sqrt(0.5)
    t = 1.0 / (1.0 + 0.3275911 * x)
    e = jnp.exp(-(x * x))
    poly = t * (0.254829592 + t * (-0.284496736 + t * (1.421413741 + t * (-1.453152027 + t * 1.061405429))))
    half = 0.5 * poly * e
    cdf = jnp.where(z > 0, 1.0 - half, half)
    return z * cdf, cdf + z * e * (1.0 / math.sqrt(2.0 * math.pi))

def col_sum(m): return jnp.sum(m, axis=0, keepdims=True)

def pick_matrix(places_row, keep_count, slots):
    pos = lax.broadcasted_iota(jnp.int32, (slots, ROWS_E), 0)
    r = lax.broadcasted_iota(jnp.int32, (slots, ROWS_E), 1)
    return ((pos == places_row) & (r < keep_count)).astype(BF16)

V = pl.BlockSpec(memory_space=pltpu.VMEM); A = pl.BlockSpec(memory_space=pl.ANY); S = pl.BlockSpec(memory_space=pltpu.SMEM)
D = pltpu.SemaphoreType.DMA
def params(mb=56): return pltpu.CompilerParams(vmem_limit_bytes=mb*2**20)

def head_rows(block, j):
    parts = []
    if j > 0: parts.append(jnp.zeros((HD*j, block.shape[1]), block.dtype))
    parts.append(block[HD*j:HD*(j+1)])
    if j < 3: parts.append(jnp.zeros((HD*(3-j), block.shape[1]), block.dtype))
    return jnp.concatenate(parts, 0)

def head_lanes(block, j):
    lane = lax.broadcasted_iota(jnp.int32, block.shape, 1)
    return jnp.where((lane >= HD*j) & (lane < HD*(j+1)), block, jnp.zeros_like(block))

def dead_bias(count, n):
    return jnp.where(lax.broadcasted_iota(jnp.int32, (n - SHORT, 1), 0) + SHORT < count, 0.0, FAR_BELOW)

SMALL_AT = ((0, 8), (8, 16), (24, 1), (25, 1))


def place_rows(pick, rows):
    terms, left = [], rows
    for _ in range(3):
        terms.append(left.astype(BF16))
        left = left - terms[-1].astype(F32)
    return nn(jnp.concatenate([pick] * 3, 1), jnp.concatenate(terms, 0))


def front_kernel(Z, chunks, *refs):
    n = 11
    lengths, orders, patches_h, given, refs = refs[0], refs[1], refs[2], refs[3:17], refs[17:]
    fulls, refs = refs[:n], refs[n:]
    info, places, e_gains, d_gains, e_bias, d_bias = refs[:6]
    enc_o, x_o, m_o, o_o, x1_o, u_o, dg_o, p_o, X_o, q_o, k_o, v_o, att_o, L_o = refs[6:20]
    refs = refs[20:]
    shards, cast, here, patches = refs[:14], refs[14 : 14 + n], refs[14 + n : 22 + n], refs[22 + n]
    get, put = refs[23 + n : 25 + n]
    engine = Gather(Z, cast, fulls, chunks, refs[25 + n :])
    loads = [pltpu.make_async_copy(given[i], shards[i], get.at[i]) for i in range(14)]
    for load in loads:
        load.start()
    load_patches = pltpu.make_async_copy(patches_h, patches, get.at[14])
    load_patches.start()
    cube = lax.axis_index(AXES)
    info[0] = lengths[cube]
    heads = orders[:, :ROWS_E]
    mine = lax.broadcasted_iota(jnp.int32, heads.shape, 0) == cube
    places[...] = jnp.sum(jnp.where(mine, heads, 0), axis=0, keepdims=True)
    small = cast[0]
    small[...] = jnp.zeros_like(small)
    for (row, _), k in zip(SMALL_AT, range(4)):
        loads[k].wait()
        small[row : row + shards[k].shape[0], : shards[k].shape[1]] = shards[k][...].astype(BF16)
    engine.greet()
    steps = iter(range(engine.ticks))
    ready = set([0])

    def tick():
        t = next(steps)
        if t < len(chunks) and chunks[t][0] not in ready:
            i = chunks[t][0]
            ready.add(i)
            loads[i + 3].wait()
            cast[i][...] = shards[i + 3][...].astype(BF16)
        engine.tick(t)

    def bring(i):
        engine.arrived(i)
        pltpu.make_async_copy(fulls[i], here[i], put.at[i]).start()

    def got(i):
        pltpu.make_async_copy(fulls[i], here[i], put.at[i]).wait()

    def mat(i):
        shape = here[i].shape
        return here[i][...].reshape(8 * Z * shape[4], shape[5])

    for _ in range(3):
        tick()
    load_patches.wait()
    count = info[0]
    visible = count // 10
    x = tn(pick_matrix(places[...], visible, patches.shape[0]), patches[...])
    x_o[...] = x
    hat, _ = norm_parts(x)
    tick()
    bring(0)
    tick()
    got(0)
    values = here[0][...].reshape(8 * Z, SMALL_ROWS, 128).astype(F32)
    for out, (row, rows) in zip((e_gains, d_gains, e_bias, d_bias), SMALL_AT):
        w = out.shape[1] // (8 * Z)
        out[...] = jnp.concatenate([values[i, row : row + rows, :w] for i in range(8 * Z)], 1)
    h = (hat * (1.0 + e_gains[0:1]) + e_gains[1:2]).astype(BF16)
    tick()
    tick()
    bring(1)
    tick()
    bring(2)
    got(1)
    W = x.shape[1]
    m = nn(h, mat(1))
    q = (m[:, :W] + e_gains[4:5]).astype(BF16)
    k = m[:, W : 2 * W].astype(BF16)
    val = (m[:, 2 * W :] + e_gains[5:6]).astype(BF16)
    m_o[...] = jnp.concatenate([q, k, val], 1)
    tick()
    live = lax.broadcasted_iota(jnp.int32, (ROWS_E, ROWS_E), 1) < visible
    hs = W // HEADS_E
    outs = []
    for j in range(HEADS_E):
        sl = slice(hs * j, hs * (j + 1))
        s = jnp.where(live, nt(q[:, sl], k[:, sl]) * hs**-0.5, FAR_BELOW)
        e = jnp.exp(s - jnp.max(s, axis=-1, keepdims=True))
        p = e / jnp.sum(e, axis=-1, keepdims=True)
        p_o[j] = p
        outs.append(nn(p.astype(BF16), val[:, sl]).astype(BF16))
    o = jnp.concatenate(outs, 1)
    o_o[...] = o
    tick()
    got(2)
    x1 = x + (nn(o, mat(2)) + e_gains[6:7])
    x1_o[...] = x1
    hat2, _ = norm_parts(x1)
    h2 = (hat2 * (1.0 + e_gains[2:3]) + e_gains[3:4]).astype(BF16)
    tick()
    bring(3)
    tick()
    got(3)
    u, dg = gelu_parts(nn(h2, mat(3)) + e_bias[...])
    u = u.astype(BF16)
    u_o[...] = u
    dg_o[...] = dg
    tick()
    tick()
    bring(4)
    tick()
    bring(5)
    got(4)
    encoded = (x1 + (nn(u, mat(4)) + e_gains[7:8])).astype(BF16)
    enc_o[...] = encoded
    tick()
    bring(6)
    got(5)
    emb = nn(encoded, mat(5)) + d_gains[8:9]
    tick()
    bring(7)
    slots = X_o.shape[0]
    pick = pick_matrix(places[...], visible, slots)
    seen = jnp.sum(pick.astype(F32), axis=1, keepdims=True)
    got(6)
    X = place_rows(pick, emb) + (1.0 - seen) * d_gains[9:10] + mat(6).T.astype(F32)
    X_o[...] = X
    hat, _ = norm_parts(X)
    h = (hat * (1.0 + d_gains[0:1]) + d_gains[1:2]).astype(BF16)
    tick()
    got(7)
    m = nn(h, mat(7))
    W = X.shape[1]
    q_o[...] = (m[:, :W] + d_gains[4:5]).astype(BF16)
    k_o[...] = (m[:, W : 2 * W] * (HD**-0.5 * math.log2(math.e))).astype(BF16)
    v_o[...] = (m[:, 2 * W :] + d_gains[5:6]).astype(BF16)
    bias = dead_bias(count, slots)
    rest = list(steps)

    @pl.loop(0, W // GROUP)
    def _(g):
        for at, t in enumerate(rest):

            @pl.when(g == at)
            def _():
                engine.tick(t)

        cols = pl.ds(pl.multiple_of(g * GROUP, GROUP), GROUP)
        kg = k_o[:, cols]
        qT = q_o[:, cols].T
        vT = v_o[:, cols].T
        outs = []
        for j in range(4):
            rows = slice(HD * j, HD * (j + 1))
            s = nn(kg, head_rows(qT, j))
            s = jnp.concatenate([s[:SHORT], s[SHORT:] + bias], 0)
            high = jnp.max(s, axis=0, keepdims=True)
            p = jnp.exp2(s - high)
            total = jnp.sum(p, axis=0, keepdims=True)
            o = nn(vT[rows], p.astype(BF16))
            outs.append((o * (1.0 / total)).astype(BF16))
            L_o[g, j : j + 1, :] = high + jnp.log2(total)
        att_o[:, cols] = jnp.concatenate(outs, 0).T

    for i in range(8, n):
        engine.arrived(i)
    engine.finish()


def front(lengths, orders, patches, small_shards, arrays, Z):
    shapes = [(SMALL_ROWS, 128)] + [a.shape for a in arrays]
    n, count = len(shapes), 8 * Z
    cuts = (1, 3, 1, 3, 3, 1, 1, 1, 1, 1, 1)
    chunks = []
    for i, (shape, parts) in enumerate(zip(shapes, cuts)):
        w = shape[1] // parts
        chunks += [(i, w * t, w) for t in range(parts)]
    slots, W = patches.shape
    Fw, dW, dF = shapes[3][1], shapes[5][1], shapes[9][1]
    sd = jax.ShapeDtypeStruct
    outs = [sd((2, Z, 2, 2) + s, BF16) for s in shapes]
    outs += [sd((1,), jnp.int32), sd((1, ROWS_E), jnp.int32)]
    outs += [sd((8, W), F32), sd((16, dW), F32), sd((1, Fw), F32), sd((1, dF), F32)]
    R = ROWS_E
    outs += [sd((R, W), BF16), sd((R, W), F32), sd((R, 3 * W), BF16), sd((R, W), BF16)]
    outs += [sd((R, W), F32), sd((R, Fw), BF16), sd((R, Fw), F32), sd((HEADS_E, R, R), F32)]
    outs += [sd((slots, dW), F32)] + [sd((slots, dW), BF16)] * 4
    outs += [sd((dW // GROUP, 4, slots), F32)]
    m = len(chunks)
    given = (*small_shards, *arrays)
    return pl.pallas_call(
        functools.partial(front_kernel, Z, chunks),
        out_shape=outs,
        in_specs=[S, V, A] + [A] * 14,
        out_specs=[A] * n + [S] + [V] * 19,
        scratch_shapes=[pltpu.VMEM(a.shape, F32) for a in given]
        + [pltpu.VMEM(s, BF16) for s in shapes]
        + [pltpu.VMEM(o.shape, BF16) for o in outs[:8]]
        + [pltpu.VMEM((slots, W), BF16), D((15,)), D((8,)), D((m,)), D((m, Z - 1)), D((m, Z - 1))]
        + [D((m, 4)), D((m, 4)), D((m, 5)), D((m, 5))],
        compiler_params=pltpu.CompilerParams(
            collective_id=0, has_side_effects=True, vmem_limit_bytes=62 * 2**20
        ),
    )(lengths, orders, patches, *given)


def dec_mid_kernel(steps, info, x_r, o_r, cot_r, gains, bias, proj, fc1, fc2,
                   dec_o, gx1_o, go_o, gfc2_o, gfc1_o, gproj_o, gvec_o, gbias_o, afc2, afc1, aproj):
    i = pl.program_id(0)
    @pl.when(i == 0)
    def _():
        for ref in (afc2, afc1, aproj, gvec_o, gbias_o): ref[...] = jnp.zeros_like(ref)
    n = x_r.shape[0]
    live = lax.broadcasted_iota(jnp.int32, (n, 1), 0) + i * n < info[0]
    o = o_r[...]
    x1 = x_r[...] + (nn(o, proj[...]) + gains[6:7])
    hat, r = norm_parts(x1)
    h2 = (hat * (1.0 + gains[2:3]) + gains[3:4]).astype(BF16)
    u, dg = gelu_parts(nn(h2, fc1[...]) + bias[...])
    u = u.astype(BF16)
    y = x1 + (nn(u, fc2[...]) + gains[7:8])
    dec_o[...] = jnp.where(live, y, 0.0).astype(BF16)
    G = jnp.where(live, cot_r[...].astype(F32), 0.0)
    gy = G.astype(BF16)
    afc2[...] += tn(u, gy)
    gz = (nt(gy, fc2[...]) * dg).astype(BF16)
    gbias_o[...] += col_sum(gz.astype(F32))
    afc1[...] += tn(h2, gz)
    gh2 = nt(gz, fc1[...])
    gvec_o[0:1, :] += col_sum(gh2 * hat)
    gvec_o[1:2, :] += col_sum(gh2)
    gx1 = G + norm_back(gh2, hat, r, gains[2:3])
    gx1_o[...] = gx1
    ga = gx1.astype(BF16)
    gvec_o[2:3, :] += col_sum(ga.astype(F32))
    gvec_o[3:4, :] += col_sum(G)
    aproj[...] += tn(o, ga)
    go_o[...] = nt(ga, proj[...]).astype(BF16)
    @pl.when(i == steps - 1)
    def _():
        gfc2_o[...] = afc2[...].astype(BF16)
        gfc1_o[...] = afc1[...].astype(BF16)
        gproj_o[...] = aproj[...].astype(BF16)

def dec_mid(info, x, o, cot, gains, bias, proj, fc1, fc2, tile=256):
    n, W = x.shape
    sd = jax.ShapeDtypeStruct
    full = lambda a: pl.BlockSpec(a.shape, lambda i: (0,)*a.ndim)
    row = pl.BlockSpec((tile, W), lambda i: (i, 0))
    Fw = fc1.shape[1]
    outs = (sd((n, W), BF16), sd((n, W), F32), sd((n, W), BF16), sd(fc2.shape, BF16), sd(fc1.shape, BF16), sd(proj.shape, BF16), sd((8, W), F32), sd((1, Fw), F32))
    return pl.pallas_call(functools.partial(dec_mid_kernel, n//tile), grid=(n//tile,), out_shape=outs,
        in_specs=[S, row, row, row, full(gains), full(bias), full(proj), full(fc1), full(fc2)],
        out_specs=(row, row, row) + tuple(full(a) for a in outs[3:]),
        scratch_shapes=[pltpu.VMEM(w.shape, F32) for w in (fc2, fc1, proj)],
        compiler_params=params())(info, x, o, cot, gains, bias, proj, fc1, fc2)

def dec_post_kernel(steps, info, places, x_r, gx1_r, gq_r, gk_r, gv_r, gains, qkv, gqkv_o, gposT_o, gemb_o, gvec_o, aqkv, aemb):
    i = pl.program_id(0)
    @pl.when(i == 0)
    def _():
        for ref in (aqkv, aemb, gvec_o): ref[...] = jnp.zeros_like(ref)
    n = x_r.shape[0]
    x = x_r[...]
    hat, r = norm_parts(x)
    h = (hat * (1.0 + gains[0:1]) + gains[1:2]).astype(BF16)
    gm = jnp.concatenate([gq_r[...], gk_r[...], gv_r[...]], 1)
    W = x.shape[1]
    aqkv[...] += tn(h, gm)
    gh = nt(gm, qkv[...])
    gvec_o[0:1, :] += col_sum(gh * hat)
    gvec_o[1:2, :] += col_sum(gh)
    gvec_o[4:5, :] += col_sum(gq_r[...].astype(F32))
    gvec_o[5:6, :] += col_sum(gv_r[...].astype(F32))
    gx = gx1_r[...] + norm_back(gh, hat, r, gains[0:1])
    gxb = gx.astype(BF16)
    gposT_o[...] = gxb.T
    pos_i = lax.broadcasted_iota(jnp.int32, (n, ROWS_E), 0) + i * n
    rr = lax.broadcasted_iota(jnp.int32, (n, ROWS_E), 1)
    pick = ((pos_i == places[...]) & (rr < info[0] // 10)).astype(BF16)
    seen = jnp.sum(pick.astype(F32), axis=1, keepdims=True)
    aemb[...] += tn(pick, gxb)
    gvec_o[9:10, :] += col_sum(gx * (1.0 - seen))
    @pl.when(i == steps - 1)
    def _():
        gqkv_o[...] = aqkv[...].astype(BF16)
        gemb_o[...] = aemb[...].astype(BF16)
        gvec_o[8:9, :] = col_sum(aemb[...])

def dec_post(info, places, x, gx1, gq, gk, gv, gains, qkv, tile=256):
    n, W = x.shape
    sd = jax.ShapeDtypeStruct
    full = lambda a: pl.BlockSpec(a.shape, lambda i: (0,)*a.ndim)
    row = pl.BlockSpec((tile, W), lambda i: (i, 0))
    outs = (sd(qkv.shape, BF16), sd((W, n), BF16), sd((ROWS_E, W), BF16), sd((16, W), F32))
    return pl.pallas_call(functools.partial(dec_post_kernel, n//tile), grid=(n//tile,), out_shape=outs,
        in_specs=[S, full(places), row, row, row, row, row, full(gains), full(qkv)],
        out_specs=(full(outs[0]), pl.BlockSpec((W, tile), lambda i: (0, i)), full(outs[2]), full(outs[3])),
        scratch_shapes=[pltpu.VMEM(qkv.shape, F32), pltpu.VMEM((ROWS_E, W), F32)],
        compiler_params=params())(info, places, x, gx1, gq, gk, gv, gains, qkv)

SPOTS = (0, 2, 4, 6, 8, 10, 12, 14, 16)


def attend_back_kernel(Z, chunks, info, q_ref, k_ref, v_ref, go_ref, o_ref, L_ref, *refs):
    blocks, (gq_ref, gk_ref, gv_ref), outs, rest = refs[:3], refs[3:6], refs[6:9], refs[9:]
    lands, rest = rest[:3], rest[3:]
    engine = Scatter(Z, take_buffers(rest[:-7], blocks, (True,) * 3, lands), chunks, rest[-7:])
    g = pl.program_id(0)

    @pl.when(g == 0)
    def _():
        engine.greet()

    q = q_ref[...]
    k = k_ref[...]
    v = v_ref[...]
    go = go_ref[...]
    bias = dead_bias(info[0], k.shape[0])
    qT, kT, goT, oT = q.T, k.T, go.T, o_ref[...].T
    inner_all = goT.astype(F32) * oT.astype(F32)
    ak = av = None
    gqs = []
    for j in range(4):
        for step in range(4):
            if 4 * step + j in SPOTS:

                @pl.when(g == step)
                def _():
                    engine.tick(SPOTS.index(4 * step + j))

        rows = slice(HD * j, HD * (j + 1))
        s = nn(k, head_rows(qT, j))
        s = jnp.concatenate([s[:SHORT], s[SHORT:] + bias], 0)
        p = jnp.exp2(s - L_ref[0, j : j + 1, :])
        gp = nn(v, head_rows(goT, j))
        inner = jnp.sum(inner_all[rows], axis=0, keepdims=True)
        gs = (p * (gp - inner)).astype(BF16)
        a = nn(p.astype(BF16), head_lanes(go, j))
        b = nn(gs, head_lanes(q, j))
        av = a if av is None else av + a
        ak = b if ak is None else ak + b
        gqs.append((nn(kT[rows], gs) * math.log(2.0)).astype(BF16))
    gq_ref[...] = jnp.concatenate(gqs, 0).T
    gk_ref[...] = (ak * HD**-0.5).astype(BF16)
    gv_ref[...] = av.astype(BF16)

    @pl.when(g == 3)
    def _():
        engine.tick(SPOTS.index(16))
        engine.finish()
        for out, land in zip(outs, lands):
            out[...] = land[...]


def attend_back(info, q, k, v, go, o, L, grads, Z):
    n, W = k.shape
    blk = pl.BlockSpec((n, GROUP), lambda g: (0, g))
    shapes = [a.shape[4:] for a in grads]
    chunks = []
    for i, (r, c) in enumerate(shapes[:2]):
        chunks += [(i, 0, c // 2), (i, c // 2, c // 2)]
    chunks.append((2, 0, shapes[2][1]))
    buffers, sems = scatter_buffers(shapes, (True,) * 3, Z, chunks)
    outs = [jax.ShapeDtypeStruct((Z, *s), BF16) for s in shapes]
    return pl.pallas_call(
        functools.partial(attend_back_kernel, Z, chunks),
        grid=(W // GROUP,),
        out_shape=[jax.ShapeDtypeStruct((n, W), BF16)] * 3 + outs,
        in_specs=[S, blk, blk, blk, blk, blk, pl.BlockSpec((1, 4, n), lambda g: (g, 0, 0))]
        + [A] * 3,
        out_specs=[blk] * 3 + [V] * 3,
        scratch_shapes=[pltpu.VMEM(a.shape, BF16) for a in outs] + buffers + sems,
        compiler_params=pltpu.CompilerParams(
            collective_id=1, has_side_effects=True, vmem_limit_bytes=60 * 2**20
        ),
    )(info, q, k, v, go, o, L, *grads)


def enc_bwd_kernel(Z, chunks, *refs):
    given, small_in, blocks_in = refs[:14], refs[14:18], refs[18:20]
    gx_o, outs, rest = refs[20], refs[21:29], refs[29:]
    local, made, rest = rest[:13], rest[13:19], rest[19:]
    e_vec, e_bias, whole, sem = rest[-11:-7]
    loaded = (True, True) + (False,) * 6
    engine = Scatter(
        Z, take_buffers(rest[:-11], (*blocks_in, *made), loaded, outs), chunks, rest[-7:]
    )
    g_embed, g_fc2, g_fc1, g_proj, g_qkv, g_small = made
    gains, mid_vec, post_vec, d_bias = small_in
    places = (*local, local[8].at[:, pl.ds(0, given[13].shape[1])])
    loads = [pltpu.make_async_copy(given[i], places[i], sem.at[i]) for i in range(14)]
    for load in loads[:13]:
        load.start()

    def got(i):
        loads[i].wait()
        return places[i][...]

    engine.greet()
    steps = iter(range(engine.ticks))

    def tick():
        engine.tick(next(steps))

    def store(ref, value):
        ref[...] = value.astype(BF16).reshape(ref.shape)

    tick()
    ge = got(0)
    store(g_embed, tn(got(1), ge))
    gy = nt(ge, got(2)).astype(BF16)
    G = gy.astype(F32)
    tick()
    u = got(3)
    store(g_fc2, tn(u, gy))
    tick()
    gz = (nt(gy, got(4)) * got(5)).astype(BF16)
    e_bias[...] = col_sum(gz.astype(F32))
    tick()
    hat2, r2 = norm_parts(got(6))
    h2 = (hat2 * (1.0 + gains[2:3]) + gains[3:4]).astype(BF16)
    store(g_fc1, tn(h2, gz))
    tick()
    gh2 = nt(gz, got(8))
    loads[13].start()
    e_vec[2:3, :] = col_sum(gh2 * hat2)
    e_vec[3:4, :] = col_sum(gh2)
    gx1 = G + norm_back(gh2, hat2, r2, gains[2:3])
    ga = gx1.astype(BF16)
    e_vec[6:7, :] = col_sum(ga.astype(F32))
    e_vec[7:8, :] = col_sum(G)
    store(g_proj, tn(got(7), ga))
    tick()
    go = nt(ga, got(9)).astype(BF16)
    for i in (10, 11, 12):
        loads[i].wait()
    m_r, p_r, x_r = places[10:13]
    W = gx1.shape[1]
    hs = W // HEADS_E
    gq, gk, gv = [], [], []
    for j in range(HEADS_E):
        q = m_r[:, hs * j : hs * (j + 1)]
        k = m_r[:, W + hs * j : W + hs * (j + 1)]
        val = m_r[:, 2 * W + hs * j : 2 * W + hs * (j + 1)]
        g = go[:, hs * j : hs * (j + 1)]
        p = p_r[j]
        gv.append(tn(p.astype(BF16), g).astype(BF16))
        gp = nt(g, val)
        gs = (p * (gp - jnp.sum(gp * p, axis=-1, keepdims=True))).astype(BF16)
        gq.append((nn(gs, k) * hs**-0.5).astype(BF16))
        gk.append((tn(gs, q) * hs**-0.5).astype(BF16))
        if j == HEADS_E // 2:
            tick()
    gm = jnp.concatenate(gq + gk + gv, 1)
    tick()
    e_vec[4:5, :] = col_sum(gm[:, :W].astype(F32))
    e_vec[5:6, :] = col_sum(gm[:, 2 * W :].astype(F32))
    hat, r = norm_parts(x_r[...])
    h = (hat * (1.0 + gains[0:1]) + gains[1:2]).astype(BF16)
    store(g_qkv, tn(h, gm))
    tick()
    gh = nt(gm, got(13))
    e_vec[0:1, :] = col_sum(gh * hat)
    e_vec[1:2, :] = col_sum(gh)
    gx_o[...] = gx1 + norm_back(gh, hat, r, gains[0:1])
    pack(g_small, e_vec, e_bias, mid_vec, post_vec, d_bias, whole)
    for t in steps:
        engine.tick(t)
    engine.finish()


def pack(out, e_vec, e_bias, mid_vec, post_vec, d_bias, whole):
    Z = out.shape[1]
    count = 8 * Z
    whole[...] = jnp.zeros_like(whole)
    whole[0:2] = post_vec[0:2]
    whole[2:4] = mid_vec[0:2]
    whole[4:6] = post_vec[4:6]
    whole[6:8] = mid_vec[2:4]
    whole[8:10] = post_vec[8:10]
    out[...] = jnp.zeros_like(out)
    for ref, row, rows in ((e_vec, 0, 8), (whole, 8, 16), (e_bias, 24, 1), (d_bias, 25, 1)):
        w = ref.shape[1] // count
        values = ref[...].astype(BF16)
        for i in range(count):
            at = (i // (4 * Z), i // 4 % Z, i // 2 % 2, i % 2)
            out[(*at, slice(row, row + rows), slice(0, w))] = values[:, w * i : w * i + w]


def enc_bwd(encoded, gemb, embed, kept, mats, small_in, blocks_in, Z):
    x, m, o, x1, u, dg, p = kept
    qkv, proj, fc1, fc2 = mats
    given = (gemb, encoded, embed, u, fc2, dg, x1, o, fc1, proj, m, p, x, qkv)
    count = 8 * Z

    def block_shape(a):
        return (a.shape[0] // count, a.shape[1])

    shapes = [a.shape[4:] for a in blocks_in]
    shapes += [block_shape(a) for a in (embed, fc2, fc1, proj, qkv)] + [(SMALL_ROWS, 128)]
    W, Fw = fc1.shape
    chunks = [(0, 0, shapes[0][1]), (1, 0, shapes[1][1]), (2, 0, shapes[2][1])]
    chunks += [(3, t * W // 3, W // 3) for t in range(3)]
    chunks += [(4, t * Fw // 3, Fw // 3) for t in range(3)]
    chunks += [(5, 0, W)] + [(6, t * W, W) for t in range(3)] + [(7, 0, 128)]
    loaded = (True, True) + (False,) * 6
    buffers, sems = scatter_buffers(shapes, loaded, Z, chunks)
    sd = jax.ShapeDtypeStruct
    return pl.pallas_call(
        functools.partial(enc_bwd_kernel, Z, chunks),
        out_shape=[sd(x.shape, F32)] + [sd((Z, *s), BF16) for s in shapes],
        in_specs=[A] * 14 + [V] * 4 + [A] * 2,
        out_specs=[V] * 9,
        scratch_shapes=[pltpu.VMEM(a.shape, a.dtype) for a in given[:13]]
        + [pltpu.VMEM((2, Z, 2, 2, *s), BF16) for s in shapes[2:]]
        + buffers
        + [pltpu.VMEM((8, W), F32), pltpu.VMEM((1, Fw), F32), pltpu.VMEM((16, embed.shape[1]), F32)]
        + [D((14,))]
        + sems,
        compiler_params=pltpu.CompilerParams(
            collective_id=2, has_side_effects=True, vmem_limit_bytes=62 * 2**20
        ),
    )(*given, *small_in, *blocks_in)


def last_kernel(n, info, places, gx, *refs):
    ins, g_patch, outs = refs[:n], refs[n], refs[n + 1 :]
    pick = pick_matrix(places[...], info[0] // 10, g_patch.shape[0])
    g_patch[...] = place_rows(pick, gx[...])

    def total(ref):
        acc = ref[0].astype(F32)
        for d in range(1, ref.shape[0]):
            acc = acc + ref[d].astype(F32)
        return acc

    small = total(ins[0])
    for out, row in zip(outs[:4], (0, 8, 24, 25)):
        out[...] = small[row : row + out.shape[0], : out.shape[1]]
    for i, ref in enumerate(ins[1:]):
        outs[4 + i][...] = total(ref)


def last_sums(info, places, gx, arrays, shapes):
    return pl.pallas_call(
        functools.partial(last_kernel, len(arrays)),
        out_shape=[jax.ShapeDtypeStruct(s, F32) for s in shapes],
        in_specs=[S] + [V] * (2 + len(arrays)),
        compiler_params=params(),
    )(info, places, gx, *arrays)


def body(
    patches,
    lengths,
    keep_order,
    e_vectors,
    e_qkv,
    e_proj,
    e_fc1,
    e_fc1_bias,
    e_fc2,
    embed,
    d_vectors,
    dec_pos,
    d_qkv,
    d_proj,
    d_fc1,
    d_fc1_bias,
    d_fc2,
    cotangent,
):
    Z = lax.axis_size("dp") // 4
    slots = patches.shape[1]
    smalls = (e_vectors, d_vectors, e_fc1_bias.reshape(1, -1), d_fc1_bias.reshape(1, -1))
    shards = (e_qkv, e_proj, e_fc1, e_fc2, embed, dec_pos.T, d_qkv, d_proj, d_fc1, d_fc2)
    made = front(lengths, keep_order, patches[0], smalls, shards, Z)
    mats = [m.reshape(-1, m.shape[-1]) for m in made[1:11]]
    w_qkv, w_proj, w_fc1, w_fc2, w_embed, posT, dw_qkv, dw_proj, dw_fc1, dw_fc2 = mats
    info, places, e_gains, d_gains, e_bias, d_bias, encoded, *kept = made[11:25]
    x, q, k, v, o, L = made[25:]
    decoded, gx1, go, gd_fc2, gd_fc1, gd_proj, mid_vec, gd_bias = dec_mid(
        info, x, o, cotangent[0], d_gains, d_bias, dw_proj, dw_fc1, dw_fc2
    )

    def blocks(m):
        return m.reshape((2, Z, 2, 2, -1, m.shape[-1]))

    gq, gk, gv, *early = attend_back(
        info, q, k, v, go, o, L, [blocks(m) for m in (gd_fc2, gd_fc1, gd_proj)], Z
    )
    gd_qkv, g_posT, gemb, post_vec = dec_post(
        info, places, x, gx1, gq, gk, gv, d_gains, dw_qkv
    )
    gx, *late = enc_bwd(
        encoded,
        gemb,
        w_embed,
        kept,
        (w_qkv, w_proj, w_fc1, w_fc2),
        (e_gains, mid_vec, post_vec, gd_bias),
        (blocks(gd_qkv), blocks(g_posT)),
        Z,
    )
    pd_qkv, p_pos, p_embed, p_fc2, p_fc1, p_proj, p_qkv, p_small = late
    parts = (p_small, p_qkv, p_proj, p_fc1, p_fc2, p_embed, p_pos, pd_qkv, *early[::-1])
    shapes = [(slots, patches.shape[2])] + [m.shape for m in smalls + shards]
    g_patch, *out = last_sums(info, places, gx, parts, shapes)
    re_vec, rd_vec, re_bias, rd_bias = out[:4]
    re_qkv, re_proj, re_fc1, re_fc2, r_embed, r_pos, rd_qkv, rd_proj, rd_fc1, rd_fc2 = out[4:]
    return (
        decoded[None],
        g_patch[None],
        re_vec,
        re_qkv,
        re_proj,
        re_fc1,
        re_bias.reshape(-1),
        re_fc2,
        r_embed,
        rd_vec,
        r_pos.T,
        rd_qkv,
        rd_proj,
        rd_fc1,
        rd_bias.reshape(-1),
        rd_fc2,
    )


def solution(mesh):
    rows, columns, cubes = P(AXES, None), P(None, AXES), P(AXES, None, None)
    weights = (columns, rows, rows, rows, P(AXES), rows, rows, columns, columns)
    weights = weights + (rows, rows, rows, P(AXES), rows)
    return jax.shard_map(
        body,
        mesh=mesh,
        in_specs=(cubes, P(), P()) + weights + (cubes,),
        out_specs=(cubes, cubes) + weights,
        check_vma=False,
    )
```

```python
import functools
import math

import jax
import jax.numpy as jnp
from jax import lax
from jax.experimental import pallas as pl
from jax.experimental.pallas import tpu as pltpu
from jax.sharding import PartitionSpec as P

HEADS_E = 12
HEADS_D = 16
VIS = 104
SHORT = 576
HD = 32
GROUP = 128
F32 = jnp.float32
BF16 = jnp.bfloat16
AXES = ("segment", "dp")
MESH = pl.DeviceIdType.MESH
ROWS_E = 128
NORM_EPS = 1e-06
FAR_BELOW = -1e30


SMALL_ROWS = 32


def place():
    s = lax.axis_index("segment")
    dp = lax.axis_index("dp")
    return s, dp // 4, (dp // 2) % 2, dp % 2


def device(s, z, y, c):
    return (s, (z * 2 + y) * 2 + c)


def halves(columns):
    return (columns // 2, columns // 2) if columns % 256 == 0 else (columns, 0)


def greet(peers):
    barrier = pltpu.get_barrier_semaphore()
    for peer in peers:
        pl.semaphore_signal(barrier, inc=1, device_id=peer, device_id_type=MESH)
    pl.semaphore_wait(barrier, len(peers))


class Gather:
    def __init__(self, Z, shards, outs, chunks, sems):
        self.Z, self.shards, self.outs, self.chunks = Z, shards, outs, chunks
        self.loc, self.zs, self.zr, self.ms, self.mr, self.cs, self.cr = sems
        self.s, self.z, self.y, self.c = s, z, y, c = place()
        self.X, self.Y = device(1 - s, z, y, c), device(s, z, 1 - y, c)
        self.C = device(s, z, y, 1 - c)
        self.z_peers = [device(s, lax.rem(z + d, Z), y, c) for d in range(1, Z)]

    def greet(self):
        greet(self.z_peers + [self.X, self.Y, self.C])

    def copy(self, src, dst, ss, rs, target):
        return pltpu.make_async_remote_copy(
            src_ref=src,
            dst_ref=dst,
            send_sem=ss,
            recv_sem=rs,
            device_id=target,
            device_id_type=MESH,
        )

    def own(self, m):
        i, start, width = self.chunks[m]
        cols = pl.ds(start, width)
        return pltpu.make_async_copy(
            self.shards[i].at[:, cols],
            self.outs[i].at[self.s, self.z, self.y, self.c, :, cols],
            self.loc.at[m],
        )

    def copies(self, m, stage):
        i, start, width = self.chunks[m]
        ka, kb = halves(width)
        s, z, y, c = self.s, self.z, self.y, self.c
        o = self.outs[i]
        cols, A = pl.ds(start, width), pl.ds(start, ka)
        B = pl.ds(start + ka, kb) if kb else None
        if stage == 0:
            return [
                self.copy(
                    self.shards[i].at[:, cols],
                    o.at[s, z, y, c, :, cols],
                    self.zs.at[m, d],
                    self.zr.at[m, d],
                    self.z_peers[d],
                )
                for d in range(self.Z - 1)
            ]
        if stage == 1:
            made = [(o.at[s, :, y, c, :, A], 0, self.X)]
            if kb:
                made.append((o.at[s, :, y, c, :, B], 1, self.Y))
        elif stage == 2:
            made = [(o.at[:, :, y, c, :, A], 2, self.Y)]
            if kb:
                made.append((o.at[s, :, :, c, :, B], 3, self.X))
        elif stage == 11:
            made = [(o.at[s, :, y, c, :, cols], 0, self.C)]
        elif stage == 12:
            made = [(o.at[1 - s, :, y, c, :, A], 1, self.C)]
            if kb:
                made.append((o.at[s, :, 1 - y, c, :, B], 2, self.C))
        else:
            made = [(o.at[:, :, 1 - y, c, :, A], 3, self.C)]
            if kb:
                made.append((o.at[1 - s, :, :, c, :, B], 4, self.C))
        ss, rs = (self.cs, self.cr) if stage > 10 else (self.ms, self.mr)
        return [self.copy(ref, ref, ss.at[m, k], rs.at[m, k], target) for ref, k, target in made]

    def stage(self, m, stage):
        if stage == 0:
            self.own(m).start()
        else:
            if stage == 1:
                self.own(m).wait()
            for copy in self.copies(m, stage - 1):
                copy.wait_recv()
        if stage < 3:
            for copy in self.copies(m, stage):
                copy.start()
        if stage > 0:
            for copy in self.copies(m, stage + 10):
                copy.start()

    @property
    def ticks(self):
        return len(self.chunks) + 6

    def tick(self, t):
        for k in range(4):
            if 0 <= t - 2 * k < len(self.chunks):
                self.stage(t - 2 * k, k)

    def arrived(self, i):
        for m, chunk in enumerate(self.chunks):
            if chunk[0] == i:
                for stage in (11, 12, 13):
                    for copy in self.copies(m, stage):
                        copy.wait_recv()

    def finish(self):
        for m in range(len(self.chunks)):
            for stage in (0, 1, 2, 11, 12, 13):
                for copy in self.copies(m, stage):
                    copy.wait_send()


class Scatter:
    def __init__(self, Z, arrays, chunks, sems):
        self.Z, self.arrays, self.chunks = Z, arrays, chunks
        self.loc, self.cs, self.cr, self.ms, self.mr, self.zs, self.zr = sems
        self.s, self.z, self.y, self.c = s, z, y, c = place()
        self.X, self.Y = device(1 - s, z, y, c), device(s, z, 1 - y, c)
        self.C = device(s, z, y, 1 - c)
        self.z_peers = [device(s, lax.rem(z + d, Z), y, c) for d in range(1, Z)]

    def greet(self):
        greet(self.z_peers + [self.X, self.Y, self.C])

    def parts(self, m):
        i, start, width = self.chunks[m]
        ka, kb = halves(width)
        return i, start, width, ka, kb, (start // 2 if kb else start)

    def held(self, i, index, columns):
        blocks, held = self.arrays[i][:2]
        if held is None:
            ss, zz, yy = index
            return blocks.at[ss, zz, yy, self.c, :, columns]
        return held.at[(*index, slice(None), columns)]

    def copy(self, src, dst, ss, rs, target):
        return pltpu.make_async_remote_copy(
            src_ref=src,
            dst_ref=dst,
            send_sem=ss,
            recv_sem=rs,
            device_id=target,
            device_id_type=MESH,
        )

    def own(self, m):
        i, start, width, *_ = self.parts(m)
        blocks, held = self.arrays[i][:2]
        if held is None:
            return None
        cols = pl.ds(start, width)
        return pltpu.make_async_copy(
            blocks.at[:, :, :, self.c, :, cols], held.at[:, :, :, :, cols], self.loc.at[m]
        )

    def copies(self, m, stage):
        i, start, width, ka, kb, at = self.parts(m)
        s, z, y, c, Z = self.s, self.z, self.y, self.c, self.Z
        blocks, held, R0, R1A, R1B, R2A, R2B, out = self.arrays[i]
        cols, A, B = pl.ds(start, width), pl.ds(start, ka), pl.ds(start + ka, kb)
        half = pl.ds(at, ka)
        full = slice(None)
        if stage == 0:
            return [
                self.copy(
                    blocks.at[:, :, :, 1 - c, :, cols],
                    R0.at[:, :, :, :, cols],
                    self.cs.at[m],
                    self.cr.at[m],
                    self.C,
                )
            ]
        if stage == 1:
            made = [(self.held(i, (full, full, 1 - y), A), R1A.at[:, :, :, half], self.Y)]
            if kb:
                made.append((self.held(i, (1 - s, full, full), B), R1B.at[:, :, :, half], self.X))
        elif stage == 2:
            made = [(self.held(i, (1 - s, full, y), A), R2A.at[:, :, half], self.X)]
            if kb:
                made.append((self.held(i, (s, full, 1 - y), B), R2B.at[:, :, half], self.Y))
        else:
            return [
                self.copy(
                    self.held(i, (s, lax.rem(z + d, Z), y), cols),
                    out.at[d, :, cols],
                    self.zs.at[m, d - 1],
                    self.zr.at[m, d - 1],
                    self.z_peers[d - 1],
                )
                for d in range(1, Z)
            ]
        k = 2 * (stage - 1)
        return [
            self.copy(src, dst, self.ms.at[m, k + j], self.mr.at[m, k + j], target)
            for j, (src, dst, target) in enumerate(made)
        ]

    def add(self, i, index, columns, other):
        ref = self.held(i, index, columns)
        ref[...] = (ref[...].astype(F32) + other[...].astype(F32)).astype(BF16)

    def stage(self, m, stage):
        i, start, width, ka, kb, at = self.parts(m)
        s, z, y, Z = self.s, self.z, self.y, self.Z
        blocks, held, R0, R1A, R1B, R2A, R2B, out = self.arrays[i]
        cols, A, B = pl.ds(start, width), pl.ds(start, ka), pl.ds(start + ka, kb)
        half = pl.ds(at, ka)
        if stage == 0:
            own = self.own(m)
            if own is not None:
                own.start()
        else:
            if stage == 1 and held is not None:
                self.own(m).wait()
            for copy in self.copies(m, stage - 1):
                copy.wait_recv()
        if stage == 1:

            @pl.loop(0, 4 * Z)
            def _(t):
                index = (t // (Z * 2), (t // 2) % Z, t % 2)
                self.add(i, index, cols, R0.at[(*index, slice(None), cols)])

        elif stage == 2:

            @pl.loop(0, 2 * Z)
            def _(t):
                u, zz = t // Z, t % Z
                self.add(i, (u, zz, y), A, R1A.at[u, zz, :, half])
                if kb:
                    self.add(i, (s, zz, u), B, R1B.at[zz, u, :, half])

        elif stage == 3:

            @pl.loop(0, Z)
            def _(zz):
                self.add(i, (s, zz, y), A, R2A.at[zz, :, half])
                if kb:
                    self.add(i, (s, zz, y), B, R2B.at[zz, :, half])

        elif stage == 4:
            out[0, :, cols] = self.held(i, (s, z, y), cols)[...]
            return
        for copy in self.copies(m, stage):
            copy.start()

    @property
    def ticks(self):
        return len(self.chunks) + 4

    def tick(self, t):
        for k in range(5):
            if 0 <= t - k < len(self.chunks):
                self.stage(t - k, k)

    def finish(self):
        for m in range(len(self.chunks)):
            for stage in range(4):
                for copy in self.copies(m, stage):
                    copy.wait_send()


def scatter_buffers(shapes, loaded, Z, chunks):
    refs = []
    for (r, k), load in zip(shapes, loaded):
        ka, kb = halves(k)
        kb = max(kb, 128)
        if load:
            refs.append((2, Z, 2, r, k))
        refs += [(2, Z, 2, r, k), (2, Z, r, ka), (Z, 2, r, kb), (Z, r, ka), (Z, r, kb)]
    n = len(chunks)
    D = pltpu.SemaphoreType.DMA
    return [pltpu.VMEM(s, BF16) for s in refs], [
        D((n,)),
        D((n,)),
        D((n,)),
        D((n, 4)),
        D((n, 4)),
        D((n, Z - 1)),
        D((n, Z - 1)),
    ]


def take_buffers(refs, blocks, loaded, outs):
    refs = list(refs)
    arrays = []
    for block, load, out in zip(blocks, loaded, outs):
        held = refs.pop(0) if load else None
        arrays.append((block, held, *(refs.pop(0) for _ in range(5)), out))
    return arrays


def nn(a, b): return jnp.dot(a, b, preferred_element_type=F32)
def nt(a, b): return lax.dot_general(a, b, (((1,), (1,)), ((), ())), preferred_element_type=F32)
def tn(a, b): return lax.dot_general(a, b, (((0,), (0,)), ((), ())), preferred_element_type=F32)

def norm_parts(x):
    center = x - jnp.mean(x, axis=-1, keepdims=True)
    r = lax.rsqrt(jnp.mean(center * center, axis=-1, keepdims=True) + NORM_EPS)
    return center * r, r

def norm_back(g, hat, r, gain):
    w = g * (1.0 + gain)
    return r * (w - jnp.mean(w, axis=-1, keepdims=True) - hat * jnp.mean(w * hat, axis=-1, keepdims=True))

def gelu_parts(z):
    x = jnp.abs(z) * math.sqrt(0.5)
    t = 1.0 / (1.0 + 0.3275911 * x)
    e = jnp.exp(-(x * x))
    poly = t * (0.254829592 + t * (-0.284496736 + t * (1.421413741 + t * (-1.453152027 + t * 1.061405429))))
    half = 0.5 * poly * e
    cdf = jnp.where(z > 0, 1.0 - half, half)
    return z * cdf, cdf + z * e * (1.0 / math.sqrt(2.0 * math.pi))

def col_sum(m): return jnp.sum(m, axis=0, keepdims=True)

def pick_matrix(places_row, keep_count, slots):
    pos = lax.broadcasted_iota(jnp.int32, (slots, ROWS_E), 0)
    r = lax.broadcasted_iota(jnp.int32, (slots, ROWS_E), 1)
    return ((pos == places_row) & (r < keep_count)).astype(BF16)

V = pl.BlockSpec(memory_space=pltpu.VMEM); A = pl.BlockSpec(memory_space=pl.ANY); S = pl.BlockSpec(memory_space=pltpu.SMEM)
D = pltpu.SemaphoreType.DMA
def params(mb=56): return pltpu.CompilerParams(vmem_limit_bytes=mb*2**20)

def head_rows(block, j):
    parts = []
    if j > 0: parts.append(jnp.zeros((HD*j, block.shape[1]), block.dtype))
    parts.append(block[HD*j:HD*(j+1)])
    if j < 3: parts.append(jnp.zeros((HD*(3-j), block.shape[1]), block.dtype))
    return jnp.concatenate(parts, 0)

def head_lanes(block, j):
    lane = lax.broadcasted_iota(jnp.int32, block.shape, 1)
    return jnp.where((lane >= HD*j) & (lane < HD*(j+1)), block, jnp.zeros_like(block))

def dead_bias(count, n):
    return jnp.where(lax.broadcasted_iota(jnp.int32, (n - SHORT, 1), 0) + SHORT < count, 0.0, FAR_BELOW)

SMALL_AT = ((0, 8), (8, 16), (24, 1), (25, 1))


def place_rows(pick, rows):
    terms, left = [], rows
    for _ in range(3):
        terms.append(left.astype(BF16))
        left = left - terms[-1].astype(F32)
    return nn(jnp.concatenate([pick] * 3, 1), jnp.concatenate(terms, 0))


def front_kernel(Z, chunks, *refs):
    n = 11
    lengths, orders, patches_h, given, refs = refs[0], refs[1], refs[2], refs[3:17], refs[17:]
    fulls, refs = refs[: n - 1], refs[n - 1 :]
    info, places, e_gains, d_gains, e_bias, d_bias = refs[:6]
    enc_o, x_o, m_o, o_o, x1_o, u_o, dg_o, p_o, X_o, q_o, k_o, v_o, att_o, L_o = refs[6:20]
    refs = refs[20:]
    shards, cast, here, refs = refs[:14], refs[14 : 14 + n], refs[14 + n : 14 + 2 * n], refs[14 + 2 * n :]
    patches, get, put, pick_s, bias_s, high_s, sum_s, oT_s, qkv_s = refs[:9]
    engine = Gather(Z, cast, here, chunks, refs[9:])
    loads = [pltpu.make_async_copy(given[i], shards[i], get.at[i]) for i in range(14)]
    for load in loads:
        load.start()
    load_patches = pltpu.make_async_copy(patches_h, patches, get.at[14])
    load_patches.start()
    cube = lax.axis_index(AXES)
    info[0] = lengths[cube]
    heads = orders[:, :ROWS_E]
    mine = lax.broadcasted_iota(jnp.int32, heads.shape, 0) == cube
    places[...] = jnp.sum(jnp.where(mine, heads, 0), axis=0, keepdims=True)
    small = cast[0]
    small[...] = jnp.zeros_like(small)
    for (row, _), k in zip(SMALL_AT, range(4)):
        loads[k].wait()
        small[row : row + shards[k].shape[0], : shards[k].shape[1]] = shards[k][...].astype(BF16)
    engine.greet()
    steps = iter(range(engine.ticks))

    def advance(t):
        if t < len(chunks) and chunks[t][0] and chunks[t][0] not in [m[0] for m in chunks[:t]]:
            i = chunks[t][0]
            loads[i + 3].wait()
            cast[i][...] = shards[i + 3][...].astype(BF16)
        engine.tick(t)

    def tick():
        advance(next(steps))

    def keep(i):
        return pltpu.make_async_copy(here[i], fulls[i - 1], put.at[i - 1])

    def bring(i):
        engine.arrived(i)
        if i:
            keep(i).start()

    def mat(i):
        shape = here[i].shape
        return here[i][...].reshape(8 * Z * shape[4], shape[5])

    for _ in range(7):
        tick()
    bring(0)
    load_patches.wait()
    count = info[0]
    visible = count // 10
    slots = patches.shape[0]
    pick_s[...] = pick_matrix(places[...], visible, slots)
    x = tn(pick_s[...], patches[...])
    x_o[...] = x
    tick()
    bring(6)
    values = here[0][...].reshape(8 * Z, SMALL_ROWS, 128).astype(F32)
    for out, (row, rows) in zip((e_gains, d_gains, e_bias, d_bias), SMALL_AT):
        w = out.shape[1] // (8 * Z)
        out[...] = jnp.concatenate([values[i, row : row + rows, :w] for i in range(8 * Z)], 1)
    tick()
    bring(7)
    X = d_gains[9:10] + mat(6).T.astype(F32)
    X_o[...] = X
    hat, _ = norm_parts(X)
    h = (hat * (1.0 + d_gains[0:1]) + d_gains[1:2]).astype(BF16)
    tick()
    dW = X.shape[1]

    def three(m):
        q = (m[:, :dW] + d_gains[4:5]).astype(BF16)
        k = (m[:, dW : 2 * dW] * (HD**-0.5 * math.log2(math.e))).astype(BF16)
        return q, k, (m[:, 2 * dW :] + d_gains[5:6]).astype(BF16)

    q_o[...], k_o[...], v_o[...] = three(nn(h, mat(7)))
    spot = lax.broadcasted_iota(jnp.int32, (slots, 1), 0)
    seen = jnp.sum(pick_s[...].astype(F32), axis=1, keepdims=True)
    bias_s[...] = jnp.where((spot < count) & (seen < 0.5), 0.0, FAR_BELOW)

    def masked_keys(g, turn):
        cols = pl.ds(pl.multiple_of(g * GROUP, GROUP), GROUP)
        kg = k_o[:, cols]
        qT = q_o[:, cols].T
        vT = v_o[:, cols].T
        for j in range(4):
            if j % 2 == 0:
                turn(j // 2)
            rows = slice(HD * j, HD * (j + 1))
            s = nn(kg, head_rows(qT, j)) + bias_s[...]
            high = jnp.max(s, axis=0, keepdims=True)
            p = jnp.exp2(s - high)
            high_s[g, j : j + 1, :] = high
            sum_s[g, j : j + 1, :] = jnp.sum(p, axis=0, keepdims=True)
            oT_s[g, rows, :] = nn(vT[rows], p.astype(BF16))

    groups = dW // GROUP
    turns = [next(steps) for _ in range(2 * (groups - 1))]

    @pl.loop(0, groups - 1)
    def _(g):
        def turn(k):
            for at in range(groups - 1):

                @pl.when(g == at)
                def _():
                    advance(turns[2 * at + k])

        masked_keys(g, turn)

    bring(1)
    bring(2)
    hat, _ = norm_parts(x)
    h = (hat * (1.0 + e_gains[0:1]) + e_gains[1:2]).astype(BF16)
    W = x.shape[1]
    m = nn(h, mat(1))
    q = (m[:, :W] + e_gains[4:5]).astype(BF16)
    k = m[:, W : 2 * W].astype(BF16)
    val = (m[:, 2 * W :] + e_gains[5:6]).astype(BF16)
    m_o[...] = jnp.concatenate([q, k, val], 1)
    live = lax.broadcasted_iota(jnp.int32, (ROWS_E, ROWS_E), 1) < visible
    hs = W // HEADS_E
    outs = []
    for j in range(HEADS_E):
        sl = slice(hs * j, hs * (j + 1))
        s = jnp.where(live, nt(q[:, sl], k[:, sl]) * hs**-0.5, FAR_BELOW)
        e = jnp.exp(s - jnp.max(s, axis=-1, keepdims=True))
        p = e / jnp.sum(e, axis=-1, keepdims=True)
        p_o[j] = p
        outs.append(nn(p.astype(BF16), val[:, sl]).astype(BF16))
    o = jnp.concatenate(outs, 1)
    o_o[...] = o
    tick()
    bring(3)
    x1 = x + (nn(o, mat(2)) + e_gains[6:7])
    x1_o[...] = x1
    hat2, _ = norm_parts(x1)
    h2 = (hat2 * (1.0 + e_gains[2:3]) + e_gains[3:4]).astype(BF16)
    u, dg = gelu_parts(nn(h2, mat(3)) + e_bias[...])
    u = u.astype(BF16)
    u_o[...] = u
    dg_o[...] = dg
    masked_keys(groups - 1, lambda k: tick())
    bring(4)
    tick()
    bring(5)
    encoded = (x1 + (nn(u, mat(4)) + e_gains[7:8])).astype(BF16)
    enc_o[...] = encoded
    here_pos = nn(mat(6), pick_s[...]).T
    Xv = nn(encoded, mat(5)) + d_gains[8:9] + here_pos
    hat, _ = norm_parts(Xv)
    h = (hat * (1.0 + d_gains[0:1]) + d_gains[1:2]).astype(BF16)
    qv, kv, vv = three(nn(h, mat(7)))
    qkv_s[...] = jnp.concatenate([qv, kv, vv], 1)
    seen = jnp.sum(pick_s[...].astype(F32), axis=1, keepdims=True) > 0.5
    X_o[...] = jnp.where(seen, place_rows(pick_s[...], Xv), X_o[...])
    for i, ref in enumerate((q_o, k_o, v_o)):
        placed = nn(pick_s[...], qkv_s[:, dW * i : dW * (i + 1)]).astype(BF16)
        ref[...] = jnp.where(seen, placed, ref[...])
    tick()
    rest = list(steps)
    seen_row = nt(jnp.ones((8, ROWS_E), BF16), pick_s[...])[0:1] > 0.5
    slot = lax.broadcasted_iota(jnp.int32, (ROWS_E, 1), 0)
    slot_bias = jnp.where(slot < visible, 0.0, FAR_BELOW)
    bias = dead_bias(count, slots)

    @pl.loop(0, groups)
    def _(g):
        for at, t in enumerate(rest):

            @pl.when(g == at)
            def _():
                advance(t)

        cols = pl.ds(pl.multiple_of(g * GROUP, GROUP), GROUP)
        vcols = pl.ds(pl.multiple_of(g * GROUP + 2 * dW, GROUP), GROUP)
        kcols = pl.ds(pl.multiple_of(g * GROUP + dW, GROUP), GROUP)
        qT = q_o[:, cols].T
        kvg = qkv_s[:, kcols]
        vvT = qkv_s[:, vcols].T
        qvT = qkv_s[:, cols].T
        s = nn(k_o[:, cols], jnp.concatenate([head_rows(qvT, j) for j in range(4)], 1))
        s = jnp.concatenate([s[:SHORT], s[SHORT:] + bias], 0)
        high = jnp.max(s, axis=0, keepdims=True)
        p = jnp.exp2(s - high)
        total = jnp.sum(p, axis=0, keepdims=True)
        o = nn(v_o[:, cols].T, p.astype(BF16)) * (1.0 / total)
        L = high + jnp.log2(total)
        per_head = [slice(ROWS_E * j, ROWS_E * (j + 1)) for j in range(4)]
        ov = jnp.concatenate([o[HD * j : HD * (j + 1), per_head[j]] for j in range(4)], 0)
        oT_seen = nt(ov.astype(BF16), pick_s[...])
        terms, left = [], jnp.concatenate([L[:, sl] for sl in per_head], 0)
        for _ in range(3):
            terms.append(left.astype(BF16))
            left = left - terms[-1].astype(F32)
        L_seen = nt(jnp.concatenate(terms, 1), jnp.concatenate([pick_s[...]] * 3, 1))
        outs = []
        for j in range(4):
            rows = slice(HD * j, HD * (j + 1))
            s = nn(kvg, head_rows(qT, j)) + slot_bias
            before = high_s[g, j : j + 1, :]
            high = jnp.maximum(jnp.max(s, axis=0, keepdims=True), before)
            p = jnp.exp2(s - high)
            kept = jnp.exp2(before - high)
            total = jnp.sum(p, axis=0, keepdims=True) + sum_s[g, j : j + 1, :] * kept
            o = nn(vvT[rows], p.astype(BF16)) + oT_s[g, rows, :] * kept
            o = jnp.where(seen_row, oT_seen[rows], o * (1.0 / total))
            outs.append(o.astype(BF16))
            L = high + jnp.log2(total)
            L_o[g, j : j + 1, :] = jnp.where(seen_row, L_seen[j : j + 1], L)
        att_o[:, cols] = jnp.concatenate(outs, 0).T

    for i in range(8, n):
        bring(i)
    engine.finish()
    for i in range(1, n):
        keep(i).wait()


def front(lengths, orders, patches, small_shards, arrays, Z):
    shapes = [(SMALL_ROWS, 128)] + [a.shape for a in arrays]
    n, count = len(shapes), 8 * Z
    cuts = (1, 3, 1, 3, 3, 1, 1, 1, 1, 1, 1)
    chunks = []
    for i in (0, 6, 7, 1, 2, 3, 4, 5, 8, 9, 10):
        w = shapes[i][1] // cuts[i]
        chunks += [(i, w * t, w) for t in range(cuts[i])]
    slots, W = patches.shape
    Fw, dW, dF = shapes[3][1], shapes[5][1], shapes[9][1]
    sd = jax.ShapeDtypeStruct
    outs = [sd((2, Z, 2, 2) + s, BF16) for s in shapes[1:]]
    outs += [sd((1,), jnp.int32), sd((1, ROWS_E), jnp.int32)]
    outs += [sd((8, W), F32), sd((16, dW), F32), sd((1, Fw), F32), sd((1, dF), F32)]
    R = ROWS_E
    outs += [sd((R, W), BF16), sd((R, W), F32), sd((R, 3 * W), BF16), sd((R, W), BF16)]
    outs += [sd((R, W), F32), sd((R, Fw), BF16), sd((R, Fw), F32), sd((HEADS_E, R, R), F32)]
    outs += [sd((slots, dW), F32)] + [sd((slots, dW), BF16)] * 4
    outs += [sd((dW // GROUP, 4, slots), F32)]
    m = len(chunks)
    given = (*small_shards, *arrays)
    return pl.pallas_call(
        functools.partial(front_kernel, Z, chunks),
        out_shape=outs,
        in_specs=[S, V, A] + [A] * 14,
        out_specs=[A] * (n - 1) + [S] + [V] * 19,
        scratch_shapes=[pltpu.VMEM(a.shape, F32) for a in given]
        + [pltpu.VMEM(s, BF16) for s in shapes]
        + [pltpu.VMEM((2, Z, 2, 2) + s, BF16) for s in shapes]
        + [pltpu.VMEM((slots, W), BF16), D((15,)), D((n - 1,))]
        + [pltpu.VMEM((slots, R), BF16), pltpu.VMEM((slots, 1), F32)]
        + [pltpu.VMEM((dW // GROUP, 4, slots), F32)] * 2
        + [pltpu.VMEM((dW // GROUP, GROUP, slots), F32), pltpu.VMEM((R, 3 * dW), BF16)]
        + [D((m,)), D((m, Z - 1)), D((m, Z - 1))]
        + [D((m, 4)), D((m, 4)), D((m, 5)), D((m, 5))],
        compiler_params=pltpu.CompilerParams(
            collective_id=0, has_side_effects=True, vmem_limit_bytes=62 * 2**20
        ),
    )(lengths, orders, patches, *given)


def dec_mid_kernel(steps, FC, info, x_r, o_r, cot_r, gains, bias, proj, fc1, fc2,
                   dec_o, gx1_o, go_o, gfc2_o, gfc1_o, gproj_o, gvec_o, gbias_o, *acc):
    i = pl.program_id(0)
    n, W = x_r.shape
    Fw = fc1.shape[1]
    if steps > 1:
        afc2, afc1, aproj = acc
        @pl.when(i == 0)
        def _():
            for ref in (afc2, afc1, aproj): ref[...] = jnp.zeros_like(ref)
    @pl.when(i == 0)
    def _():
        for ref in (gvec_o, gbias_o): ref[...] = jnp.zeros_like(ref)
    live = lax.broadcasted_iota(jnp.int32, (n, 1), 0) + i * n < info[0]
    o = o_r[...]
    x1 = x_r[...] + (nn(o, proj[...]) + gains[6:7])
    hat, r = norm_parts(x1)
    h2 = (hat * (1.0 + gains[2:3]) + gains[3:4]).astype(BF16)
    G = jnp.where(live, cot_r[...].astype(F32), 0.0)
    gy = G.astype(BF16)
    def first(c):
        sl = slice(c*FC, (c+1)*FC)
        return nn(h2, fc1[:, sl]), nt(gy, fc2[sl, :])
    nc = Fw//FC
    y = None; gh2 = None
    nxt = first(0)
    for c in range(nc):
        sl = slice(c*FC, (c+1)*FC)
        z, gu = nxt
        if c+1 < nc: nxt = first(c+1)
        u, dg = gelu_parts(z + bias[:, sl])
        u = u.astype(BF16)
        gz32 = gu * dg
        gz = gz32.astype(BF16)
        yc = nn(u, fc2[sl, :])
        y = yc if y is None else y + yc
        gc = nt(gz, fc1[:, sl])
        gh2 = gc if gh2 is None else gh2 + gc
        gbias_o[:, sl] += col_sum(gz.astype(F32))
        if steps > 1:
            afc2[sl, :] += tn(u, gy)
            afc1[:, sl] += tn(h2, gz)
        else:
            gfc2_o[sl, :] = tn(u, gy).astype(BF16)
            gfc1_o[:, sl] = tn(h2, gz).astype(BF16)
    y = x1 + (y + gains[7:8])
    dec_o[...] = jnp.where(live, y, 0.0).astype(BF16)
    gvec_o[0:1, :] += col_sum(gh2 * hat)
    gvec_o[1:2, :] += col_sum(gh2)
    gx1 = G + norm_back(gh2, hat, r, gains[2:3])
    gx1_o[...] = gx1
    ga = gx1.astype(BF16)
    gvec_o[2:3, :] += col_sum(ga.astype(F32))
    gvec_o[3:4, :] += col_sum(G)
    go_o[...] = nt(ga, proj[...]).astype(BF16)
    if steps > 1:
        aproj[...] += tn(o, ga)
        @pl.when(i == steps - 1)
        def _():
            gfc2_o[...] = afc2[...].astype(BF16)
            gfc1_o[...] = afc1[...].astype(BF16)
            gproj_o[...] = aproj[...].astype(BF16)
    else:
        gproj_o[...] = tn(o, ga).astype(BF16)

def dec_mid(info, x, o, cot, gains, bias, proj, fc1, fc2, tile=1024, FC=1024):
    n, W = x.shape
    sd = jax.ShapeDtypeStruct
    full = lambda a: pl.BlockSpec(a.shape, lambda i: (0,)*a.ndim)
    row = pl.BlockSpec((tile, W), lambda i: (i, 0))
    Fw = fc1.shape[1]
    outs = (sd((n, W), BF16), sd((n, W), F32), sd((n, W), BF16), sd(fc2.shape, BF16), sd(fc1.shape, BF16), sd(proj.shape, BF16), sd((8, W), F32), sd((1, Fw), F32))
    return pl.pallas_call(functools.partial(dec_mid_kernel, n//tile, FC), grid=(n//tile,), out_shape=outs,
        in_specs=[S, row, row, row, full(gains), full(bias), full(proj), full(fc1), full(fc2)],
        out_specs=(row, row, row) + tuple(full(a) for a in outs[3:]),
        scratch_shapes=[pltpu.VMEM(w.shape, F32) for w in (fc2, fc1, proj)] if n > tile else [],
        compiler_params=params(60))(info, x, o, cot, gains, bias, proj, fc1, fc2)

def dec_post_kernel(steps, info, places, x_r, gx1_r, gq_r, gk_r, gv_r, gains, qkv, gqkv_o, gposT_o, gemb_o, gvec_o, aqkv, aemb):
    i = pl.program_id(0)
    @pl.when(i == 0)
    def _():
        for ref in (aqkv, aemb, gvec_o): ref[...] = jnp.zeros_like(ref)
    n = x_r.shape[0]
    x = x_r[...]
    hat, r = norm_parts(x)
    h = (hat * (1.0 + gains[0:1]) + gains[1:2]).astype(BF16)
    gm = jnp.concatenate([gq_r[...], gk_r[...], gv_r[...]], 1)
    W = x.shape[1]
    aqkv[...] += tn(h, gm)
    gh = nt(gm, qkv[...])
    gvec_o[0:1, :] += col_sum(gh * hat)
    gvec_o[1:2, :] += col_sum(gh)
    gvec_o[4:5, :] += col_sum(gq_r[...].astype(F32))
    gvec_o[5:6, :] += col_sum(gv_r[...].astype(F32))
    gx = gx1_r[...] + norm_back(gh, hat, r, gains[0:1])
    gxb = gx.astype(BF16)
    gposT_o[...] = gxb.T
    pos_i = lax.broadcasted_iota(jnp.int32, (n, ROWS_E), 0) + i * n
    rr = lax.broadcasted_iota(jnp.int32, (n, ROWS_E), 1)
    pick = ((pos_i == places[...]) & (rr < info[0] // 10)).astype(BF16)
    seen = jnp.sum(pick.astype(F32), axis=1, keepdims=True)
    aemb[...] += tn(pick, gxb)
    gvec_o[9:10, :] += col_sum(gx * (1.0 - seen))
    @pl.when(i == steps - 1)
    def _():
        gqkv_o[...] = aqkv[...].astype(BF16)
        gemb_o[...] = aemb[...].astype(BF16)
        gvec_o[8:9, :] = col_sum(aemb[...])

def dec_post(info, places, x, gx1, gq, gk, gv, gains, qkv, tile=256):
    n, W = x.shape
    sd = jax.ShapeDtypeStruct
    full = lambda a: pl.BlockSpec(a.shape, lambda i: (0,)*a.ndim)
    row = pl.BlockSpec((tile, W), lambda i: (i, 0))
    outs = (sd(qkv.shape, BF16), sd((W, n), BF16), sd((ROWS_E, W), BF16), sd((16, W), F32))
    return pl.pallas_call(functools.partial(dec_post_kernel, n//tile), grid=(n//tile,), out_shape=outs,
        in_specs=[S, full(places), row, row, row, row, row, full(gains), full(qkv)],
        out_specs=(full(outs[0]), pl.BlockSpec((W, tile), lambda i: (0, i)), full(outs[2]), full(outs[3])),
        scratch_shapes=[pltpu.VMEM(qkv.shape, F32), pltpu.VMEM((ROWS_E, W), F32)],
        compiler_params=params())(info, places, x, gx1, gq, gk, gv, gains, qkv)

SPOTS = (0, 2, 4, 6, 8, 10, 12, 14, 16)


def attend_back_kernel(Z, chunks, info, q_ref, k_ref, v_ref, go_ref, o_ref, L_ref, *refs):
    blocks, (gq_ref, gk_ref, gv_ref), outs, rest = refs[:3], refs[3:6], refs[6:9], refs[9:]
    lands, rest = rest[:3], rest[3:]
    engine = Scatter(Z, take_buffers(rest[:-7], blocks, (True,) * 3, lands), chunks, rest[-7:])
    g = pl.program_id(0)

    @pl.when(g == 0)
    def _():
        engine.greet()

    q = q_ref[...]
    k = k_ref[...]
    v = v_ref[...]
    go = go_ref[...]
    bias = dead_bias(info[0], k.shape[0])
    qT, kT, goT, oT = q.T, k.T, go.T, o_ref[...].T
    inner_all = goT.astype(F32) * oT.astype(F32)
    ak = av = None
    gqs = []
    for j in range(4):
        for step in range(4):
            if 4 * step + j in SPOTS:

                @pl.when(g == step)
                def _():
                    engine.tick(SPOTS.index(4 * step + j))

        rows = slice(HD * j, HD * (j + 1))
        s = nn(k, head_rows(qT, j))
        s = jnp.concatenate([s[:SHORT], s[SHORT:] + bias], 0)
        p = jnp.exp2(s - L_ref[0, j : j + 1, :])
        gp = nn(v, head_rows(goT, j))
        inner = jnp.sum(inner_all[rows], axis=0, keepdims=True)
        gs = (p * (gp - inner)).astype(BF16)
        a = nn(p.astype(BF16), head_lanes(go, j))
        b = nn(gs, head_lanes(q, j))
        av = a if av is None else av + a
        ak = b if ak is None else ak + b
        gqs.append((nn(kT[rows], gs) * math.log(2.0)).astype(BF16))
    gq_ref[...] = jnp.concatenate(gqs, 0).T
    gk_ref[...] = (ak * HD**-0.5).astype(BF16)
    gv_ref[...] = av.astype(BF16)

    @pl.when(g == 3)
    def _():
        engine.tick(SPOTS.index(16))
        engine.finish()
        for out, land in zip(outs, lands):
            out[...] = land[...]


def attend_back(info, q, k, v, go, o, L, grads, Z):
    n, W = k.shape
    blk = pl.BlockSpec((n, GROUP), lambda g: (0, g))
    shapes = [a.shape[4:] for a in grads]
    chunks = []
    for i, (r, c) in enumerate(shapes[:2]):
        chunks += [(i, 0, c // 2), (i, c // 2, c // 2)]
    chunks.append((2, 0, shapes[2][1]))
    buffers, sems = scatter_buffers(shapes, (True,) * 3, Z, chunks)
    outs = [jax.ShapeDtypeStruct((Z, *s), BF16) for s in shapes]
    return pl.pallas_call(
        functools.partial(attend_back_kernel, Z, chunks),
        grid=(W // GROUP,),
        out_shape=[jax.ShapeDtypeStruct((n, W), BF16)] * 3 + outs,
        in_specs=[S, blk, blk, blk, blk, blk, pl.BlockSpec((1, 4, n), lambda g: (g, 0, 0))]
        + [A] * 3,
        out_specs=[blk] * 3 + [V] * 3,
        scratch_shapes=[pltpu.VMEM(a.shape, BF16) for a in outs] + buffers + sems,
        compiler_params=pltpu.CompilerParams(
            collective_id=1, has_side_effects=True, vmem_limit_bytes=60 * 2**20
        ),
    )(info, q, k, v, go, o, L, *grads)


def enc_bwd_kernel(Z, chunks, *refs):
    given, small_in, blocks_in = refs[:14], refs[14:18], refs[18:20]
    gx_o, outs, rest = refs[20], refs[21:29], refs[29:]
    local, made, rest = rest[:13], rest[13:19], rest[19:]
    e_vec, e_bias, whole, sem = rest[-11:-7]
    loaded = (True, True) + (False,) * 6
    engine = Scatter(
        Z, take_buffers(rest[:-11], (*blocks_in, *made), loaded, outs), chunks, rest[-7:]
    )
    g_embed, g_fc2, g_fc1, g_proj, g_qkv, g_small = made
    gains, mid_vec, post_vec, d_bias = small_in
    places = (*local, local[8].at[:, pl.ds(0, given[13].shape[1])])
    loads = [pltpu.make_async_copy(given[i], places[i], sem.at[i]) for i in range(14)]
    for load in loads[:13]:
        load.start()

    def got(i):
        loads[i].wait()
        return places[i][...]

    engine.greet()
    steps = iter(range(engine.ticks))

    def tick():
        engine.tick(next(steps))

    def store(ref, value):
        ref[...] = value.astype(BF16).reshape(ref.shape)

    tick()
    ge = got(0)
    store(g_embed, tn(got(1), ge))
    gy = nt(ge, got(2)).astype(BF16)
    G = gy.astype(F32)
    tick()
    u = got(3)
    store(g_fc2, tn(u, gy))
    tick()
    gz = (nt(gy, got(4)) * got(5)).astype(BF16)
    e_bias[...] = col_sum(gz.astype(F32))
    tick()
    hat2, r2 = norm_parts(got(6))
    h2 = (hat2 * (1.0 + gains[2:3]) + gains[3:4]).astype(BF16)
    store(g_fc1, tn(h2, gz))
    tick()
    gh2 = nt(gz, got(8))
    loads[13].start()
    e_vec[2:3, :] = col_sum(gh2 * hat2)
    e_vec[3:4, :] = col_sum(gh2)
    gx1 = G + norm_back(gh2, hat2, r2, gains[2:3])
    ga = gx1.astype(BF16)
    e_vec[6:7, :] = col_sum(ga.astype(F32))
    e_vec[7:8, :] = col_sum(G)
    store(g_proj, tn(got(7), ga))
    tick()
    go = nt(ga, got(9)).astype(BF16)
    for i in (10, 11, 12):
        loads[i].wait()
    m_r, p_r, x_r = places[10:13]
    W = gx1.shape[1]
    hs = W // HEADS_E
    gq, gk, gv = [], [], []
    for j in range(HEADS_E):
        q = m_r[:, hs * j : hs * (j + 1)]
        k = m_r[:, W + hs * j : W + hs * (j + 1)]
        val = m_r[:, 2 * W + hs * j : 2 * W + hs * (j + 1)]
        g = go[:, hs * j : hs * (j + 1)]
        p = p_r[j]
        gv.append(tn(p.astype(BF16), g).astype(BF16))
        gp = nt(g, val)
        gs = (p * (gp - jnp.sum(gp * p, axis=-1, keepdims=True))).astype(BF16)
        gq.append((nn(gs, k) * hs**-0.5).astype(BF16))
        gk.append((tn(gs, q) * hs**-0.5).astype(BF16))
        if j == HEADS_E // 2:
            tick()
    gm = jnp.concatenate(gq + gk + gv, 1)
    tick()
    e_vec[4:5, :] = col_sum(gm[:, :W].astype(F32))
    e_vec[5:6, :] = col_sum(gm[:, 2 * W :].astype(F32))
    hat, r = norm_parts(x_r[...])
    h = (hat * (1.0 + gains[0:1]) + gains[1:2]).astype(BF16)
    store(g_qkv, tn(h, gm))
    tick()
    gh = nt(gm, got(13))
    e_vec[0:1, :] = col_sum(gh * hat)
    e_vec[1:2, :] = col_sum(gh)
    gx_o[...] = gx1 + norm_back(gh, hat, r, gains[0:1])
    pack(g_small, e_vec, e_bias, mid_vec, post_vec, d_bias, whole)
    for t in steps:
        engine.tick(t)
    engine.finish()


def pack(out, e_vec, e_bias, mid_vec, post_vec, d_bias, whole):
    Z = out.shape[1]
    count = 8 * Z
    whole[...] = jnp.zeros_like(whole)
    whole[0:2] = post_vec[0:2]
    whole[2:4] = mid_vec[0:2]
    whole[4:6] = post_vec[4:6]
    whole[6:8] = mid_vec[2:4]
    whole[8:10] = post_vec[8:10]
    out[...] = jnp.zeros_like(out)
    for ref, row, rows in ((e_vec, 0, 8), (whole, 8, 16), (e_bias, 24, 1), (d_bias, 25, 1)):
        w = ref.shape[1] // count
        values = ref[...].astype(BF16)
        for i in range(count):
            at = (i // (4 * Z), i // 4 % Z, i // 2 % 2, i % 2)
            out[(*at, slice(row, row + rows), slice(0, w))] = values[:, w * i : w * i + w]


def enc_bwd(encoded, gemb, embed, kept, mats, small_in, blocks_in, Z):
    x, m, o, x1, u, dg, p = kept
    qkv, proj, fc1, fc2 = mats
    given = (gemb, encoded, embed, u, fc2, dg, x1, o, fc1, proj, m, p, x, qkv)
    count = 8 * Z

    def block_shape(a):
        return (a.shape[0] // count, a.shape[1])

    shapes = [a.shape[4:] for a in blocks_in]
    shapes += [block_shape(a) for a in (embed, fc2, fc1, proj, qkv)] + [(SMALL_ROWS, 128)]
    W, Fw = fc1.shape
    chunks = [(0, 0, shapes[0][1]), (1, 0, shapes[1][1]), (2, 0, shapes[2][1])]
    chunks += [(3, t * W // 3, W // 3) for t in range(3)]
    chunks += [(4, t * Fw // 3, Fw // 3) for t in range(3)]
    chunks += [(5, 0, W)] + [(6, t * W, W) for t in range(3)] + [(7, 0, 128)]
    loaded = (True, True) + (False,) * 6
    buffers, sems = scatter_buffers(shapes, loaded, Z, chunks)
    sd = jax.ShapeDtypeStruct
    return pl.pallas_call(
        functools.partial(enc_bwd_kernel, Z, chunks),
        out_shape=[sd(x.shape, F32)] + [sd((Z, *s), BF16) for s in shapes],
        in_specs=[A] * 14 + [V] * 4 + [A] * 2,
        out_specs=[V] * 9,
        scratch_shapes=[pltpu.VMEM(a.shape, a.dtype) for a in given[:13]]
        + [pltpu.VMEM((2, Z, 2, 2, *s), BF16) for s in shapes[2:]]
        + buffers
        + [pltpu.VMEM((8, W), F32), pltpu.VMEM((1, Fw), F32), pltpu.VMEM((16, embed.shape[1]), F32)]
        + [D((14,))]
        + sems,
        compiler_params=pltpu.CompilerParams(
            collective_id=2, has_side_effects=True, vmem_limit_bytes=62 * 2**20
        ),
    )(*given, *small_in, *blocks_in)


def last_kernel(n, info, places, gx, *refs):
    ins, g_patch, outs = refs[:n], refs[n], refs[n + 1 :]
    pick = pick_matrix(places[...], info[0] // 10, g_patch.shape[0])
    g_patch[...] = place_rows(pick, gx[...])

    def total(ref):
        acc = ref[0].astype(F32)
        for d in range(1, ref.shape[0]):
            acc = acc + ref[d].astype(F32)
        return acc

    small = total(ins[0])
    for out, row in zip(outs[:4], (0, 8, 24, 25)):
        out[...] = small[row : row + out.shape[0], : out.shape[1]]
    for i, ref in enumerate(ins[1:]):
        outs[4 + i][...] = total(ref)


def last_sums(info, places, gx, arrays, shapes):
    return pl.pallas_call(
        functools.partial(last_kernel, len(arrays)),
        out_shape=[jax.ShapeDtypeStruct(s, F32) for s in shapes],
        in_specs=[S] + [V] * (2 + len(arrays)),
        compiler_params=params(),
    )(info, places, gx, *arrays)


def body(
    patches,
    lengths,
    keep_order,
    e_vectors,
    e_qkv,
    e_proj,
    e_fc1,
    e_fc1_bias,
    e_fc2,
    embed,
    d_vectors,
    dec_pos,
    d_qkv,
    d_proj,
    d_fc1,
    d_fc1_bias,
    d_fc2,
    cotangent,
):
    Z = lax.axis_size("dp") // 4
    slots = patches.shape[1]
    smalls = (e_vectors, d_vectors, e_fc1_bias.reshape(1, -1), d_fc1_bias.reshape(1, -1))
    shards = (e_qkv, e_proj, e_fc1, e_fc2, embed, dec_pos.T, d_qkv, d_proj, d_fc1, d_fc2)
    made = front(lengths, keep_order, patches[0], smalls, shards, Z)
    mats = [m.reshape(-1, m.shape[-1]) for m in made[:10]]
    w_qkv, w_proj, w_fc1, w_fc2, w_embed, posT, dw_qkv, dw_proj, dw_fc1, dw_fc2 = mats
    info, places, e_gains, d_gains, e_bias, d_bias, encoded, *kept = made[10:24]
    x, q, k, v, o, L = made[24:]
    decoded, gx1, go, gd_fc2, gd_fc1, gd_proj, mid_vec, gd_bias = dec_mid(
        info, x, o, cotangent[0], d_gains, d_bias, dw_proj, dw_fc1, dw_fc2
    )

    def blocks(m):
        return m.reshape((2, Z, 2, 2, -1, m.shape[-1]))

    gq, gk, gv, *early = attend_back(
        info, q, k, v, go, o, L, [blocks(m) for m in (gd_fc2, gd_fc1, gd_proj)], Z
    )
    gd_qkv, g_posT, gemb, post_vec = dec_post(
        info, places, x, gx1, gq, gk, gv, d_gains, dw_qkv
    )
    gx, *late = enc_bwd(
        encoded,
        gemb,
        w_embed,
        kept,
        (w_qkv, w_proj, w_fc1, w_fc2),
        (e_gains, mid_vec, post_vec, gd_bias),
        (blocks(gd_qkv), blocks(g_posT)),
        Z,
    )
    pd_qkv, p_pos, p_embed, p_fc2, p_fc1, p_proj, p_qkv, p_small = late
    parts = (p_small, p_qkv, p_proj, p_fc1, p_fc2, p_embed, p_pos, pd_qkv, *early[::-1])
    shapes = [(slots, patches.shape[2])] + [m.shape for m in smalls + shards]
    g_patch, *out = last_sums(info, places, gx, parts, shapes)
    re_vec, rd_vec, re_bias, rd_bias = out[:4]
    re_qkv, re_proj, re_fc1, re_fc2, r_embed, r_pos, rd_qkv, rd_proj, rd_fc1, rd_fc2 = out[4:]
    return (
        decoded[None],
        g_patch[None],
        re_vec,
        re_qkv,
        re_proj,
        re_fc1,
        re_bias.reshape(-1),
        re_fc2,
        r_embed,
        rd_vec,
        r_pos.T,
        rd_qkv,
        rd_proj,
        rd_fc1,
        rd_bias.reshape(-1),
        rd_fc2,
    )


def solution(mesh):
    rows, columns, cubes = P(AXES, None), P(None, AXES), P(AXES, None, None)
    weights = (columns, rows, rows, rows, P(AXES), rows, rows, columns, columns)
    weights = weights + (rows, rows, rows, P(AXES), rows)
    return jax.shard_map(
        body,
        mesh=mesh,
        in_specs=(cubes, P(), P()) + weights + (cubes,),
        out_specs=(cubes, cubes) + weights,
        check_vma=False,
    )
```

```python
import functools
import math

import jax
import jax.numpy as jnp
from jax import lax
from jax.experimental import pallas as pl
from jax.experimental.pallas import tpu as pltpu
from jax.sharding import PartitionSpec as P

HEADS_E = 12
HEADS_D = 16
VIS = 104
SHORT = 576
HD = 32
GROUP = 128
F32 = jnp.float32
BF16 = jnp.bfloat16
AXES = ("segment", "dp")
MESH = pl.DeviceIdType.MESH
ROWS_E = 128
NORM_EPS = 1e-06
FAR_BELOW = -1e30


SMALL_ROWS = 32


def place():
    s = lax.axis_index("segment")
    dp = lax.axis_index("dp")
    return s, dp // 4, (dp // 2) % 2, dp % 2


def device(s, z, y, c):
    return (s, (z * 2 + y) * 2 + c)


def halves(columns):
    return (columns // 2, columns // 2) if columns % 256 == 0 else (columns, 0)


def greet(peers):
    barrier = pltpu.get_barrier_semaphore()
    for peer in peers:
        pl.semaphore_signal(barrier, inc=1, device_id=peer, device_id_type=MESH)
    pl.semaphore_wait(barrier, len(peers))


class Gather:
    def __init__(self, Z, shards, outs, chunks, sems):
        self.Z, self.shards, self.outs, self.chunks = Z, shards, outs, chunks
        self.loc, self.zs, self.zr, self.ms, self.mr, self.cs, self.cr = sems
        self.s, self.z, self.y, self.c = s, z, y, c = place()
        self.X, self.Y = device(1 - s, z, y, c), device(s, z, 1 - y, c)
        self.C = device(s, z, y, 1 - c)
        self.z_peers = [device(s, lax.rem(z + d, Z), y, c) for d in range(1, Z)]

    def greet(self):
        greet(self.z_peers + [self.X, self.Y, self.C])

    def copy(self, src, dst, ss, rs, target):
        return pltpu.make_async_remote_copy(
            src_ref=src,
            dst_ref=dst,
            send_sem=ss,
            recv_sem=rs,
            device_id=target,
            device_id_type=MESH,
        )

    def own(self, m):
        i, start, width = self.chunks[m]
        cols = pl.ds(start, width)
        return pltpu.make_async_copy(
            self.shards[i].at[:, cols],
            self.outs[i].at[self.s, self.z, self.y, self.c, :, cols],
            self.loc.at[m],
        )

    def copies(self, m, stage):
        i, start, width = self.chunks[m]
        ka, kb = halves(width)
        s, z, y, c = self.s, self.z, self.y, self.c
        o = self.outs[i]
        cols, A = pl.ds(start, width), pl.ds(start, ka)
        B = pl.ds(start + ka, kb) if kb else None
        if stage == 0:
            return [
                self.copy(
                    self.shards[i].at[:, cols],
                    o.at[s, z, y, c, :, cols],
                    self.zs.at[m, d],
                    self.zr.at[m, d],
                    self.z_peers[d],
                )
                for d in range(self.Z - 1)
            ]
        if stage == 1:
            made = [(o.at[s, :, y, c, :, A], 0, self.X)]
            if kb:
                made.append((o.at[s, :, y, c, :, B], 1, self.Y))
        elif stage == 2:
            made = [(o.at[:, :, y, c, :, A], 2, self.Y)]
            if kb:
                made.append((o.at[s, :, :, c, :, B], 3, self.X))
        elif stage == 11:
            made = [(o.at[s, :, y, c, :, cols], 0, self.C)]
        elif stage == 12:
            made = [(o.at[1 - s, :, y, c, :, A], 1, self.C)]
            if kb:
                made.append((o.at[s, :, 1 - y, c, :, B], 2, self.C))
        else:
            made = [(o.at[:, :, 1 - y, c, :, A], 3, self.C)]
            if kb:
                made.append((o.at[1 - s, :, :, c, :, B], 4, self.C))
        ss, rs = (self.cs, self.cr) if stage > 10 else (self.ms, self.mr)
        return [self.copy(ref, ref, ss.at[m, k], rs.at[m, k], target) for ref, k, target in made]

    def stage(self, m, stage):
        if stage == 0:
            self.own(m).start()
        else:
            if stage == 1:
                self.own(m).wait()
            for copy in self.copies(m, stage - 1):
                copy.wait_recv()
        if stage < 3:
            for copy in self.copies(m, stage):
                copy.start()
        if stage > 0:
            for copy in self.copies(m, stage + 10):
                copy.start()

    @property
    def ticks(self):
        return len(self.chunks) + 6

    def tick(self, t):
        for k in range(4):
            if 0 <= t - 2 * k < len(self.chunks):
                self.stage(t - 2 * k, k)

    def arrived(self, i):
        for m, chunk in enumerate(self.chunks):
            if chunk[0] == i:
                for stage in (11, 12, 13):
                    for copy in self.copies(m, stage):
                        copy.wait_recv()

    def finish(self):
        for m in range(len(self.chunks)):
            for stage in (0, 1, 2, 11, 12, 13):
                for copy in self.copies(m, stage):
                    copy.wait_send()


class Scatter:
    def __init__(self, Z, arrays, chunks, sems):
        self.Z, self.arrays, self.chunks = Z, arrays, chunks
        self.loc, self.cs, self.cr, self.ms, self.mr, self.zs, self.zr = sems
        self.s, self.z, self.y, self.c = s, z, y, c = place()
        self.X, self.Y = device(1 - s, z, y, c), device(s, z, 1 - y, c)
        self.C = device(s, z, y, 1 - c)
        self.z_peers = [device(s, lax.rem(z + d, Z), y, c) for d in range(1, Z)]

    def greet(self):
        greet(self.z_peers + [self.X, self.Y, self.C])

    def parts(self, m):
        i, start, width = self.chunks[m]
        ka, kb = halves(width)
        return i, start, width, ka, kb, (start // 2 if kb else start)

    def held(self, i, index, columns):
        blocks, held = self.arrays[i][:2]
        if held is None:
            ss, zz, yy = index
            return blocks.at[ss, zz, yy, self.c, :, columns]
        return held.at[(*index, slice(None), columns)]

    def copy(self, src, dst, ss, rs, target):
        return pltpu.make_async_remote_copy(
            src_ref=src,
            dst_ref=dst,
            send_sem=ss,
            recv_sem=rs,
            device_id=target,
            device_id_type=MESH,
        )

    def own(self, m):
        i, start, width, *_ = self.parts(m)
        blocks, held = self.arrays[i][:2]
        if held is None:
            return None
        cols = pl.ds(start, width)
        return pltpu.make_async_copy(
            blocks.at[:, :, :, self.c, :, cols], held.at[:, :, :, :, cols], self.loc.at[m]
        )

    def copies(self, m, stage):
        i, start, width, ka, kb, at = self.parts(m)
        s, z, y, c, Z = self.s, self.z, self.y, self.c, self.Z
        blocks, held, R0, R1A, R1B, R2A, R2B, out = self.arrays[i]
        cols, A, B = pl.ds(start, width), pl.ds(start, ka), pl.ds(start + ka, kb)
        half = pl.ds(at, ka)
        full = slice(None)
        if stage == 0:
            return [
                self.copy(
                    blocks.at[:, :, :, 1 - c, :, cols],
                    R0.at[:, :, :, :, cols],
                    self.cs.at[m],
                    self.cr.at[m],
                    self.C,
                )
            ]
        if stage == 1:
            made = [(self.held(i, (full, full, 1 - y), A), R1A.at[:, :, :, half], self.Y)]
            if kb:
                made.append((self.held(i, (1 - s, full, full), B), R1B.at[:, :, :, half], self.X))
        elif stage == 2:
            made = [(self.held(i, (1 - s, full, y), A), R2A.at[:, :, half], self.X)]
            if kb:
                made.append((self.held(i, (s, full, 1 - y), B), R2B.at[:, :, half], self.Y))
        else:
            return [
                self.copy(
                    self.held(i, (s, lax.rem(z + d, Z), y), cols),
                    out.at[d, :, cols],
                    self.zs.at[m, d - 1],
                    self.zr.at[m, d - 1],
                    self.z_peers[d - 1],
                )
                for d in range(1, Z)
            ]
        k = 2 * (stage - 1)
        return [
            self.copy(src, dst, self.ms.at[m, k + j], self.mr.at[m, k + j], target)
            for j, (src, dst, target) in enumerate(made)
        ]

    def add(self, i, index, columns, other):
        ref = self.held(i, index, columns)
        ref[...] = (ref[...].astype(F32) + other[...].astype(F32)).astype(BF16)

    def stage(self, m, stage):
        i, start, width, ka, kb, at = self.parts(m)
        s, z, y, Z = self.s, self.z, self.y, self.Z
        blocks, held, R0, R1A, R1B, R2A, R2B, out = self.arrays[i]
        cols, A, B = pl.ds(start, width), pl.ds(start, ka), pl.ds(start + ka, kb)
        half = pl.ds(at, ka)
        if stage == 0:
            own = self.own(m)
            if own is not None:
                own.start()
        else:
            if stage == 1 and held is not None:
                self.own(m).wait()
            for copy in self.copies(m, stage - 1):
                copy.wait_recv()
        if stage == 1:

            @pl.loop(0, 4 * Z)
            def _(t):
                index = (t // (Z * 2), (t // 2) % Z, t % 2)
                self.add(i, index, cols, R0.at[(*index, slice(None), cols)])

        elif stage == 2:

            @pl.loop(0, 2 * Z)
            def _(t):
                u, zz = t // Z, t % Z
                self.add(i, (u, zz, y), A, R1A.at[u, zz, :, half])
                if kb:
                    self.add(i, (s, zz, u), B, R1B.at[zz, u, :, half])

        elif stage == 3:

            @pl.loop(0, Z)
            def _(zz):
                self.add(i, (s, zz, y), A, R2A.at[zz, :, half])
                if kb:
                    self.add(i, (s, zz, y), B, R2B.at[zz, :, half])

        elif stage == 4:
            out[0, :, cols] = self.held(i, (s, z, y), cols)[...]
            return
        for copy in self.copies(m, stage):
            copy.start()

    @property
    def ticks(self):
        return len(self.chunks) + 4

    def tick(self, t):
        for k in range(5):
            if 0 <= t - k < len(self.chunks):
                self.stage(t - k, k)

    def finish(self):
        for m in range(len(self.chunks)):
            for stage in range(4):
                for copy in self.copies(m, stage):
                    copy.wait_send()


def scatter_buffers(shapes, loaded, Z, chunks):
    refs = []
    for (r, k), load in zip(shapes, loaded):
        ka, kb = halves(k)
        kb = max(kb, 128)
        if load:
            refs.append((2, Z, 2, r, k))
        refs += [(2, Z, 2, r, k), (2, Z, r, ka), (Z, 2, r, kb), (Z, r, ka), (Z, r, kb)]
    n = len(chunks)
    D = pltpu.SemaphoreType.DMA
    return [pltpu.VMEM(s, BF16) for s in refs], [
        D((n,)),
        D((n,)),
        D((n,)),
        D((n, 4)),
        D((n, 4)),
        D((n, Z - 1)),
        D((n, Z - 1)),
    ]


def take_buffers(refs, blocks, loaded, outs):
    refs = list(refs)
    arrays = []
    for block, load, out in zip(blocks, loaded, outs):
        held = refs.pop(0) if load else None
        arrays.append((block, held, *(refs.pop(0) for _ in range(5)), out))
    return arrays


def nn(a, b): return jnp.dot(a, b, preferred_element_type=F32)
def nt(a, b): return lax.dot_general(a, b, (((1,), (1,)), ((), ())), preferred_element_type=F32)
def tn(a, b): return lax.dot_general(a, b, (((0,), (0,)), ((), ())), preferred_element_type=F32)

def norm_parts(x):
    center = x - jnp.mean(x, axis=-1, keepdims=True)
    r = lax.rsqrt(jnp.mean(center * center, axis=-1, keepdims=True) + NORM_EPS)
    return center * r, r

def norm_back(g, hat, r, gain):
    w = g * (1.0 + gain)
    return r * (w - jnp.mean(w, axis=-1, keepdims=True) - hat * jnp.mean(w * hat, axis=-1, keepdims=True))

def gelu_parts(z):
    x = jnp.abs(z) * math.sqrt(0.5)
    t = 1.0 / (1.0 + 0.3275911 * x)
    e = jnp.exp(-(x * x))
    poly = t * (0.254829592 + t * (-0.284496736 + t * (1.421413741 + t * (-1.453152027 + t * 1.061405429))))
    half = 0.5 * poly * e
    cdf = jnp.where(z > 0, 1.0 - half, half)
    return z * cdf, cdf + z * e * (1.0 / math.sqrt(2.0 * math.pi))

def col_sum(m): return jnp.sum(m, axis=0, keepdims=True)

def pick_matrix(places_row, keep_count, slots):
    pos = lax.broadcasted_iota(jnp.int32, (slots, ROWS_E), 0)
    r = lax.broadcasted_iota(jnp.int32, (slots, ROWS_E), 1)
    return ((pos == places_row) & (r < keep_count)).astype(BF16)

V = pl.BlockSpec(memory_space=pltpu.VMEM); A = pl.BlockSpec(memory_space=pl.ANY); S = pl.BlockSpec(memory_space=pltpu.SMEM)
D = pltpu.SemaphoreType.DMA
def params(mb=56): return pltpu.CompilerParams(vmem_limit_bytes=mb*2**20)

def head_rows(block, j):
    parts = []
    if j > 0: parts.append(jnp.zeros((HD*j, block.shape[1]), block.dtype))
    parts.append(block[HD*j:HD*(j+1)])
    if j < 3: parts.append(jnp.zeros((HD*(3-j), block.shape[1]), block.dtype))
    return jnp.concatenate(parts, 0)

def head_lanes(block, j):
    lane = lax.broadcasted_iota(jnp.int32, block.shape, 1)
    return jnp.where((lane >= HD*j) & (lane < HD*(j+1)), block, jnp.zeros_like(block))

def dead_bias(count, n):
    return jnp.where(lax.broadcasted_iota(jnp.int32, (n - SHORT, 1), 0) + SHORT < count, 0.0, FAR_BELOW)

SMALL_AT = ((0, 8), (8, 16), (24, 1), (25, 1))


def place_rows(pick, rows):
    terms, left = [], rows
    for _ in range(3):
        terms.append(left.astype(BF16))
        left = left - terms[-1].astype(F32)
    return nn(jnp.concatenate([pick] * 3, 1), jnp.concatenate(terms, 0))


def front_kernel(Z, chunks, *refs):
    n = 11
    lengths, orders, patches_h, given, refs = refs[0], refs[1], refs[2], refs[3:17], refs[17:]
    fulls, refs = refs[: n - 1], refs[n - 1 :]
    info, places, e_gains, d_gains, e_bias, d_bias = refs[:6]
    enc_o, x_o, m_o, o_o, x1_o, u_o, dg_o, p_o, X_o, q_o, k_o, v_o, att_o, L_o = refs[6:20]
    refs = refs[20:]
    shards, cast, here, refs = refs[:14], refs[14 : 14 + n], refs[14 + n : 14 + 2 * n], refs[14 + 2 * n :]
    patches, get, put, pick_s, bias_s, high_s, sum_s, oT_s, qkv_s = refs[:9]
    engine = Gather(Z, cast, here, chunks, refs[9:])
    loads = [pltpu.make_async_copy(given[i], shards[i], get.at[i]) for i in range(14)]
    for load in loads:
        load.start()
    load_patches = pltpu.make_async_copy(patches_h, patches, get.at[14])
    load_patches.start()
    cube = lax.axis_index(AXES)
    info[0] = lengths[cube]
    heads = orders[:, :ROWS_E]
    mine = lax.broadcasted_iota(jnp.int32, heads.shape, 0) == cube
    places[...] = jnp.sum(jnp.where(mine, heads, 0), axis=0, keepdims=True)
    small = cast[0]
    small[...] = jnp.zeros_like(small)
    for (row, _), k in zip(SMALL_AT, range(4)):
        loads[k].wait()
        small[row : row + shards[k].shape[0], : shards[k].shape[1]] = shards[k][...].astype(BF16)
    engine.greet()
    steps = iter(range(engine.ticks))

    def advance(t):
        if t < len(chunks) and chunks[t][0] and chunks[t][0] not in [m[0] for m in chunks[:t]]:
            i = chunks[t][0]
            loads[i + 3].wait()
            cast[i][...] = shards[i + 3][...].astype(BF16)
        engine.tick(t)

    def tick():
        advance(next(steps))

    def keep(i):
        return pltpu.make_async_copy(here[i], fulls[i - 1], put.at[i - 1])

    def bring(i):
        engine.arrived(i)
        if i:
            keep(i).start()

    def mat(i):
        shape = here[i].shape
        return here[i][...].reshape(8 * Z * shape[4], shape[5])

    for _ in range(7):
        tick()
    bring(0)
    load_patches.wait()
    count = info[0]
    visible = count // 10
    slots = patches.shape[0]
    pick_s[...] = pick_matrix(places[...], visible, slots)
    x = tn(pick_s[...], patches[...])
    x_o[...] = x
    tick()
    bring(6)
    values = here[0][...].reshape(8 * Z, SMALL_ROWS, 128).astype(F32)
    for out, (row, rows) in zip((e_gains, d_gains, e_bias, d_bias), SMALL_AT):
        w = out.shape[1] // (8 * Z)
        out[...] = jnp.concatenate([values[i, row : row + rows, :w] for i in range(8 * Z)], 1)
    tick()
    bring(7)
    X = d_gains[9:10] + mat(6).T.astype(F32)
    X_o[...] = X
    hat, _ = norm_parts(X)
    h = (hat * (1.0 + d_gains[0:1]) + d_gains[1:2]).astype(BF16)
    tick()
    dW = X.shape[1]

    def three(m):
        q = (m[:, :dW] + d_gains[4:5]).astype(BF16)
        k = (m[:, dW : 2 * dW] * (HD**-0.5 * math.log2(math.e))).astype(BF16)
        return q, k, (m[:, 2 * dW :] + d_gains[5:6]).astype(BF16)

    q_o[...], k_o[...], v_o[...] = three(nn(h, mat(7)))
    spot = lax.broadcasted_iota(jnp.int32, (slots, 1), 0)
    seen = jnp.sum(pick_s[...].astype(F32), axis=1, keepdims=True)
    bias_s[...] = jnp.where((spot < count) & (seen < 0.5), 0.0, FAR_BELOW)

    def masked_keys(g, turn):
        cols = pl.ds(pl.multiple_of(g * GROUP, GROUP), GROUP)
        kg = k_o[:, cols]
        qT = q_o[:, cols].T
        vT = v_o[:, cols].T
        for j in range(4):
            if j % 2 == 0:
                turn(j // 2)
            rows = slice(HD * j, HD * (j + 1))
            s = nn(kg, head_rows(qT, j)) + bias_s[...]
            high = jnp.max(s, axis=0, keepdims=True)
            p = jnp.exp2(s - high)
            high_s[g, j : j + 1, :] = high
            sum_s[g, j : j + 1, :] = jnp.sum(p, axis=0, keepdims=True)
            oT_s[g, rows, :] = nn(vT[rows], p.astype(BF16))

    groups = dW // GROUP
    turns = [next(steps) for _ in range(2 * (groups - 1))]

    @pl.loop(0, groups - 1)
    def _(g):
        def turn(k):
            for at in range(groups - 1):

                @pl.when(g == at)
                def _():
                    advance(turns[2 * at + k])

        masked_keys(g, turn)

    bring(1)
    bring(2)
    hat, _ = norm_parts(x)
    h = (hat * (1.0 + e_gains[0:1]) + e_gains[1:2]).astype(BF16)
    W = x.shape[1]
    m = nn(h, mat(1))
    q = (m[:, :W] + e_gains[4:5]).astype(BF16)
    k = m[:, W : 2 * W].astype(BF16)
    val = (m[:, 2 * W :] + e_gains[5:6]).astype(BF16)
    m_o[...] = jnp.concatenate([q, k, val], 1)
    live = lax.broadcasted_iota(jnp.int32, (ROWS_E, ROWS_E), 1) < visible
    hs = W // HEADS_E
    outs = []
    for j in range(HEADS_E):
        sl = slice(hs * j, hs * (j + 1))
        s = jnp.where(live, nt(q[:, sl], k[:, sl]) * hs**-0.5, FAR_BELOW)
        e = jnp.exp(s - jnp.max(s, axis=-1, keepdims=True))
        p = e / jnp.sum(e, axis=-1, keepdims=True)
        p_o[j] = p
        outs.append(nn(p.astype(BF16), val[:, sl]).astype(BF16))
    o = jnp.concatenate(outs, 1)
    o_o[...] = o
    tick()
    bring(3)
    x1 = x + (nn(o, mat(2)) + e_gains[6:7])
    x1_o[...] = x1
    hat2, _ = norm_parts(x1)
    h2 = (hat2 * (1.0 + e_gains[2:3]) + e_gains[3:4]).astype(BF16)
    u, dg = gelu_parts(nn(h2, mat(3)) + e_bias[...])
    u = u.astype(BF16)
    u_o[...] = u
    dg_o[...] = dg
    masked_keys(groups - 1, lambda k: tick())
    bring(4)
    tick()
    bring(5)
    encoded = (x1 + (nn(u, mat(4)) + e_gains[7:8])).astype(BF16)
    enc_o[...] = encoded
    here_pos = nn(mat(6), pick_s[...]).T
    Xv = nn(encoded, mat(5)) + d_gains[8:9] + here_pos
    hat, _ = norm_parts(Xv)
    h = (hat * (1.0 + d_gains[0:1]) + d_gains[1:2]).astype(BF16)
    qv, kv, vv = three(nn(h, mat(7)))
    qkv_s[...] = jnp.concatenate([qv, kv, vv], 1)
    seen = jnp.sum(pick_s[...].astype(F32), axis=1, keepdims=True) > 0.5
    X_o[...] = jnp.where(seen, place_rows(pick_s[...], Xv), X_o[...])
    for i, ref in enumerate((q_o, k_o, v_o)):
        placed = nn(pick_s[...], qkv_s[:, dW * i : dW * (i + 1)]).astype(BF16)
        ref[...] = jnp.where(seen, placed, ref[...])
    tick()
    rest = list(steps)
    seen_row = nt(jnp.ones((8, ROWS_E), BF16), pick_s[...])[0:1] > 0.5
    slot = lax.broadcasted_iota(jnp.int32, (ROWS_E, 1), 0)
    slot_bias = jnp.where(slot < visible, 0.0, FAR_BELOW)
    bias = dead_bias(count, slots)

    @pl.loop(0, groups)
    def _(g):
        for at, t in enumerate(rest):

            @pl.when(g == at)
            def _():
                advance(t)

        cols = pl.ds(pl.multiple_of(g * GROUP, GROUP), GROUP)
        vcols = pl.ds(pl.multiple_of(g * GROUP + 2 * dW, GROUP), GROUP)
        kcols = pl.ds(pl.multiple_of(g * GROUP + dW, GROUP), GROUP)
        qT = q_o[:, cols].T
        kvg = qkv_s[:, kcols]
        vvT = qkv_s[:, vcols].T
        qvT = qkv_s[:, cols].T
        s = nn(k_o[:, cols], jnp.concatenate([head_rows(qvT, j) for j in range(4)], 1))
        s = jnp.concatenate([s[:SHORT], s[SHORT:] + bias], 0)
        high = jnp.max(s, axis=0, keepdims=True)
        p = jnp.exp2(s - high)
        total = jnp.sum(p, axis=0, keepdims=True)
        o = nn(v_o[:, cols].T, p.astype(BF16)) * (1.0 / total)
        L = high + jnp.log2(total)
        per_head = [slice(ROWS_E * j, ROWS_E * (j + 1)) for j in range(4)]
        ov = jnp.concatenate([o[HD * j : HD * (j + 1), per_head[j]] for j in range(4)], 0)
        oT_seen = nt(ov.astype(BF16), pick_s[...])
        terms, left = [], jnp.concatenate([L[:, sl] for sl in per_head], 0)
        for _ in range(3):
            terms.append(left.astype(BF16))
            left = left - terms[-1].astype(F32)
        L_seen = nt(jnp.concatenate(terms, 1), jnp.concatenate([pick_s[...]] * 3, 1))
        outs = []
        for j in range(4):
            rows = slice(HD * j, HD * (j + 1))
            s = nn(kvg, head_rows(qT, j)) + slot_bias
            before = high_s[g, j : j + 1, :]
            high = jnp.maximum(jnp.max(s, axis=0, keepdims=True), before)
            p = jnp.exp2(s - high)
            kept = jnp.exp2(before - high)
            total = jnp.sum(p, axis=0, keepdims=True) + sum_s[g, j : j + 1, :] * kept
            o = nn(vvT[rows], p.astype(BF16)) + oT_s[g, rows, :] * kept
            o = jnp.where(seen_row, oT_seen[rows], o * (1.0 / total))
            outs.append(o.astype(BF16))
            L = high + jnp.log2(total)
            L_o[g, j : j + 1, :] = jnp.where(seen_row, L_seen[j : j + 1], L)
        att_o[:, cols] = jnp.concatenate(outs, 0).T

    for i in range(8, n):
        bring(i)
    engine.finish()
    for i in range(1, n):
        keep(i).wait()


def front(lengths, orders, patches, small_shards, arrays, Z):
    shapes = [(SMALL_ROWS, 128)] + [a.shape for a in arrays]
    n, count = len(shapes), 8 * Z
    cuts = (1, 3, 1, 3, 3, 1, 1, 1, 1, 2, 2)
    chunks = []
    for i in (0, 6, 7, 1, 2, 3, 4, 5, 8, 9, 10):
        w = shapes[i][1] // cuts[i]
        chunks += [(i, w * t, w) for t in range(cuts[i])]
    slots, W = patches.shape
    Fw, dW, dF = shapes[3][1], shapes[5][1], shapes[9][1]
    sd = jax.ShapeDtypeStruct
    outs = [sd((2, Z, 2, 2) + s, BF16) for s in shapes[1:]]
    outs += [sd((1,), jnp.int32), sd((1, ROWS_E), jnp.int32)]
    outs += [sd((8, W), F32), sd((16, dW), F32), sd((1, Fw), F32), sd((1, dF), F32)]
    R = ROWS_E
    outs += [sd((R, W), BF16), sd((R, W), F32), sd((R, 3 * W), BF16), sd((R, W), BF16)]
    outs += [sd((R, W), F32), sd((R, Fw), BF16), sd((R, Fw), F32), sd((HEADS_E, R, R), F32)]
    outs += [sd((slots, dW), F32)] + [sd((slots, dW), BF16)] * 4
    outs += [sd((dW // GROUP, 4, slots), F32)]
    m = len(chunks)
    given = (*small_shards, *arrays)
    return pl.pallas_call(
        functools.partial(front_kernel, Z, chunks),
        out_shape=outs,
        in_specs=[S, V, A] + [A] * 14,
        out_specs=[A] * (n - 1) + [S] + [V] * 19,
        scratch_shapes=[pltpu.VMEM(a.shape, F32) for a in given]
        + [pltpu.VMEM(s, BF16) for s in shapes]
        + [pltpu.VMEM((2, Z, 2, 2) + s, BF16) for s in shapes]
        + [pltpu.VMEM((slots, W), BF16), D((15,)), D((n - 1,))]
        + [pltpu.VMEM((slots, R), BF16), pltpu.VMEM((slots, 1), F32)]
        + [pltpu.VMEM((dW // GROUP, 4, slots), F32)] * 2
        + [pltpu.VMEM((dW // GROUP, GROUP, slots), F32), pltpu.VMEM((R, 3 * dW), BF16)]
        + [D((m,)), D((m, Z - 1)), D((m, Z - 1))]
        + [D((m, 4)), D((m, 4)), D((m, 5)), D((m, 5))],
        compiler_params=pltpu.CompilerParams(
            collective_id=0, has_side_effects=True, vmem_limit_bytes=62 * 2**20
        ),
    )(lengths, orders, patches, *given)


def dec_mid_kernel(steps, FC, info, x_r, o_r, cot_r, gains, bias, proj, fc1, fc2,
                   dec_o, gx1_o, go_o, gfc2_o, gfc1_o, gproj_o, gvec_o, gbias_o, *acc):
    i = pl.program_id(0)
    n, W = x_r.shape
    Fw = fc1.shape[1]
    if steps > 1:
        afc2, afc1, aproj = acc
        @pl.when(i == 0)
        def _():
            for ref in (afc2, afc1, aproj): ref[...] = jnp.zeros_like(ref)
    @pl.when(i == 0)
    def _():
        for ref in (gvec_o, gbias_o): ref[...] = jnp.zeros_like(ref)
    live = lax.broadcasted_iota(jnp.int32, (n, 1), 0) + i * n < info[0]
    o = o_r[...]
    x1 = x_r[...] + (nn(o, proj[...]) + gains[6:7])
    hat, r = norm_parts(x1)
    h2 = (hat * (1.0 + gains[2:3]) + gains[3:4]).astype(BF16)
    G = jnp.where(live, cot_r[...].astype(F32), 0.0)
    gy = G.astype(BF16)
    def first(c):
        sl = slice(c*FC, (c+1)*FC)
        return nn(h2, fc1[:, sl]), nt(gy, fc2[sl, :])
    nc = Fw//FC
    y = None; gh2 = None
    nxt = first(0)
    for c in range(nc):
        sl = slice(c*FC, (c+1)*FC)
        z, gu = nxt
        if c+1 < nc: nxt = first(c+1)
        u, dg = gelu_parts(z + bias[:, sl])
        u = u.astype(BF16)
        gz32 = gu * dg
        gz = gz32.astype(BF16)
        yc = nn(u, fc2[sl, :])
        y = yc if y is None else y + yc
        gc = nt(gz, fc1[:, sl])
        gh2 = gc if gh2 is None else gh2 + gc
        gbias_o[:, sl] += col_sum(gz.astype(F32))
        if steps > 1:
            afc2[sl, :] += tn(u, gy)
            afc1[:, sl] += tn(h2, gz)
        else:
            gfc2_o[sl, :] = tn(u, gy).astype(BF16)
            gfc1_o[:, sl] = tn(h2, gz).astype(BF16)
    y = x1 + (y + gains[7:8])
    dec_o[...] = jnp.where(live, y, 0.0).astype(BF16)
    gvec_o[0:1, :] += col_sum(gh2 * hat)
    gvec_o[1:2, :] += col_sum(gh2)
    gx1 = G + norm_back(gh2, hat, r, gains[2:3])
    gx1_o[...] = gx1
    ga = gx1.astype(BF16)
    gvec_o[2:3, :] += col_sum(ga.astype(F32))
    gvec_o[3:4, :] += col_sum(G)
    go_o[...] = nt(ga, proj[...]).astype(BF16)
    if steps > 1:
        aproj[...] += tn(o, ga)
        @pl.when(i == steps - 1)
        def _():
            gfc2_o[...] = afc2[...].astype(BF16)
            gfc1_o[...] = afc1[...].astype(BF16)
            gproj_o[...] = aproj[...].astype(BF16)
    else:
        gproj_o[...] = tn(o, ga).astype(BF16)

def dec_mid(info, x, o, cot, gains, bias, proj, fc1, fc2, tile=1024, FC=1024):
    n, W = x.shape
    sd = jax.ShapeDtypeStruct
    full = lambda a: pl.BlockSpec(a.shape, lambda i: (0,)*a.ndim)
    row = pl.BlockSpec((tile, W), lambda i: (i, 0))
    Fw = fc1.shape[1]
    outs = (sd((n, W), BF16), sd((n, W), F32), sd((n, W), BF16), sd(fc2.shape, BF16), sd(fc1.shape, BF16), sd(proj.shape, BF16), sd((8, W), F32), sd((1, Fw), F32))
    return pl.pallas_call(functools.partial(dec_mid_kernel, n//tile, FC), grid=(n//tile,), out_shape=outs,
        in_specs=[S, row, row, row, full(gains), full(bias), full(proj), full(fc1), full(fc2)],
        out_specs=(row, row, row) + tuple(full(a) for a in outs[3:]),
        scratch_shapes=[pltpu.VMEM(w.shape, F32) for w in (fc2, fc1, proj)] if n > tile else [],
        compiler_params=params(60))(info, x, o, cot, gains, bias, proj, fc1, fc2)

def dec_post_kernel(steps, info, places, x_r, gx1_r, gq_r, gk_r, gv_r, gains, qkv, gqkv_o, gposT_o, gemb_o, gvec_o, aqkv, aemb):
    i = pl.program_id(0)
    @pl.when(i == 0)
    def _():
        for ref in (aqkv, aemb, gvec_o): ref[...] = jnp.zeros_like(ref)
    n = x_r.shape[0]
    x = x_r[...]
    hat, r = norm_parts(x)
    h = (hat * (1.0 + gains[0:1]) + gains[1:2]).astype(BF16)
    gm = jnp.concatenate([gq_r[...], gk_r[...], gv_r[...]], 1)
    W = x.shape[1]
    aqkv[...] += tn(h, gm)
    gh = nt(gm, qkv[...])
    gvec_o[0:1, :] += col_sum(gh * hat)
    gvec_o[1:2, :] += col_sum(gh)
    gvec_o[4:5, :] += col_sum(gq_r[...].astype(F32))
    gvec_o[5:6, :] += col_sum(gv_r[...].astype(F32))
    gx = gx1_r[...] + norm_back(gh, hat, r, gains[0:1])
    gxb = gx.astype(BF16)
    gposT_o[...] = gxb.T
    pos_i = lax.broadcasted_iota(jnp.int32, (n, ROWS_E), 0) + i * n
    rr = lax.broadcasted_iota(jnp.int32, (n, ROWS_E), 1)
    pick = ((pos_i == places[...]) & (rr < info[0] // 10)).astype(BF16)
    seen = jnp.sum(pick.astype(F32), axis=1, keepdims=True)
    aemb[...] += tn(pick, gxb)
    gvec_o[9:10, :] += col_sum(gx * (1.0 - seen))
    @pl.when(i == steps - 1)
    def _():
        gqkv_o[...] = aqkv[...].astype(BF16)
        gemb_o[...] = aemb[...].astype(BF16)
        gvec_o[8:9, :] = col_sum(aemb[...])

def dec_post(info, places, x, gx1, gq, gk, gv, gains, qkv, tile=1024):
    n, W = x.shape
    sd = jax.ShapeDtypeStruct
    full = lambda a: pl.BlockSpec(a.shape, lambda i: (0,)*a.ndim)
    row = pl.BlockSpec((tile, W), lambda i: (i, 0))
    outs = (sd(qkv.shape, BF16), sd((W, n), BF16), sd((ROWS_E, W), BF16), sd((16, W), F32))
    return pl.pallas_call(functools.partial(dec_post_kernel, n//tile), grid=(n//tile,), out_shape=outs,
        in_specs=[S, full(places), row, row, row, row, row, full(gains), full(qkv)],
        out_specs=(full(outs[0]), pl.BlockSpec((W, tile), lambda i: (0, i)), full(outs[2]), full(outs[3])),
        scratch_shapes=[pltpu.VMEM(qkv.shape, F32), pltpu.VMEM((ROWS_E, W), F32)],
        compiler_params=params())(info, places, x, gx1, gq, gk, gv, gains, qkv)

SPOTS = (0, 2, 4, 6, 8, 10, 12, 14, 16)


def attend_back_kernel(Z, chunks, info, q_ref, k_ref, v_ref, go_ref, o_ref, L_ref, *refs):
    blocks, (gq_ref, gk_ref, gv_ref), outs, rest = refs[:3], refs[3:6], refs[6:9], refs[9:]
    lands, rest = rest[:3], rest[3:]
    engine = Scatter(Z, take_buffers(rest[:-7], blocks, (True,) * 3, lands), chunks, rest[-7:])
    g = pl.program_id(0)

    @pl.when(g == 0)
    def _():
        engine.greet()

    q = q_ref[...]
    k = k_ref[...]
    v = v_ref[...]
    go = go_ref[...]
    bias = dead_bias(info[0], k.shape[0])
    qT, kT, goT, oT = q.T, k.T, go.T, o_ref[...].T
    inner_all = goT.astype(F32) * oT.astype(F32)
    ak = av = None
    gqs = []
    for j in range(4):
        for step in range(4):
            if 4 * step + j in SPOTS:

                @pl.when(g == step)
                def _():
                    engine.tick(SPOTS.index(4 * step + j))

        rows = slice(HD * j, HD * (j + 1))
        s = nn(k, head_rows(qT, j))
        s = jnp.concatenate([s[:SHORT], s[SHORT:] + bias], 0)
        p = jnp.exp2(s - L_ref[0, j : j + 1, :])
        gp = nn(v, head_rows(goT, j))
        inner = jnp.sum(inner_all[rows], axis=0, keepdims=True)
        gs = (p * (gp - inner)).astype(BF16)
        a = nn(p.astype(BF16), head_lanes(go, j))
        b = nn(gs, head_lanes(q, j))
        av = a if av is None else av + a
        ak = b if ak is None else ak + b
        gqs.append((nn(kT[rows], gs) * math.log(2.0)).astype(BF16))
    gq_ref[...] = jnp.concatenate(gqs, 0).T
    gk_ref[...] = (ak * HD**-0.5).astype(BF16)
    gv_ref[...] = av.astype(BF16)

    @pl.when(g == 3)
    def _():
        engine.tick(SPOTS.index(16))
        engine.finish()
        for out, land in zip(outs, lands):
            out[...] = land[...]


def attend_back(info, q, k, v, go, o, L, grads, Z):
    n, W = k.shape
    blk = pl.BlockSpec((n, GROUP), lambda g: (0, g))
    shapes = [a.shape[4:] for a in grads]
    chunks = []
    for i, (r, c) in enumerate(shapes[:2]):
        chunks += [(i, 0, c // 2), (i, c // 2, c // 2)]
    chunks.append((2, 0, shapes[2][1]))
    buffers, sems = scatter_buffers(shapes, (True,) * 3, Z, chunks)
    outs = [jax.ShapeDtypeStruct((Z, *s), BF16) for s in shapes]
    return pl.pallas_call(
        functools.partial(attend_back_kernel, Z, chunks),
        grid=(W // GROUP,),
        out_shape=[jax.ShapeDtypeStruct((n, W), BF16)] * 3 + outs,
        in_specs=[S, blk, blk, blk, blk, blk, pl.BlockSpec((1, 4, n), lambda g: (g, 0, 0))]
        + [A] * 3,
        out_specs=[blk] * 3 + [V] * 3,
        scratch_shapes=[pltpu.VMEM(a.shape, BF16) for a in outs] + buffers + sems,
        compiler_params=pltpu.CompilerParams(
            collective_id=1, has_side_effects=True, vmem_limit_bytes=60 * 2**20
        ),
    )(info, q, k, v, go, o, L, *grads)


def enc_bwd_kernel(Z, chunks, *refs):
    given, small_in, blocks_in = refs[:14], refs[14:18], refs[18:20]
    gx_o, outs, rest = refs[20], refs[21:29], refs[29:]
    local, made, rest = rest[:13], rest[13:19], rest[19:]
    e_vec, e_bias, whole, sem = rest[-11:-7]
    loaded = (True, True) + (False,) * 6
    engine = Scatter(
        Z, take_buffers(rest[:-11], (*blocks_in, *made), loaded, outs), chunks, rest[-7:]
    )
    g_embed, g_fc2, g_fc1, g_proj, g_qkv, g_small = made
    gains, mid_vec, post_vec, d_bias = small_in
    places = (*local, local[8].at[:, pl.ds(0, given[13].shape[1])])
    loads = [pltpu.make_async_copy(given[i], places[i], sem.at[i]) for i in range(14)]
    for load in loads[:13]:
        load.start()

    def got(i):
        loads[i].wait()
        return places[i][...]

    engine.greet()
    steps = iter(range(engine.ticks))

    def tick():
        engine.tick(next(steps))

    def store(ref, value):
        ref[...] = value.astype(BF16).reshape(ref.shape)

    tick()
    ge = got(0)
    store(g_embed, tn(got(1), ge))
    gy = nt(ge, got(2)).astype(BF16)
    G = gy.astype(F32)
    tick()
    u = got(3)
    store(g_fc2, tn(u, gy))
    tick()
    gz = (nt(gy, got(4)) * got(5)).astype(BF16)
    e_bias[...] = col_sum(gz.astype(F32))
    tick()
    hat2, r2 = norm_parts(got(6))
    h2 = (hat2 * (1.0 + gains[2:3]) + gains[3:4]).astype(BF16)
    store(g_fc1, tn(h2, gz))
    tick()
    gh2 = nt(gz, got(8))
    loads[13].start()
    e_vec[2:3, :] = col_sum(gh2 * hat2)
    e_vec[3:4, :] = col_sum(gh2)
    gx1 = G + norm_back(gh2, hat2, r2, gains[2:3])
    ga = gx1.astype(BF16)
    e_vec[6:7, :] = col_sum(ga.astype(F32))
    e_vec[7:8, :] = col_sum(G)
    store(g_proj, tn(got(7), ga))
    tick()
    go = nt(ga, got(9)).astype(BF16)
    for i in (10, 11, 12):
        loads[i].wait()
    m_r, p_r, x_r = places[10:13]
    W = gx1.shape[1]
    hs = W // HEADS_E
    gq, gk, gv = [], [], []
    for j in range(HEADS_E):
        q = m_r[:, hs * j : hs * (j + 1)]
        k = m_r[:, W + hs * j : W + hs * (j + 1)]
        val = m_r[:, 2 * W + hs * j : 2 * W + hs * (j + 1)]
        g = go[:, hs * j : hs * (j + 1)]
        p = p_r[j]
        gv.append(tn(p.astype(BF16), g).astype(BF16))
        gp = nt(g, val)
        gs = (p * (gp - jnp.sum(gp * p, axis=-1, keepdims=True))).astype(BF16)
        gq.append((nn(gs, k) * hs**-0.5).astype(BF16))
        gk.append((tn(gs, q) * hs**-0.5).astype(BF16))
        if j == HEADS_E // 2:
            tick()
    gm = jnp.concatenate(gq + gk + gv, 1)
    tick()
    e_vec[4:5, :] = col_sum(gm[:, :W].astype(F32))
    e_vec[5:6, :] = col_sum(gm[:, 2 * W :].astype(F32))
    hat, r = norm_parts(x_r[...])
    h = (hat * (1.0 + gains[0:1]) + gains[1:2]).astype(BF16)
    store(g_qkv, tn(h, gm))
    tick()
    gh = nt(gm, got(13))
    e_vec[0:1, :] = col_sum(gh * hat)
    e_vec[1:2, :] = col_sum(gh)
    gx_o[...] = gx1 + norm_back(gh, hat, r, gains[0:1])
    pack(g_small, e_vec, e_bias, mid_vec, post_vec, d_bias, whole)
    for t in steps:
        engine.tick(t)
    engine.finish()


def pack(out, e_vec, e_bias, mid_vec, post_vec, d_bias, whole):
    Z = out.shape[1]
    count = 8 * Z
    whole[...] = jnp.zeros_like(whole)
    whole[0:2] = post_vec[0:2]
    whole[2:4] = mid_vec[0:2]
    whole[4:6] = post_vec[4:6]
    whole[6:8] = mid_vec[2:4]
    whole[8:10] = post_vec[8:10]
    out[...] = jnp.zeros_like(out)
    for ref, row, rows in ((e_vec, 0, 8), (whole, 8, 16), (e_bias, 24, 1), (d_bias, 25, 1)):
        w = ref.shape[1] // count
        values = ref[...].astype(BF16)
        for i in range(count):
            at = (i // (4 * Z), i // 4 % Z, i // 2 % 2, i % 2)
            out[(*at, slice(row, row + rows), slice(0, w))] = values[:, w * i : w * i + w]


def enc_bwd(encoded, gemb, embed, kept, mats, small_in, blocks_in, Z):
    x, m, o, x1, u, dg, p = kept
    qkv, proj, fc1, fc2 = mats
    given = (gemb, encoded, embed, u, fc2, dg, x1, o, fc1, proj, m, p, x, qkv)
    count = 8 * Z

    def block_shape(a):
        return (a.shape[0] // count, a.shape[1])

    shapes = [a.shape[4:] for a in blocks_in]
    shapes += [block_shape(a) for a in (embed, fc2, fc1, proj, qkv)] + [(SMALL_ROWS, 128)]
    W, Fw = fc1.shape
    chunks = [(0, 0, shapes[0][1]), (1, 0, shapes[1][1]), (2, 0, shapes[2][1])]
    chunks += [(3, t * W // 3, W // 3) for t in range(3)]
    chunks += [(4, t * Fw // 3, Fw // 3) for t in range(3)]
    chunks += [(5, 0, W)] + [(6, t * W, W) for t in range(3)] + [(7, 0, 128)]
    loaded = (True, True) + (False,) * 6
    buffers, sems = scatter_buffers(shapes, loaded, Z, chunks)
    sd = jax.ShapeDtypeStruct
    return pl.pallas_call(
        functools.partial(enc_bwd_kernel, Z, chunks),
        out_shape=[sd(x.shape, F32)] + [sd((Z, *s), BF16) for s in shapes],
        in_specs=[A] * 14 + [V] * 4 + [A] * 2,
        out_specs=[V] * 9,
        scratch_shapes=[pltpu.VMEM(a.shape, a.dtype) for a in given[:13]]
        + [pltpu.VMEM((2, Z, 2, 2, *s), BF16) for s in shapes[2:]]
        + buffers
        + [pltpu.VMEM((8, W), F32), pltpu.VMEM((1, Fw), F32), pltpu.VMEM((16, embed.shape[1]), F32)]
        + [D((14,))]
        + sems,
        compiler_params=pltpu.CompilerParams(
            collective_id=2, has_side_effects=True, vmem_limit_bytes=62 * 2**20
        ),
    )(*given, *small_in, *blocks_in)


def last_kernel(n, info, places, gx, *refs):
    ins, g_patch, outs = refs[:n], refs[n], refs[n + 1 :]
    pick = pick_matrix(places[...], info[0] // 10, g_patch.shape[0])
    g_patch[...] = place_rows(pick, gx[...])

    def total(ref):
        acc = ref[0].astype(F32)
        for d in range(1, ref.shape[0]):
            acc = acc + ref[d].astype(F32)
        return acc

    small = total(ins[0])
    for out, row in zip(outs[:4], (0, 8, 24, 25)):
        out[...] = small[row : row + out.shape[0], : out.shape[1]]
    for i, ref in enumerate(ins[1:]):
        outs[4 + i][...] = total(ref)


def last_sums(info, places, gx, arrays, shapes):
    return pl.pallas_call(
        functools.partial(last_kernel, len(arrays)),
        out_shape=[jax.ShapeDtypeStruct(s, F32) for s in shapes],
        in_specs=[S] + [V] * (2 + len(arrays)),
        compiler_params=params(),
    )(info, places, gx, *arrays)


def body(
    patches,
    lengths,
    keep_order,
    e_vectors,
    e_qkv,
    e_proj,
    e_fc1,
    e_fc1_bias,
    e_fc2,
    embed,
    d_vectors,
    dec_pos,
    d_qkv,
    d_proj,
    d_fc1,
    d_fc1_bias,
    d_fc2,
    cotangent,
):
    Z = lax.axis_size("dp") // 4
    slots = patches.shape[1]
    smalls = (e_vectors, d_vectors, e_fc1_bias.reshape(1, -1), d_fc1_bias.reshape(1, -1))
    shards = (e_qkv, e_proj, e_fc1, e_fc2, embed, dec_pos.T, d_qkv, d_proj, d_fc1, d_fc2)
    made = front(lengths, keep_order, patches[0], smalls, shards, Z)
    mats = [m.reshape(-1, m.shape[-1]) for m in made[:10]]
    w_qkv, w_proj, w_fc1, w_fc2, w_embed, posT, dw_qkv, dw_proj, dw_fc1, dw_fc2 = mats
    info, places, e_gains, d_gains, e_bias, d_bias, encoded, *kept = made[10:24]
    x, q, k, v, o, L = made[24:]
    decoded, gx1, go, gd_fc2, gd_fc1, gd_proj, mid_vec, gd_bias = dec_mid(
        info, x, o, cotangent[0], d_gains, d_bias, dw_proj, dw_fc1, dw_fc2
    )

    def blocks(m):
        return m.reshape((2, Z, 2, 2, -1, m.shape[-1]))

    gq, gk, gv, *early = attend_back(
        info, q, k, v, go, o, L, [blocks(m) for m in (gd_fc2, gd_fc1, gd_proj)], Z
    )
    gd_qkv, g_posT, gemb, post_vec = dec_post(
        info, places, x, gx1, gq, gk, gv, d_gains, dw_qkv
    )
    gx, *late = enc_bwd(
        encoded,
        gemb,
        w_embed,
        kept,
        (w_qkv, w_proj, w_fc1, w_fc2),
        (e_gains, mid_vec, post_vec, gd_bias),
        (blocks(gd_qkv), blocks(g_posT)),
        Z,
    )
    pd_qkv, p_pos, p_embed, p_fc2, p_fc1, p_proj, p_qkv, p_small = late
    parts = (p_small, p_qkv, p_proj, p_fc1, p_fc2, p_embed, p_pos, pd_qkv, *early[::-1])
    shapes = [(slots, patches.shape[2])] + [m.shape for m in smalls + shards]
    g_patch, *out = last_sums(info, places, gx, parts, shapes)
    re_vec, rd_vec, re_bias, rd_bias = out[:4]
    re_qkv, re_proj, re_fc1, re_fc2, r_embed, r_pos, rd_qkv, rd_proj, rd_fc1, rd_fc2 = out[4:]
    return (
        decoded[None],
        g_patch[None],
        re_vec,
        re_qkv,
        re_proj,
        re_fc1,
        re_bias.reshape(-1),
        re_fc2,
        r_embed,
        rd_vec,
        r_pos.T,
        rd_qkv,
        rd_proj,
        rd_fc1,
        rd_bias.reshape(-1),
        rd_fc2,
    )


def solution(mesh):
    rows, columns, cubes = P(AXES, None), P(None, AXES), P(AXES, None, None)
    weights = (columns, rows, rows, rows, P(AXES), rows, rows, columns, columns)
    weights = weights + (rows, rows, rows, P(AXES), rows)
    return jax.shard_map(
        body,
        mesh=mesh,
        in_specs=(cubes, P(), P()) + weights + (cubes,),
        out_specs=(cubes, cubes) + weights,
        check_vma=False,
    )
```

```python
import functools
import math

import jax
import jax.numpy as jnp
from jax import lax
from jax.experimental import pallas as pl
from jax.experimental.pallas import tpu as pltpu
from jax.sharding import PartitionSpec as P

HEADS_E = 12
HEADS_D = 16
VIS = 104
SHORT = 576
HD = 32
GROUP = 128
F32 = jnp.float32
BF16 = jnp.bfloat16
AXES = ("segment", "dp")
MESH = pl.DeviceIdType.MESH
ROWS_E = 128
NORM_EPS = 1e-06
FAR_BELOW = -1e30


SMALL_ROWS = 32


def place():
    s = lax.axis_index("segment")
    dp = lax.axis_index("dp")
    return s, dp // 4, (dp // 2) % 2, dp % 2


def device(s, z, y, c):
    return (s, (z * 2 + y) * 2 + c)


def halves(columns):
    return (columns // 2, columns // 2) if columns % 256 == 0 else (columns, 0)


def greet(peers):
    barrier = pltpu.get_barrier_semaphore()
    for peer in peers:
        pl.semaphore_signal(barrier, inc=1, device_id=peer, device_id_type=MESH)
    pl.semaphore_wait(barrier, len(peers))


class Gather:
    def __init__(self, Z, shards, outs, chunks, sems):
        self.Z, self.shards, self.outs, self.chunks = Z, shards, outs, chunks
        self.loc, self.zs, self.zr, self.ms, self.mr, self.cs, self.cr = sems
        self.s, self.z, self.y, self.c = s, z, y, c = place()
        self.X, self.Y = device(1 - s, z, y, c), device(s, z, 1 - y, c)
        self.C = device(s, z, y, 1 - c)
        self.z_peers = [device(s, lax.rem(z + d, Z), y, c) for d in range(1, Z)]

    def greet(self):
        greet(self.z_peers + [self.X, self.Y, self.C])

    def copy(self, src, dst, ss, rs, target):
        return pltpu.make_async_remote_copy(
            src_ref=src,
            dst_ref=dst,
            send_sem=ss,
            recv_sem=rs,
            device_id=target,
            device_id_type=MESH,
        )

    def own(self, m):
        i, start, width = self.chunks[m]
        cols = pl.ds(start, width)
        return pltpu.make_async_copy(
            self.shards[i].at[:, cols],
            self.outs[i].at[self.s, self.z, self.y, self.c, :, cols],
            self.loc.at[m],
        )

    def copies(self, m, stage):
        i, start, width = self.chunks[m]
        ka, kb = halves(width)
        s, z, y, c = self.s, self.z, self.y, self.c
        o = self.outs[i]
        cols, A = pl.ds(start, width), pl.ds(start, ka)
        B = pl.ds(start + ka, kb) if kb else None
        if stage == 0:
            return [
                self.copy(
                    self.shards[i].at[:, cols],
                    o.at[s, z, y, c, :, cols],
                    self.zs.at[m, d],
                    self.zr.at[m, d],
                    self.z_peers[d],
                )
                for d in range(self.Z - 1)
            ]
        if stage == 1:
            made = [(o.at[s, :, y, c, :, A], 0, self.X)]
            if kb:
                made.append((o.at[s, :, y, c, :, B], 1, self.Y))
        elif stage == 2:
            made = [(o.at[:, :, y, c, :, A], 2, self.Y)]
            if kb:
                made.append((o.at[s, :, :, c, :, B], 3, self.X))
        elif stage == 11:
            made = [(o.at[s, :, y, c, :, cols], 0, self.C)]
        elif stage == 12:
            made = [(o.at[1 - s, :, y, c, :, A], 1, self.C)]
            if kb:
                made.append((o.at[s, :, 1 - y, c, :, B], 2, self.C))
        else:
            made = [(o.at[:, :, 1 - y, c, :, A], 3, self.C)]
            if kb:
                made.append((o.at[1 - s, :, :, c, :, B], 4, self.C))
        ss, rs = (self.cs, self.cr) if stage > 10 else (self.ms, self.mr)
        return [self.copy(ref, ref, ss.at[m, k], rs.at[m, k], target) for ref, k, target in made]

    def stage(self, m, stage):
        if stage == 0:
            self.own(m).start()
        else:
            if stage == 1:
                self.own(m).wait()
            for copy in self.copies(m, stage - 1):
                copy.wait_recv()
        if stage < 3:
            for copy in self.copies(m, stage):
                copy.start()
        if stage > 0:
            for copy in self.copies(m, stage + 10):
                copy.start()

    @property
    def ticks(self):
        return len(self.chunks) + 6

    def tick(self, t):
        for k in range(4):
            if 0 <= t - 2 * k < len(self.chunks):
                self.stage(t - 2 * k, k)

    def arrived(self, i):
        for m, chunk in enumerate(self.chunks):
            if chunk[0] == i:
                for stage in (11, 12, 13):
                    for copy in self.copies(m, stage):
                        copy.wait_recv()

    def finish(self):
        for m in range(len(self.chunks)):
            for stage in (0, 1, 2, 11, 12, 13):
                for copy in self.copies(m, stage):
                    copy.wait_send()


class Scatter:
    def __init__(self, Z, arrays, chunks, sems):
        self.Z, self.arrays, self.chunks = Z, arrays, chunks
        self.loc, self.cs, self.cr, self.ms, self.mr, self.zs, self.zr = sems
        self.s, self.z, self.y, self.c = s, z, y, c = place()
        self.X, self.Y = device(1 - s, z, y, c), device(s, z, 1 - y, c)
        self.C = device(s, z, y, 1 - c)
        self.z_peers = [device(s, lax.rem(z + d, Z), y, c) for d in range(1, Z)]

    def greet(self):
        greet(self.z_peers + [self.X, self.Y, self.C])

    def parts(self, m):
        i, start, width = self.chunks[m]
        ka, kb = halves(width)
        return i, start, width, ka, kb, (start // 2 if kb else start)

    def held(self, i, index, columns):
        blocks, held = self.arrays[i][:2]
        if held is None:
            ss, zz, yy = index
            return blocks.at[ss, zz, yy, self.c, :, columns]
        return held.at[(*index, slice(None), columns)]

    def copy(self, src, dst, ss, rs, target):
        return pltpu.make_async_remote_copy(
            src_ref=src,
            dst_ref=dst,
            send_sem=ss,
            recv_sem=rs,
            device_id=target,
            device_id_type=MESH,
        )

    def own(self, m):
        i, start, width, *_ = self.parts(m)
        blocks, held = self.arrays[i][:2]
        if held is None:
            return None
        cols = pl.ds(start, width)
        return pltpu.make_async_copy(
            blocks.at[:, :, :, self.c, :, cols], held.at[:, :, :, :, cols], self.loc.at[m]
        )

    def copies(self, m, stage):
        i, start, width, ka, kb, at = self.parts(m)
        s, z, y, c, Z = self.s, self.z, self.y, self.c, self.Z
        blocks, held, R0, R1A, R1B, R2A, R2B, out = self.arrays[i]
        cols, A, B = pl.ds(start, width), pl.ds(start, ka), pl.ds(start + ka, kb)
        half = pl.ds(at, ka)
        full = slice(None)
        if stage == 0:
            return [
                self.copy(
                    blocks.at[:, :, :, 1 - c, :, cols],
                    R0.at[:, :, :, :, cols],
                    self.cs.at[m],
                    self.cr.at[m],
                    self.C,
                )
            ]
        if stage == 1:
            made = [(self.held(i, (full, full, 1 - y), A), R1A.at[:, :, :, half], self.Y)]
            if kb:
                made.append((self.held(i, (1 - s, full, full), B), R1B.at[:, :, :, half], self.X))
        elif stage == 2:
            made = [(self.held(i, (1 - s, full, y), A), R2A.at[:, :, half], self.X)]
            if kb:
                made.append((self.held(i, (s, full, 1 - y), B), R2B.at[:, :, half], self.Y))
        else:
            return [
                self.copy(
                    self.held(i, (s, lax.rem(z + d, Z), y), cols),
                    out.at[d, :, cols],
                    self.zs.at[m, d - 1],
                    self.zr.at[m, d - 1],
                    self.z_peers[d - 1],
                )
                for d in range(1, Z)
            ]
        k = 2 * (stage - 1)
        return [
            self.copy(src, dst, self.ms.at[m, k + j], self.mr.at[m, k + j], target)
            for j, (src, dst, target) in enumerate(made)
        ]

    def add(self, i, index, columns, other):
        ref = self.held(i, index, columns)
        ref[...] = ref[...] + other[...]

    def stage(self, m, stage):
        i, start, width, ka, kb, at = self.parts(m)
        s, z, y, Z = self.s, self.z, self.y, self.Z
        blocks, held, R0, R1A, R1B, R2A, R2B, out = self.arrays[i]
        cols, A, B = pl.ds(start, width), pl.ds(start, ka), pl.ds(start + ka, kb)
        half = pl.ds(at, ka)
        if stage == 0:
            own = self.own(m)
            if own is not None:
                own.start()
        else:
            if stage == 1 and held is not None:
                self.own(m).wait()
            for copy in self.copies(m, stage - 1):
                copy.wait_recv()
        if stage == 1:

            @pl.loop(0, 4 * Z)
            def _(t):
                index = (t // (Z * 2), (t // 2) % Z, t % 2)
                self.add(i, index, cols, R0.at[(*index, slice(None), cols)])

        elif stage == 2:

            @pl.loop(0, 2 * Z)
            def _(t):
                u, zz = t // Z, t % Z
                self.add(i, (u, zz, y), A, R1A.at[u, zz, :, half])
                if kb:
                    self.add(i, (s, zz, u), B, R1B.at[zz, u, :, half])

        elif stage == 3:

            @pl.loop(0, Z)
            def _(zz):
                self.add(i, (s, zz, y), A, R2A.at[zz, :, half])
                if kb:
                    self.add(i, (s, zz, y), B, R2B.at[zz, :, half])

        elif stage == 4:
            out[0, :, cols] = self.held(i, (s, z, y), cols)[...]
            return
        for copy in self.copies(m, stage):
            copy.start()

    @property
    def ticks(self):
        return len(self.chunks) + 4

    def tick(self, t):
        for k in range(5):
            if 0 <= t - k < len(self.chunks):
                self.stage(t - k, k)

    def finish(self):
        for m in range(len(self.chunks)):
            for stage in range(4):
                for copy in self.copies(m, stage):
                    copy.wait_send()


def scatter_buffers(shapes, loaded, Z, chunks):
    refs = []
    for (r, k), load in zip(shapes, loaded):
        ka, kb = halves(k)
        kb = max(kb, 128)
        if load:
            refs.append((2, Z, 2, r, k))
        refs += [(2, Z, 2, r, k), (2, Z, r, ka), (Z, 2, r, kb), (Z, r, ka), (Z, r, kb)]
    n = len(chunks)
    D = pltpu.SemaphoreType.DMA
    return [pltpu.VMEM(s, BF16) for s in refs], [
        D((n,)),
        D((n,)),
        D((n,)),
        D((n, 4)),
        D((n, 4)),
        D((n, Z - 1)),
        D((n, Z - 1)),
    ]


def take_buffers(refs, blocks, loaded, outs):
    refs = list(refs)
    arrays = []
    for block, load, out in zip(blocks, loaded, outs):
        held = refs.pop(0) if load else None
        arrays.append((block, held, *(refs.pop(0) for _ in range(5)), out))
    return arrays


def nn(a, b): return jnp.dot(a, b, preferred_element_type=F32)
def nt(a, b): return lax.dot_general(a, b, (((1,), (1,)), ((), ())), preferred_element_type=F32)
def tn(a, b): return lax.dot_general(a, b, (((0,), (0,)), ((), ())), preferred_element_type=F32)

def norm_parts(x):
    center = x - jnp.mean(x, axis=-1, keepdims=True)
    r = lax.rsqrt(jnp.mean(center * center, axis=-1, keepdims=True) + NORM_EPS)
    return center * r, r

def norm_back(g, hat, r, gain):
    w = g * (1.0 + gain)
    return r * (w - jnp.mean(w, axis=-1, keepdims=True) - hat * jnp.mean(w * hat, axis=-1, keepdims=True))

def gelu_parts(z):
    x = jnp.abs(z) * math.sqrt(0.5)
    t = 1.0 / (1.0 + 0.3275911 * x)
    e = jnp.exp(-(x * x))
    poly = t * (0.254829592 + t * (-0.284496736 + t * (1.421413741 + t * (-1.453152027 + t * 1.061405429))))
    half = 0.5 * poly * e
    cdf = jnp.where(z > 0, 1.0 - half, half)
    return z * cdf, cdf + z * e * (1.0 / math.sqrt(2.0 * math.pi))

def col_sum(m): return jnp.sum(m, axis=0, keepdims=True)

def pick_matrix(places_row, keep_count, slots):
    pos = lax.broadcasted_iota(jnp.int32, (slots, ROWS_E), 0)
    r = lax.broadcasted_iota(jnp.int32, (slots, ROWS_E), 1)
    return ((pos == places_row) & (r < keep_count)).astype(BF16)

V = pl.BlockSpec(memory_space=pltpu.VMEM); A = pl.BlockSpec(memory_space=pl.ANY); S = pl.BlockSpec(memory_space=pltpu.SMEM)
D = pltpu.SemaphoreType.DMA
def params(mb=56): return pltpu.CompilerParams(vmem_limit_bytes=mb*2**20)

def head_rows(block, j):
    parts = []
    if j > 0: parts.append(jnp.zeros((HD*j, block.shape[1]), block.dtype))
    parts.append(block[HD*j:HD*(j+1)])
    if j < 3: parts.append(jnp.zeros((HD*(3-j), block.shape[1]), block.dtype))
    return jnp.concatenate(parts, 0)

def head_lanes(block, j):
    lane = lax.broadcasted_iota(jnp.int32, block.shape, 1)
    return jnp.where((lane >= HD*j) & (lane < HD*(j+1)), block, jnp.zeros_like(block))

def dead_bias(count, n):
    return jnp.where(lax.broadcasted_iota(jnp.int32, (n - SHORT, 1), 0) + SHORT < count, 0.0, FAR_BELOW)

SMALL_AT = ((0, 8), (8, 16), (24, 1), (25, 1))


def place_rows(pick, rows):
    terms, left = [], rows
    for _ in range(3):
        terms.append(left.astype(BF16))
        left = left - terms[-1].astype(F32)
    return nn(jnp.concatenate([pick] * 3, 1), jnp.concatenate(terms, 0))


def front_kernel(Z, chunks, *refs):
    n = 11
    lengths, orders, patches_h, given, refs = refs[0], refs[1], refs[2], refs[3:17], refs[17:]
    fulls, refs = refs[: n - 1], refs[n - 1 :]
    info, places, e_gains, d_gains, e_bias, d_bias = refs[:6]
    enc_o, x_o, m_o, o_o, x1_o, u_o, dg_o, p_o, X_o, q_o, k_o, v_o, att_o, L_o = refs[6:20]
    refs = refs[20:]
    shards, cast, here, refs = refs[:14], refs[14 : 14 + n], refs[14 + n : 14 + 2 * n], refs[14 + 2 * n :]
    patches, get, put, pick_s, bias_s, high_s, sum_s, oT_s, qkv_s = refs[:9]
    engine = Gather(Z, cast, here, chunks, refs[9:])
    loads = [pltpu.make_async_copy(given[i], shards[i], get.at[i]) for i in range(14)]
    for load in loads:
        load.start()
    load_patches = pltpu.make_async_copy(patches_h, patches, get.at[14])
    load_patches.start()
    cube = lax.axis_index(AXES)
    info[0] = lengths[cube]
    heads = orders[:, :ROWS_E]
    mine = lax.broadcasted_iota(jnp.int32, heads.shape, 0) == cube
    places[...] = jnp.sum(jnp.where(mine, heads, 0), axis=0, keepdims=True)
    small = cast[0]
    small[...] = jnp.zeros_like(small)
    for (row, _), k in zip(SMALL_AT, range(4)):
        loads[k].wait()
        small[row : row + shards[k].shape[0], : shards[k].shape[1]] = shards[k][...].astype(BF16)
    engine.greet()
    steps = iter(range(engine.ticks))

    def advance(t):
        if t < len(chunks) and chunks[t][0] and chunks[t][0] not in [m[0] for m in chunks[:t]]:
            i = chunks[t][0]
            loads[i + 3].wait()
            cast[i][...] = shards[i + 3][...].astype(BF16)
        engine.tick(t)

    def tick():
        advance(next(steps))

    def keep(i):
        return pltpu.make_async_copy(here[i], fulls[i - 1], put.at[i - 1])

    def bring(i):
        engine.arrived(i)
        if i:
            keep(i).start()

    def mat(i):
        shape = here[i].shape
        return here[i][...].reshape(8 * Z * shape[4], shape[5])

    for _ in range(7):
        tick()
    bring(0)
    load_patches.wait()
    count = info[0]
    visible = count // 10
    slots = patches.shape[0]
    pick_s[...] = pick_matrix(places[...], visible, slots)
    x = tn(pick_s[...], patches[...])
    x_o[...] = x
    tick()
    bring(6)
    values = here[0][...].reshape(8 * Z, SMALL_ROWS, 128).astype(F32)
    for out, (row, rows) in zip((e_gains, d_gains, e_bias, d_bias), SMALL_AT):
        w = out.shape[1] // (8 * Z)
        out[...] = jnp.concatenate([values[i, row : row + rows, :w] for i in range(8 * Z)], 1)
    tick()
    bring(7)
    X = d_gains[9:10] + mat(6).T.astype(F32)
    X_o[...] = X
    hat, _ = norm_parts(X)
    h = (hat * (1.0 + d_gains[0:1]) + d_gains[1:2]).astype(BF16)
    tick()
    dW = X.shape[1]

    def three(m):
        q = (m[:, :dW] + d_gains[4:5]).astype(BF16)
        k = (m[:, dW : 2 * dW] * (HD**-0.5 * math.log2(math.e))).astype(BF16)
        return q, k, (m[:, 2 * dW :] + d_gains[5:6]).astype(BF16)

    q_o[...], k_o[...], v_o[...] = three(nn(h, mat(7)))
    spot = lax.broadcasted_iota(jnp.int32, (slots, 1), 0)
    seen = jnp.sum(pick_s[...].astype(F32), axis=1, keepdims=True)
    bias_s[...] = jnp.where((spot < count) & (seen < 0.5), 0.0, FAR_BELOW)

    def masked_keys(g, turn):
        cols = pl.ds(pl.multiple_of(g * GROUP, GROUP), GROUP)
        kg = k_o[:, cols]
        qT = q_o[:, cols].T
        vT = v_o[:, cols].T
        for j in range(4):
            if j % 2 == 0:
                turn(j // 2)
            rows = slice(HD * j, HD * (j + 1))
            s = nn(kg, head_rows(qT, j)) + bias_s[...]
            high = jnp.max(s, axis=0, keepdims=True)
            p = jnp.exp2(s - high)
            high_s[g, j : j + 1, :] = high
            sum_s[g, j : j + 1, :] = jnp.sum(p, axis=0, keepdims=True)
            oT_s[g, rows, :] = nn(vT[rows], p.astype(BF16))

    groups = dW // GROUP
    turns = [next(steps) for _ in range(2 * (groups - 1))]

    @pl.loop(0, groups - 1)
    def _(g):
        def turn(k):
            for at in range(groups - 1):

                @pl.when(g == at)
                def _():
                    advance(turns[2 * at + k])

        masked_keys(g, turn)

    bring(1)
    bring(2)
    hat, _ = norm_parts(x)
    h = (hat * (1.0 + e_gains[0:1]) + e_gains[1:2]).astype(BF16)
    W = x.shape[1]
    m = nn(h, mat(1))
    q = (m[:, :W] + e_gains[4:5]).astype(BF16)
    k = m[:, W : 2 * W].astype(BF16)
    val = (m[:, 2 * W :] + e_gains[5:6]).astype(BF16)
    m_o[...] = jnp.concatenate([q, k, val], 1)
    live = lax.broadcasted_iota(jnp.int32, (ROWS_E, ROWS_E), 1) < visible
    hs = W // HEADS_E
    outs = []
    for j in range(HEADS_E):
        sl = slice(hs * j, hs * (j + 1))
        s = jnp.where(live, nt(q[:, sl], k[:, sl]) * hs**-0.5, FAR_BELOW)
        e = jnp.exp(s - jnp.max(s, axis=-1, keepdims=True))
        p = e / jnp.sum(e, axis=-1, keepdims=True)
        p_o[j] = p
        outs.append(nn(p.astype(BF16), val[:, sl]).astype(BF16))
    o = jnp.concatenate(outs, 1)
    o_o[...] = o
    tick()
    bring(3)
    x1 = x + (nn(o, mat(2)) + e_gains[6:7])
    x1_o[...] = x1
    hat2, _ = norm_parts(x1)
    h2 = (hat2 * (1.0 + e_gains[2:3]) + e_gains[3:4]).astype(BF16)
    u, dg = gelu_parts(nn(h2, mat(3)) + e_bias[...])
    u = u.astype(BF16)
    u_o[...] = u
    dg_o[...] = dg
    masked_keys(groups - 1, lambda k: tick())
    bring(4)
    tick()
    bring(5)
    encoded = (x1 + (nn(u, mat(4)) + e_gains[7:8])).astype(BF16)
    enc_o[...] = encoded
    here_pos = nn(mat(6), pick_s[...]).T
    Xv = nn(encoded, mat(5)) + d_gains[8:9] + here_pos
    hat, _ = norm_parts(Xv)
    h = (hat * (1.0 + d_gains[0:1]) + d_gains[1:2]).astype(BF16)
    qv, kv, vv = three(nn(h, mat(7)))
    qkv_s[...] = jnp.concatenate([qv, kv, vv], 1)
    seen = jnp.sum(pick_s[...].astype(F32), axis=1, keepdims=True) > 0.5
    X_o[...] = jnp.where(seen, place_rows(pick_s[...], Xv), X_o[...])
    for i, ref in enumerate((q_o, k_o, v_o)):
        placed = nn(pick_s[...], qkv_s[:, dW * i : dW * (i + 1)]).astype(BF16)
        ref[...] = jnp.where(seen, placed, ref[...])
    tick()
    rest = list(steps)
    seen_row = nt(jnp.ones((8, ROWS_E), BF16), pick_s[...])[0:1] > 0.5
    slot = lax.broadcasted_iota(jnp.int32, (ROWS_E, 1), 0)
    slot_bias = jnp.where(slot < visible, 0.0, FAR_BELOW)
    bias = dead_bias(count, slots)

    @pl.loop(0, groups)
    def _(g):
        for at, t in enumerate(rest):

            @pl.when(g == at)
            def _():
                advance(t)

        cols = pl.ds(pl.multiple_of(g * GROUP, GROUP), GROUP)
        vcols = pl.ds(pl.multiple_of(g * GROUP + 2 * dW, GROUP), GROUP)
        kcols = pl.ds(pl.multiple_of(g * GROUP + dW, GROUP), GROUP)
        qT = q_o[:, cols].T
        kvg = qkv_s[:, kcols]
        vvT = qkv_s[:, vcols].T
        qvT = qkv_s[:, cols].T
        s = nn(k_o[:, cols], jnp.concatenate([head_rows(qvT, j) for j in range(4)], 1))
        s = jnp.concatenate([s[:SHORT], s[SHORT:] + bias], 0)
        high = jnp.max(s, axis=0, keepdims=True)
        p = jnp.exp2(s - high)
        total = jnp.sum(p, axis=0, keepdims=True)
        o = nn(v_o[:, cols].T, p.astype(BF16)) * (1.0 / total)
        L = high + jnp.log2(total)
        per_head = [slice(ROWS_E * j, ROWS_E * (j + 1)) for j in range(4)]
        ov = jnp.concatenate([o[HD * j : HD * (j + 1), per_head[j]] for j in range(4)], 0)
        oT_seen = nt(ov.astype(BF16), pick_s[...])
        terms, left = [], jnp.concatenate([L[:, sl] for sl in per_head], 0)
        for _ in range(3):
            terms.append(left.astype(BF16))
            left = left - terms[-1].astype(F32)
        L_seen = nt(jnp.concatenate(terms, 1), jnp.concatenate([pick_s[...]] * 3, 1))
        outs = []
        for j in range(4):
            rows = slice(HD * j, HD * (j + 1))
            s = nn(kvg, head_rows(qT, j)) + slot_bias
            before = high_s[g, j : j + 1, :]
            high = jnp.maximum(jnp.max(s, axis=0, keepdims=True), before)
            p = jnp.exp2(s - high)
            kept = jnp.exp2(before - high)
            total = jnp.sum(p, axis=0, keepdims=True) + sum_s[g, j : j + 1, :] * kept
            o = nn(vvT[rows], p.astype(BF16)) + oT_s[g, rows, :] * kept
            o = jnp.where(seen_row, oT_seen[rows], o * (1.0 / total))
            outs.append(o.astype(BF16))
            L = high + jnp.log2(total)
            L_o[g, j : j + 1, :] = jnp.where(seen_row, L_seen[j : j + 1], L)
        att_o[:, cols] = jnp.concatenate(outs, 0).T

    for i in range(8, n):
        bring(i)
    engine.finish()
    for i in range(1, n):
        keep(i).wait()


def front(lengths, orders, patches, small_shards, arrays, Z):
    shapes = [(SMALL_ROWS, 128)] + [a.shape for a in arrays]
    n, count = len(shapes), 8 * Z
    cuts = (1, 3, 1, 3, 3, 1, 1, 1, 1, 2, 2)
    chunks = []
    for i in (0, 6, 7, 1, 2, 3, 4, 5, 8, 9, 10):
        w = shapes[i][1] // cuts[i]
        chunks += [(i, w * t, w) for t in range(cuts[i])]
    slots, W = patches.shape
    Fw, dW, dF = shapes[3][1], shapes[5][1], shapes[9][1]
    sd = jax.ShapeDtypeStruct
    outs = [sd((2, Z, 2, 2) + s, BF16) for s in shapes[1:]]
    outs += [sd((1,), jnp.int32), sd((1, ROWS_E), jnp.int32)]
    outs += [sd((8, W), F32), sd((16, dW), F32), sd((1, Fw), F32), sd((1, dF), F32)]
    R = ROWS_E
    outs += [sd((R, W), BF16), sd((R, W), F32), sd((R, 3 * W), BF16), sd((R, W), BF16)]
    outs += [sd((R, W), F32), sd((R, Fw), BF16), sd((R, Fw), F32), sd((HEADS_E, R, R), F32)]
    outs += [sd((slots, dW), F32)] + [sd((slots, dW), BF16)] * 4
    outs += [sd((dW // GROUP, 4, slots), F32)]
    m = len(chunks)
    given = (*small_shards, *arrays)
    return pl.pallas_call(
        functools.partial(front_kernel, Z, chunks),
        out_shape=outs,
        in_specs=[S, V, A] + [A] * 14,
        out_specs=[A] * (n - 1) + [S] + [V] * 19,
        scratch_shapes=[pltpu.VMEM(a.shape, F32) for a in given]
        + [pltpu.VMEM(s, BF16) for s in shapes]
        + [pltpu.VMEM((2, Z, 2, 2) + s, BF16) for s in shapes]
        + [pltpu.VMEM((slots, W), BF16), D((15,)), D((n - 1,))]
        + [pltpu.VMEM((slots, R), BF16), pltpu.VMEM((slots, 1), F32)]
        + [pltpu.VMEM((dW // GROUP, 4, slots), F32)] * 2
        + [pltpu.VMEM((dW // GROUP, GROUP, slots), F32), pltpu.VMEM((R, 3 * dW), BF16)]
        + [D((m,)), D((m, Z - 1)), D((m, Z - 1))]
        + [D((m, 4)), D((m, 4)), D((m, 5)), D((m, 5))],
        compiler_params=pltpu.CompilerParams(
            collective_id=0, has_side_effects=True, vmem_limit_bytes=62 * 2**20
        ),
    )(lengths, orders, patches, *given)


def dec_mid_kernel(steps, FC, info, x_r, o_r, cot_r, gains, bias, proj, fc1, fc2,
                   dec_o, gx1_o, go_o, gfc2_o, gfc1_o, gproj_o, gvec_o, gbias_o, *acc):
    i = pl.program_id(0)
    n, W = x_r.shape
    Fw = fc1.shape[1]
    if steps > 1:
        afc2, afc1, aproj = acc
        @pl.when(i == 0)
        def _():
            for ref in (afc2, afc1, aproj): ref[...] = jnp.zeros_like(ref)
    @pl.when(i == 0)
    def _():
        for ref in (gvec_o, gbias_o): ref[...] = jnp.zeros_like(ref)
    live = lax.broadcasted_iota(jnp.int32, (n, 1), 0) + i * n < info[0]
    o = o_r[...]
    x1 = x_r[...] + (nn(o, proj[...]) + gains[6:7])
    hat, r = norm_parts(x1)
    h2 = (hat * (1.0 + gains[2:3]) + gains[3:4]).astype(BF16)
    G = jnp.where(live, cot_r[...].astype(F32), 0.0)
    gy = G.astype(BF16)
    def first(c):
        sl = slice(c*FC, (c+1)*FC)
        return nn(h2, fc1[:, sl]), nt(gy, fc2[sl, :])
    nc = Fw//FC
    y = None; gh2 = None
    nxt = first(0)
    for c in range(nc):
        sl = slice(c*FC, (c+1)*FC)
        z, gu = nxt
        if c+1 < nc: nxt = first(c+1)
        u, dg = gelu_parts(z + bias[:, sl])
        u = u.astype(BF16)
        gz32 = gu * dg
        gz = gz32.astype(BF16)
        yc = nn(u, fc2[sl, :])
        y = yc if y is None else y + yc
        gc = nt(gz, fc1[:, sl])
        gh2 = gc if gh2 is None else gh2 + gc
        gbias_o[:, sl] += col_sum(gz.astype(F32))
        if steps > 1:
            afc2[sl, :] += tn(u, gy)
            afc1[:, sl] += tn(h2, gz)
        else:
            gfc2_o[sl, :] = tn(u, gy).astype(BF16)
            gfc1_o[:, sl] = tn(h2, gz).astype(BF16)
    y = x1 + (y + gains[7:8])
    dec_o[...] = jnp.where(live, y, 0.0).astype(BF16)
    gvec_o[0:1, :] += col_sum(gh2 * hat)
    gvec_o[1:2, :] += col_sum(gh2)
    gx1 = G + norm_back(gh2, hat, r, gains[2:3])
    gx1_o[...] = gx1
    ga = gx1.astype(BF16)
    gvec_o[2:3, :] += col_sum(ga.astype(F32))
    gvec_o[3:4, :] += col_sum(G)
    go_o[...] = nt(ga, proj[...]).astype(BF16)
    if steps > 1:
        aproj[...] += tn(o, ga)
        @pl.when(i == steps - 1)
        def _():
            gfc2_o[...] = afc2[...].astype(BF16)
            gfc1_o[...] = afc1[...].astype(BF16)
            gproj_o[...] = aproj[...].astype(BF16)
    else:
        gproj_o[...] = tn(o, ga).astype(BF16)

def dec_mid(info, x, o, cot, gains, bias, proj, fc1, fc2, tile=1024, FC=1024):
    n, W = x.shape
    sd = jax.ShapeDtypeStruct
    full = lambda a: pl.BlockSpec(a.shape, lambda i: (0,)*a.ndim)
    row = pl.BlockSpec((tile, W), lambda i: (i, 0))
    Fw = fc1.shape[1]
    outs = (sd((n, W), BF16), sd((n, W), F32), sd((n, W), BF16), sd(fc2.shape, BF16), sd(fc1.shape, BF16), sd(proj.shape, BF16), sd((8, W), F32), sd((1, Fw), F32))
    return pl.pallas_call(functools.partial(dec_mid_kernel, n//tile, FC), grid=(n//tile,), out_shape=outs,
        in_specs=[S, row, row, row, full(gains), full(bias), full(proj), full(fc1), full(fc2)],
        out_specs=(row, row, row) + tuple(full(a) for a in outs[3:]),
        scratch_shapes=[pltpu.VMEM(w.shape, F32) for w in (fc2, fc1, proj)] if n > tile else [],
        compiler_params=params(60))(info, x, o, cot, gains, bias, proj, fc1, fc2)

def dec_post_kernel(steps, info, places, x_r, gx1_r, gq_r, gk_r, gv_r, gains, qkv, gqkv_o, gposT_o, gemb_o, gvec_o, aqkv, aemb):
    i = pl.program_id(0)
    @pl.when(i == 0)
    def _():
        for ref in (aqkv, aemb, gvec_o): ref[...] = jnp.zeros_like(ref)
    n = x_r.shape[0]
    x = x_r[...]
    hat, r = norm_parts(x)
    h = (hat * (1.0 + gains[0:1]) + gains[1:2]).astype(BF16)
    gm = jnp.concatenate([gq_r[...], gk_r[...], gv_r[...]], 1)
    W = x.shape[1]
    aqkv[...] += tn(h, gm)
    gh = nt(gm, qkv[...])
    gvec_o[0:1, :] += col_sum(gh * hat)
    gvec_o[1:2, :] += col_sum(gh)
    gvec_o[4:5, :] += col_sum(gq_r[...].astype(F32))
    gvec_o[5:6, :] += col_sum(gv_r[...].astype(F32))
    gx = gx1_r[...] + norm_back(gh, hat, r, gains[0:1])
    gxb = gx.astype(BF16)
    gposT_o[...] = gxb.T
    pos_i = lax.broadcasted_iota(jnp.int32, (n, ROWS_E), 0) + i * n
    rr = lax.broadcasted_iota(jnp.int32, (n, ROWS_E), 1)
    pick = ((pos_i == places[...]) & (rr < info[0] // 10)).astype(BF16)
    seen = jnp.sum(pick.astype(F32), axis=1, keepdims=True)
    aemb[...] += tn(pick, gxb)
    gvec_o[9:10, :] += col_sum(gx * (1.0 - seen))
    @pl.when(i == steps - 1)
    def _():
        gqkv_o[...] = aqkv[...].astype(BF16)
        gemb_o[...] = aemb[...].astype(BF16)
        gvec_o[8:9, :] = col_sum(aemb[...])

def dec_post(info, places, x, gx1, gq, gk, gv, gains, qkv, tile=1024):
    n, W = x.shape
    sd = jax.ShapeDtypeStruct
    full = lambda a: pl.BlockSpec(a.shape, lambda i: (0,)*a.ndim)
    row = pl.BlockSpec((tile, W), lambda i: (i, 0))
    outs = (sd(qkv.shape, BF16), sd((W, n), BF16), sd((ROWS_E, W), BF16), sd((16, W), F32))
    return pl.pallas_call(functools.partial(dec_post_kernel, n//tile), grid=(n//tile,), out_shape=outs,
        in_specs=[S, full(places), row, row, row, row, row, full(gains), full(qkv)],
        out_specs=(full(outs[0]), pl.BlockSpec((W, tile), lambda i: (0, i)), full(outs[2]), full(outs[3])),
        scratch_shapes=[pltpu.VMEM(qkv.shape, F32), pltpu.VMEM((ROWS_E, W), F32)],
        compiler_params=params())(info, places, x, gx1, gq, gk, gv, gains, qkv)

SPOTS = (0, 2, 4, 6, 8, 10, 12, 14, 16)


def attend_back_kernel(Z, chunks, info, q_ref, k_ref, v_ref, go_ref, o_ref, L_ref, *refs):
    blocks, (gq_ref, gk_ref, gv_ref), outs, rest = refs[:3], refs[3:6], refs[6:9], refs[9:]
    lands, rest = rest[:3], rest[3:]
    engine = Scatter(Z, take_buffers(rest[:-7], blocks, (True,) * 3, lands), chunks, rest[-7:])
    g = pl.program_id(0)

    @pl.when(g == 0)
    def _():
        engine.greet()

    q = q_ref[...]
    k = k_ref[...]
    v = v_ref[...]
    go = go_ref[...]
    bias = dead_bias(info[0], k.shape[0])
    qT, kT, goT, oT = q.T, k.T, go.T, o_ref[...].T
    inner_all = goT.astype(F32) * oT.astype(F32)
    ak = av = None
    gqs = []
    for j in range(4):
        for step in range(4):
            if 4 * step + j in SPOTS:

                @pl.when(g == step)
                def _():
                    engine.tick(SPOTS.index(4 * step + j))

        rows = slice(HD * j, HD * (j + 1))
        s = nn(k, head_rows(qT, j))
        s = jnp.concatenate([s[:SHORT], s[SHORT:] + bias], 0)
        p = jnp.exp2(s - L_ref[0, j : j + 1, :])
        gp = nn(v, head_rows(goT, j))
        inner = jnp.sum(inner_all[rows], axis=0, keepdims=True)
        gs = (p * (gp - inner)).astype(BF16)
        a = nn(p.astype(BF16), head_lanes(go, j))
        b = nn(gs, head_lanes(q, j))
        av = a if av is None else av + a
        ak = b if ak is None else ak + b
        gqs.append((nn(kT[rows], gs) * math.log(2.0)).astype(BF16))
    gq_ref[...] = jnp.concatenate(gqs, 0).T
    gk_ref[...] = (ak * HD**-0.5).astype(BF16)
    gv_ref[...] = av.astype(BF16)

    @pl.when(g == 3)
    def _():
        engine.tick(SPOTS.index(16))
        engine.finish()
        for out, land in zip(outs, lands):
            out[...] = land[...]


def attend_back(info, q, k, v, go, o, L, grads, Z):
    n, W = k.shape
    blk = pl.BlockSpec((n, GROUP), lambda g: (0, g))
    shapes = [a.shape[4:] for a in grads]
    chunks = []
    for i, (r, c) in enumerate(shapes[:2]):
        chunks += [(i, 0, c // 2), (i, c // 2, c // 2)]
    chunks.append((2, 0, shapes[2][1]))
    buffers, sems = scatter_buffers(shapes, (True,) * 3, Z, chunks)
    outs = [jax.ShapeDtypeStruct((Z, *s), BF16) for s in shapes]
    return pl.pallas_call(
        functools.partial(attend_back_kernel, Z, chunks),
        grid=(W // GROUP,),
        out_shape=[jax.ShapeDtypeStruct((n, W), BF16)] * 3 + outs,
        in_specs=[S, blk, blk, blk, blk, blk, pl.BlockSpec((1, 4, n), lambda g: (g, 0, 0))]
        + [A] * 3,
        out_specs=[blk] * 3 + [V] * 3,
        scratch_shapes=[pltpu.VMEM(a.shape, BF16) for a in outs] + buffers + sems,
        compiler_params=pltpu.CompilerParams(
            collective_id=1, has_side_effects=True, vmem_limit_bytes=60 * 2**20
        ),
    )(info, q, k, v, go, o, L, *grads)


def enc_bwd_kernel(Z, chunks, *refs):
    given, small_in, blocks_in = refs[:14], refs[14:18], refs[18:20]
    gx_o, outs, rest = refs[20], refs[21:29], refs[29:]
    local, made, rest = rest[:13], rest[13:19], rest[19:]
    e_vec, e_bias, whole, sem = rest[-11:-7]
    loaded = (True, True) + (False,) * 6
    engine = Scatter(
        Z, take_buffers(rest[:-11], (*blocks_in, *made), loaded, outs), chunks, rest[-7:]
    )
    g_embed, g_fc2, g_fc1, g_proj, g_qkv, g_small = made
    gains, mid_vec, post_vec, d_bias = small_in
    places = (*local, local[8].at[:, pl.ds(0, given[13].shape[1])])
    loads = [pltpu.make_async_copy(given[i], places[i], sem.at[i]) for i in range(14)]
    for load in loads[:13]:
        load.start()

    def got(i):
        loads[i].wait()
        return places[i][...]

    engine.greet()
    steps = iter(range(engine.ticks))

    def tick():
        engine.tick(next(steps))

    def store(ref, value):
        ref[...] = value.astype(BF16).reshape(ref.shape)

    tick()
    ge = got(0)
    store(g_embed, tn(got(1), ge))
    gy = nt(ge, got(2)).astype(BF16)
    G = gy.astype(F32)
    tick()
    u = got(3)
    store(g_fc2, tn(u, gy))
    tick()
    gz = (nt(gy, got(4)) * got(5)).astype(BF16)
    e_bias[...] = col_sum(gz.astype(F32))
    tick()
    hat2, r2 = norm_parts(got(6))
    h2 = (hat2 * (1.0 + gains[2:3]) + gains[3:4]).astype(BF16)
    store(g_fc1, tn(h2, gz))
    tick()
    gh2 = nt(gz, got(8))
    loads[13].start()
    e_vec[2:3, :] = col_sum(gh2 * hat2)
    e_vec[3:4, :] = col_sum(gh2)
    gx1 = G + norm_back(gh2, hat2, r2, gains[2:3])
    ga = gx1.astype(BF16)
    e_vec[6:7, :] = col_sum(ga.astype(F32))
    e_vec[7:8, :] = col_sum(G)
    store(g_proj, tn(got(7), ga))
    tick()
    go = nt(ga, got(9)).astype(BF16)
    for i in (10, 11, 12):
        loads[i].wait()
    m_r, p_r, x_r = places[10:13]
    W = gx1.shape[1]
    hs = W // HEADS_E
    gq, gk, gv = [], [], []
    for j in range(HEADS_E):
        q = m_r[:, hs * j : hs * (j + 1)]
        k = m_r[:, W + hs * j : W + hs * (j + 1)]
        val = m_r[:, 2 * W + hs * j : 2 * W + hs * (j + 1)]
        g = go[:, hs * j : hs * (j + 1)]
        p = p_r[j]
        gv.append(tn(p.astype(BF16), g).astype(BF16))
        gp = nt(g, val)
        gs = (p * (gp - jnp.sum(gp * p, axis=-1, keepdims=True))).astype(BF16)
        gq.append((nn(gs, k) * hs**-0.5).astype(BF16))
        gk.append((tn(gs, q) * hs**-0.5).astype(BF16))
        if j == HEADS_E // 2:
            tick()
    gm = jnp.concatenate(gq + gk + gv, 1)
    tick()
    e_vec[4:5, :] = col_sum(gm[:, :W].astype(F32))
    e_vec[5:6, :] = col_sum(gm[:, 2 * W :].astype(F32))
    hat, r = norm_parts(x_r[...])
    h = (hat * (1.0 + gains[0:1]) + gains[1:2]).astype(BF16)
    store(g_qkv, tn(h, gm))
    tick()
    gh = nt(gm, got(13))
    e_vec[0:1, :] = col_sum(gh * hat)
    e_vec[1:2, :] = col_sum(gh)
    gx_o[...] = gx1 + norm_back(gh, hat, r, gains[0:1])
    pack(g_small, e_vec, e_bias, mid_vec, post_vec, d_bias, whole)
    for t in steps:
        engine.tick(t)
    engine.finish()


def pack(out, e_vec, e_bias, mid_vec, post_vec, d_bias, whole):
    Z = out.shape[1]
    count = 8 * Z
    whole[...] = jnp.zeros_like(whole)
    whole[0:2] = post_vec[0:2]
    whole[2:4] = mid_vec[0:2]
    whole[4:6] = post_vec[4:6]
    whole[6:8] = mid_vec[2:4]
    whole[8:10] = post_vec[8:10]
    out[...] = jnp.zeros_like(out)
    for ref, row, rows in ((e_vec, 0, 8), (whole, 8, 16), (e_bias, 24, 1), (d_bias, 25, 1)):
        w = ref.shape[1] // count
        values = ref[...].astype(BF16)
        for i in range(count):
            at = (i // (4 * Z), i // 4 % Z, i // 2 % 2, i % 2)
            out[(*at, slice(row, row + rows), slice(0, w))] = values[:, w * i : w * i + w]


def enc_bwd(encoded, gemb, embed, kept, mats, small_in, blocks_in, Z):
    x, m, o, x1, u, dg, p = kept
    qkv, proj, fc1, fc2 = mats
    given = (gemb, encoded, embed, u, fc2, dg, x1, o, fc1, proj, m, p, x, qkv)
    count = 8 * Z

    def block_shape(a):
        return (a.shape[0] // count, a.shape[1])

    shapes = [a.shape[4:] for a in blocks_in]
    shapes += [block_shape(a) for a in (embed, fc2, fc1, proj, qkv)] + [(SMALL_ROWS, 128)]
    W, Fw = fc1.shape
    chunks = [(1, 0, shapes[1][1]), (0, 0, shapes[0][1]), (2, 0, shapes[2][1])]
    chunks += [(3, t * W // 3, W // 3) for t in range(3)]
    chunks += [(4, t * Fw // 3, Fw // 3) for t in range(3)]
    chunks += [(5, 0, W)] + [(6, t * W, W) for t in range(3)] + [(7, 0, 128)]
    loaded = (True, True) + (False,) * 6
    buffers, sems = scatter_buffers(shapes, loaded, Z, chunks)
    sd = jax.ShapeDtypeStruct
    return pl.pallas_call(
        functools.partial(enc_bwd_kernel, Z, chunks),
        out_shape=[sd(x.shape, F32)] + [sd((Z, *s), BF16) for s in shapes],
        in_specs=[A] * 14 + [V] * 4 + [A] * 2,
        out_specs=[V] * 9,
        scratch_shapes=[pltpu.VMEM(a.shape, a.dtype) for a in given[:13]]
        + [pltpu.VMEM((2, Z, 2, 2, *s), BF16) for s in shapes[2:]]
        + buffers
        + [pltpu.VMEM((8, W), F32), pltpu.VMEM((1, Fw), F32), pltpu.VMEM((16, embed.shape[1]), F32)]
        + [D((14,))]
        + sems,
        compiler_params=pltpu.CompilerParams(
            collective_id=2, has_side_effects=True, vmem_limit_bytes=62 * 2**20
        ),
    )(*given, *small_in, *blocks_in)


def last_kernel(n, info, places, gx, *refs):
    ins, g_patch, outs = refs[:n], refs[n], refs[n + 1 :]
    pick = pick_matrix(places[...], info[0] // 10, g_patch.shape[0])
    g_patch[...] = place_rows(pick, gx[...])

    def total(ref):
        acc = ref[0].astype(F32)
        for d in range(1, ref.shape[0]):
            acc = acc + ref[d].astype(F32)
        return acc

    small = total(ins[0])
    for out, row in zip(outs[:4], (0, 8, 24, 25)):
        out[...] = small[row : row + out.shape[0], : out.shape[1]]
    for i, ref in enumerate(ins[1:]):
        outs[4 + i][...] = total(ref)


def last_sums(info, places, gx, arrays, shapes):
    return pl.pallas_call(
        functools.partial(last_kernel, len(arrays)),
        out_shape=[jax.ShapeDtypeStruct(s, F32) for s in shapes],
        in_specs=[S] + [V] * (2 + len(arrays)),
        compiler_params=params(),
    )(info, places, gx, *arrays)


def body(
    patches,
    lengths,
    keep_order,
    e_vectors,
    e_qkv,
    e_proj,
    e_fc1,
    e_fc1_bias,
    e_fc2,
    embed,
    d_vectors,
    dec_pos,
    d_qkv,
    d_proj,
    d_fc1,
    d_fc1_bias,
    d_fc2,
    cotangent,
):
    Z = lax.axis_size("dp") // 4
    slots = patches.shape[1]
    smalls = (e_vectors, d_vectors, e_fc1_bias.reshape(1, -1), d_fc1_bias.reshape(1, -1))
    shards = (e_qkv, e_proj, e_fc1, e_fc2, embed, dec_pos.T, d_qkv, d_proj, d_fc1, d_fc2)
    made = front(lengths, keep_order, patches[0], smalls, shards, Z)
    mats = [m.reshape(-1, m.shape[-1]) for m in made[:10]]
    w_qkv, w_proj, w_fc1, w_fc2, w_embed, posT, dw_qkv, dw_proj, dw_fc1, dw_fc2 = mats
    info, places, e_gains, d_gains, e_bias, d_bias, encoded, *kept = made[10:24]
    x, q, k, v, o, L = made[24:]
    decoded, gx1, go, gd_fc2, gd_fc1, gd_proj, mid_vec, gd_bias = dec_mid(
        info, x, o, cotangent[0], d_gains, d_bias, dw_proj, dw_fc1, dw_fc2
    )

    def blocks(m):
        return m.reshape((2, Z, 2, 2, -1, m.shape[-1]))

    gq, gk, gv, *early = attend_back(
        info, q, k, v, go, o, L, [blocks(m) for m in (gd_fc2, gd_fc1, gd_proj)], Z
    )
    gd_qkv, g_posT, gemb, post_vec = dec_post(
        info, places, x, gx1, gq, gk, gv, d_gains, dw_qkv
    )
    gx, *late = enc_bwd(
        encoded,
        gemb,
        w_embed,
        kept,
        (w_qkv, w_proj, w_fc1, w_fc2),
        (e_gains, mid_vec, post_vec, gd_bias),
        (blocks(gd_qkv), blocks(g_posT)),
        Z,
    )
    pd_qkv, p_pos, p_embed, p_fc2, p_fc1, p_proj, p_qkv, p_small = late
    parts = (p_small, p_qkv, p_proj, p_fc1, p_fc2, p_embed, p_pos, pd_qkv, *early[::-1])
    shapes = [(slots, patches.shape[2])] + [m.shape for m in smalls + shards]
    g_patch, *out = last_sums(info, places, gx, parts, shapes)
    re_vec, rd_vec, re_bias, rd_bias = out[:4]
    re_qkv, re_proj, re_fc1, re_fc2, r_embed, r_pos, rd_qkv, rd_proj, rd_fc1, rd_fc2 = out[4:]
    return (
        decoded[None],
        g_patch[None],
        re_vec,
        re_qkv,
        re_proj,
        re_fc1,
        re_bias.reshape(-1),
        re_fc2,
        r_embed,
        rd_vec,
        r_pos.T,
        rd_qkv,
        rd_proj,
        rd_fc1,
        rd_bias.reshape(-1),
        rd_fc2,
    )


def solution(mesh):
    rows, columns, cubes = P(AXES, None), P(None, AXES), P(AXES, None, None)
    weights = (columns, rows, rows, rows, P(AXES), rows, rows, columns, columns)
    weights = weights + (rows, rows, rows, P(AXES), rows)
    return jax.shard_map(
        body,
        mesh=mesh,
        in_specs=(cubes, P(), P()) + weights + (cubes,),
        out_specs=(cubes, cubes) + weights,
        check_vma=False,
    )
```

```python
import functools
import math

import jax
import jax.numpy as jnp
from jax import lax
from jax.experimental import pallas as pl
from jax.experimental.pallas import tpu as pltpu
from jax.sharding import PartitionSpec as P

HEADS_E = 12
HEADS_D = 16
VIS = 104
SHORT = 576
HD = 32
GROUP = 128
F32 = jnp.float32
BF16 = jnp.bfloat16
AXES = ("segment", "dp")
MESH = pl.DeviceIdType.MESH
ROWS_E = 128
NORM_EPS = 1e-06
FAR_BELOW = -1e30


SMALL_ROWS = 32


def place():
    s = lax.axis_index("segment")
    dp = lax.axis_index("dp")
    return s, dp // 4, (dp // 2) % 2, dp % 2


def device(s, z, y, c):
    return (s, (z * 2 + y) * 2 + c)


def halves(columns):
    return (columns // 2, columns // 2) if columns % 256 == 0 else (columns, 0)


def greet(peers):
    barrier = pltpu.get_barrier_semaphore()
    for peer in peers:
        pl.semaphore_signal(barrier, inc=1, device_id=peer, device_id_type=MESH)
    pl.semaphore_wait(barrier, len(peers))


class Gather:
    def __init__(self, Z, shards, outs, chunks, sems):
        self.Z, self.shards, self.outs, self.chunks = Z, shards, outs, chunks
        self.loc, self.zs, self.zr, self.ms, self.mr, self.cs, self.cr = sems
        self.s, self.z, self.y, self.c = s, z, y, c = place()
        self.X, self.Y = device(1 - s, z, y, c), device(s, z, 1 - y, c)
        self.C = device(s, z, y, 1 - c)
        self.z_peers = [device(s, lax.rem(z + d, Z), y, c) for d in range(1, Z)]

    def greet(self):
        greet(self.z_peers + [self.X, self.Y, self.C])

    def copy(self, src, dst, ss, rs, target):
        return pltpu.make_async_remote_copy(
            src_ref=src,
            dst_ref=dst,
            send_sem=ss,
            recv_sem=rs,
            device_id=target,
            device_id_type=MESH,
        )

    def own(self, m):
        i, start, width = self.chunks[m]
        cols = pl.ds(start, width)
        return pltpu.make_async_copy(
            self.shards[i].at[:, cols],
            self.outs[i].at[self.s, self.z, self.y, self.c, :, cols],
            self.loc.at[m],
        )

    def copies(self, m, stage):
        i, start, width = self.chunks[m]
        ka, kb = halves(width)
        s, z, y, c = self.s, self.z, self.y, self.c
        o = self.outs[i]
        cols, A = pl.ds(start, width), pl.ds(start, ka)
        B = pl.ds(start + ka, kb) if kb else None
        if stage == 0:
            return [
                self.copy(
                    self.shards[i].at[:, cols],
                    o.at[s, z, y, c, :, cols],
                    self.zs.at[m, d],
                    self.zr.at[m, d],
                    self.z_peers[d],
                )
                for d in range(self.Z - 1)
            ]
        if stage == 1:
            made = [(o.at[s, :, y, c, :, A], 0, self.X)]
            if kb:
                made.append((o.at[s, :, y, c, :, B], 1, self.Y))
        elif stage == 2:
            made = [(o.at[:, :, y, c, :, A], 2, self.Y)]
            if kb:
                made.append((o.at[s, :, :, c, :, B], 3, self.X))
        elif stage == 11:
            made = [(o.at[s, :, y, c, :, cols], 0, self.C)]
        elif stage == 12:
            made = [(o.at[1 - s, :, y, c, :, A], 1, self.C)]
            if kb:
                made.append((o.at[s, :, 1 - y, c, :, B], 2, self.C))
        else:
            made = [(o.at[:, :, 1 - y, c, :, A], 3, self.C)]
            if kb:
                made.append((o.at[1 - s, :, :, c, :, B], 4, self.C))
        ss, rs = (self.cs, self.cr) if stage > 10 else (self.ms, self.mr)
        return [self.copy(ref, ref, ss.at[m, k], rs.at[m, k], target) for ref, k, target in made]

    def stage(self, m, stage):
        if stage == 0:
            self.own(m).start()
        else:
            if stage == 1:
                self.own(m).wait()
            for copy in self.copies(m, stage - 1):
                copy.wait_recv()
        if stage < 3:
            for copy in self.copies(m, stage):
                copy.start()
        if stage > 0:
            for copy in self.copies(m, stage + 10):
                copy.start()

    @property
    def ticks(self):
        return len(self.chunks) + 6

    def tick(self, t):
        for k in range(4):
            if 0 <= t - 2 * k < len(self.chunks):
                self.stage(t - 2 * k, k)

    def arrived(self, i):
        for m, chunk in enumerate(self.chunks):
            if chunk[0] == i:
                for stage in (11, 12, 13):
                    for copy in self.copies(m, stage):
                        copy.wait_recv()

    def finish(self):
        for m in range(len(self.chunks)):
            for stage in (0, 1, 2, 11, 12, 13):
                for copy in self.copies(m, stage):
                    copy.wait_send()


class Scatter:
    def __init__(self, Z, arrays, chunks, sems):
        self.Z, self.arrays, self.chunks = Z, arrays, chunks
        self.loc, self.cs, self.cr, self.ms, self.mr, self.zs, self.zr = sems
        self.s, self.z, self.y, self.c = s, z, y, c = place()
        self.X, self.Y = device(1 - s, z, y, c), device(s, z, 1 - y, c)
        self.C = device(s, z, y, 1 - c)
        self.z_peers = [device(s, lax.rem(z + d, Z), y, c) for d in range(1, Z)]

    def greet(self):
        greet(self.z_peers + [self.X, self.Y, self.C])

    def parts(self, m):
        i, start, width = self.chunks[m]
        ka, kb = halves(width)
        return i, start, width, ka, kb, (start // 2 if kb else start)

    def held(self, i, index, columns):
        blocks, held = self.arrays[i][:2]
        if held is None:
            ss, zz, yy = index
            return blocks.at[ss, zz, yy, self.c, :, columns]
        return held.at[(*index, slice(None), columns)]

    def copy(self, src, dst, ss, rs, target):
        return pltpu.make_async_remote_copy(
            src_ref=src,
            dst_ref=dst,
            send_sem=ss,
            recv_sem=rs,
            device_id=target,
            device_id_type=MESH,
        )

    def own(self, m):
        i, start, width, *_ = self.parts(m)
        blocks, held = self.arrays[i][:2]
        if held is None:
            return None
        cols = pl.ds(start, width)
        return pltpu.make_async_copy(
            blocks.at[:, :, :, self.c, :, cols], held.at[:, :, :, :, cols], self.loc.at[m]
        )

    def copies(self, m, stage):
        i, start, width, ka, kb, at = self.parts(m)
        s, z, y, c, Z = self.s, self.z, self.y, self.c, self.Z
        blocks, held, R0, R1A, R1B, R2A, R2B, out = self.arrays[i]
        cols, A, B = pl.ds(start, width), pl.ds(start, ka), pl.ds(start + ka, kb)
        half = pl.ds(at, ka)
        full = slice(None)
        if stage == 0:
            return [
                self.copy(
                    blocks.at[:, :, :, 1 - c, :, cols],
                    R0.at[:, :, :, :, cols],
                    self.cs.at[m],
                    self.cr.at[m],
                    self.C,
                )
            ]
        if stage == 1:
            made = [(self.held(i, (full, full, 1 - y), A), R1A.at[:, :, :, half], self.Y)]
            if kb:
                made.append((self.held(i, (1 - s, full, full), B), R1B.at[:, :, :, half], self.X))
        elif stage == 2:
            made = [(self.held(i, (1 - s, full, y), A), R2A.at[:, :, half], self.X)]
            if kb:
                made.append((self.held(i, (s, full, 1 - y), B), R2B.at[:, :, half], self.Y))
        else:
            return [
                self.copy(
                    self.held(i, (s, lax.rem(z + d, Z), y), cols),
                    out.at[d, :, cols],
                    self.zs.at[m, d - 1],
                    self.zr.at[m, d - 1],
                    self.z_peers[d - 1],
                )
                for d in range(1, Z)
            ]
        k = 2 * (stage - 1)
        return [
            self.copy(src, dst, self.ms.at[m, k + j], self.mr.at[m, k + j], target)
            for j, (src, dst, target) in enumerate(made)
        ]

    def add(self, i, index, columns, other):
        ref = self.held(i, index, columns)
        ref[...] = ref[...] + other[...]

    def stage(self, m, stage):
        i, start, width, ka, kb, at = self.parts(m)
        s, z, y, Z = self.s, self.z, self.y, self.Z
        blocks, held, R0, R1A, R1B, R2A, R2B, out = self.arrays[i]
        cols, A, B = pl.ds(start, width), pl.ds(start, ka), pl.ds(start + ka, kb)
        half = pl.ds(at, ka)
        if stage == 0:
            own = self.own(m)
            if own is not None:
                own.start()
        else:
            if stage == 1 and held is not None:
                self.own(m).wait()
            for copy in self.copies(m, stage - 1):
                copy.wait_recv()
        if stage == 1:

            @pl.loop(0, 4 * Z)
            def _(t):
                index = (t // (Z * 2), (t // 2) % Z, t % 2)
                self.add(i, index, cols, R0.at[(*index, slice(None), cols)])

        elif stage == 2:

            @pl.loop(0, 2 * Z)
            def _(t):
                u, zz = t // Z, t % Z
                self.add(i, (u, zz, y), A, R1A.at[u, zz, :, half])
                if kb:
                    self.add(i, (s, zz, u), B, R1B.at[zz, u, :, half])

        elif stage == 3:

            @pl.loop(0, Z)
            def _(zz):
                self.add(i, (s, zz, y), A, R2A.at[zz, :, half])
                if kb:
                    self.add(i, (s, zz, y), B, R2B.at[zz, :, half])

        elif stage == 4:
            out[0, :, cols] = self.held(i, (s, z, y), cols)[...]
            return
        for copy in self.copies(m, stage):
            copy.start()

    @property
    def ticks(self):
        return len(self.chunks) + 4

    def tick(self, t):
        for k in range(5):
            if 0 <= t - k < len(self.chunks):
                self.stage(t - k, k)

    def finish(self):
        for m in range(len(self.chunks)):
            for stage in range(4):
                for copy in self.copies(m, stage):
                    copy.wait_send()


def scatter_buffers(shapes, loaded, Z, chunks):
    refs = []
    for (r, k), load in zip(shapes, loaded):
        ka, kb = halves(k)
        kb = max(kb, 128)
        if load:
            refs.append((2, Z, 2, r, k))
        refs += [(2, Z, 2, r, k), (2, Z, r, ka), (Z, 2, r, kb), (Z, r, ka), (Z, r, kb)]
    n = len(chunks)
    D = pltpu.SemaphoreType.DMA
    return [pltpu.VMEM(s, BF16) for s in refs], [
        D((n,)),
        D((n,)),
        D((n,)),
        D((n, 4)),
        D((n, 4)),
        D((n, Z - 1)),
        D((n, Z - 1)),
    ]


def take_buffers(refs, blocks, loaded, outs):
    refs = list(refs)
    arrays = []
    for block, load, out in zip(blocks, loaded, outs):
        held = refs.pop(0) if load else None
        arrays.append((block, held, *(refs.pop(0) for _ in range(5)), out))
    return arrays


def nn(a, b): return jnp.dot(a, b, preferred_element_type=F32)
def nt(a, b): return lax.dot_general(a, b, (((1,), (1,)), ((), ())), preferred_element_type=F32)
def tn(a, b): return lax.dot_general(a, b, (((0,), (0,)), ((), ())), preferred_element_type=F32)

def norm_parts(x):
    center = x - jnp.mean(x, axis=-1, keepdims=True)
    r = lax.rsqrt(jnp.mean(center * center, axis=-1, keepdims=True) + NORM_EPS)
    return center * r, r

def norm_back(g, hat, r, gain):
    w = g * (1.0 + gain)
    return r * (w - jnp.mean(w, axis=-1, keepdims=True) - hat * jnp.mean(w * hat, axis=-1, keepdims=True))

def gelu_parts(z):
    x = jnp.abs(z) * math.sqrt(0.5)
    t = 1.0 / (1.0 + 0.3275911 * x)
    e = jnp.exp(-(x * x))
    poly = t * (0.254829592 + t * (-0.284496736 + t * (1.421413741 + t * (-1.453152027 + t * 1.061405429))))
    half = 0.5 * poly * e
    cdf = jnp.where(z > 0, 1.0 - half, half)
    return z * cdf, cdf + z * e * (1.0 / math.sqrt(2.0 * math.pi))

def col_sum(m): return jnp.sum(m, axis=0, keepdims=True)

def pick_matrix(places_row, keep_count, slots):
    pos = lax.broadcasted_iota(jnp.int32, (slots, ROWS_E), 0)
    r = lax.broadcasted_iota(jnp.int32, (slots, ROWS_E), 1)
    return ((pos == places_row) & (r < keep_count)).astype(BF16)

V = pl.BlockSpec(memory_space=pltpu.VMEM); A = pl.BlockSpec(memory_space=pl.ANY); S = pl.BlockSpec(memory_space=pltpu.SMEM)
D = pltpu.SemaphoreType.DMA
def params(mb=56): return pltpu.CompilerParams(vmem_limit_bytes=mb*2**20)

def head_rows(block, j):
    parts = []
    if j > 0: parts.append(jnp.zeros((HD*j, block.shape[1]), block.dtype))
    parts.append(block[HD*j:HD*(j+1)])
    if j < 3: parts.append(jnp.zeros((HD*(3-j), block.shape[1]), block.dtype))
    return jnp.concatenate(parts, 0)

def head_lanes(block, j):
    lane = lax.broadcasted_iota(jnp.int32, block.shape, 1)
    return jnp.where((lane >= HD*j) & (lane < HD*(j+1)), block, jnp.zeros_like(block))

def dead_bias(count, n):
    return jnp.where(lax.broadcasted_iota(jnp.int32, (n - SHORT, 1), 0) + SHORT < count, 0.0, FAR_BELOW)

SMALL_AT = ((0, 8), (8, 16), (24, 1), (25, 1))


def place_rows(pick, rows):
    terms, left = [], rows
    for _ in range(3):
        terms.append(left.astype(BF16))
        left = left - terms[-1].astype(F32)
    return nn(jnp.concatenate([pick] * 3, 1), jnp.concatenate(terms, 0))


def front_kernel(Z, chunks, *refs):
    n = 11
    lengths, orders, patches_h, given, refs = refs[0], refs[1], refs[2], refs[3:17], refs[17:]
    fulls, refs = refs[: n - 1], refs[n - 1 :]
    info, places, e_gains, d_gains, e_bias, d_bias = refs[:6]
    enc_o, x_o, m_o, o_o, x1_o, u_o, dg_o, p_o, X_o, q_o, k_o, v_o, att_o, L_o = refs[6:20]
    refs = refs[20:]
    shards, cast, here, refs = refs[:14], refs[14 : 14 + n], refs[14 + n : 14 + 2 * n], refs[14 + 2 * n :]
    patches, get, put, pick_s, bias_s, high_s, sum_s, oT_s, qkv_s = refs[:9]
    engine = Gather(Z, cast, here, chunks, refs[9:])
    loads = [pltpu.make_async_copy(given[i], shards[i], get.at[i]) for i in range(14)]
    for load in loads:
        load.start()
    load_patches = pltpu.make_async_copy(patches_h, patches, get.at[14])
    load_patches.start()
    cube = lax.axis_index(AXES)
    info[0] = lengths[cube]
    heads = orders[:, :ROWS_E]
    mine = lax.broadcasted_iota(jnp.int32, heads.shape, 0) == cube
    places[...] = jnp.sum(jnp.where(mine, heads, 0), axis=0, keepdims=True)
    small = cast[0]
    small[...] = jnp.zeros_like(small)
    for (row, _), k in zip(SMALL_AT, range(4)):
        loads[k].wait()
        small[row : row + shards[k].shape[0], : shards[k].shape[1]] = shards[k][...].astype(BF16)
    engine.greet()
    steps = iter(range(engine.ticks))

    def advance(t):
        if t < len(chunks) and chunks[t][0] and chunks[t][0] not in [m[0] for m in chunks[:t]]:
            i = chunks[t][0]
            loads[i + 3].wait()
            cast[i][...] = shards[i + 3][...].astype(BF16)
        engine.tick(t)

    def tick():
        advance(next(steps))

    def keep(i):
        return pltpu.make_async_copy(here[i], fulls[i - 1], put.at[i - 1])

    def bring(i):
        engine.arrived(i)
        if i:
            keep(i).start()

    def mat(i):
        shape = here[i].shape
        return here[i][...].reshape(8 * Z * shape[4], shape[5])

    for _ in range(7):
        tick()
    bring(0)
    load_patches.wait()
    count = info[0]
    visible = count // 10
    slots = patches.shape[0]
    pick_s[...] = pick_matrix(places[...], visible, slots)
    x = tn(pick_s[...], patches[...])
    x_o[...] = x
    tick()
    bring(6)
    values = here[0][...].reshape(8 * Z, SMALL_ROWS, 128).astype(F32)
    for out, (row, rows) in zip((e_gains, d_gains, e_bias, d_bias), SMALL_AT):
        w = out.shape[1] // (8 * Z)
        out[...] = jnp.concatenate([values[i, row : row + rows, :w] for i in range(8 * Z)], 1)
    tick()
    bring(7)
    X = d_gains[9:10] + mat(6).T.astype(F32)
    X_o[...] = X
    hat, _ = norm_parts(X)
    h = (hat * (1.0 + d_gains[0:1]) + d_gains[1:2]).astype(BF16)
    tick()
    dW = X.shape[1]

    def three(m):
        q = (m[:, :dW] + d_gains[4:5]).astype(BF16)
        k = (m[:, dW : 2 * dW] * (HD**-0.5 * math.log2(math.e))).astype(BF16)
        return q, k, (m[:, 2 * dW :] + d_gains[5:6]).astype(BF16)

    q_o[...], k_o[...], v_o[...] = three(nn(h, mat(7)))
    spot = lax.broadcasted_iota(jnp.int32, (slots, 1), 0)
    seen = jnp.sum(pick_s[...].astype(F32), axis=1, keepdims=True)
    bias_s[...] = jnp.where((spot < count) & (seen < 0.5), 0.0, FAR_BELOW)

    def masked_keys(g, turn):
        cols = pl.ds(pl.multiple_of(g * GROUP, GROUP), GROUP)
        kg = k_o[:, cols]
        qT = q_o[:, cols].T
        vT = v_o[:, cols].T
        for j in range(4):
            if j % 2 == 0:
                turn(j // 2)
            rows = slice(HD * j, HD * (j + 1))
            s = nn(kg, head_rows(qT, j)) + bias_s[...]
            high = jnp.max(s, axis=0, keepdims=True)
            p = jnp.exp2(s - high)
            high_s[g, j : j + 1, :] = high
            sum_s[g, j : j + 1, :] = jnp.sum(p, axis=0, keepdims=True)
            oT_s[g, rows, :] = nn(vT[rows], p.astype(BF16))

    groups = dW // GROUP
    turns = [next(steps) for _ in range(2 * (groups - 1))]

    @pl.loop(0, groups - 1)
    def _(g):
        def turn(k):
            for at in range(groups - 1):

                @pl.when(g == at)
                def _():
                    advance(turns[2 * at + k])

        masked_keys(g, turn)

    bring(1)
    bring(2)
    hat, _ = norm_parts(x)
    h = (hat * (1.0 + e_gains[0:1]) + e_gains[1:2]).astype(BF16)
    W = x.shape[1]
    m = nn(h, mat(1))
    q = (m[:, :W] + e_gains[4:5]).astype(BF16)
    k = m[:, W : 2 * W].astype(BF16)
    val = (m[:, 2 * W :] + e_gains[5:6]).astype(BF16)
    m_o[...] = jnp.concatenate([q, k, val], 1)
    live = lax.broadcasted_iota(jnp.int32, (ROWS_E, ROWS_E), 1) < visible
    hs = W // HEADS_E
    outs = []
    for j in range(HEADS_E):
        sl = slice(hs * j, hs * (j + 1))
        s = jnp.where(live, nt(q[:, sl], k[:, sl]) * hs**-0.5, FAR_BELOW)
        e = jnp.exp(s - jnp.max(s, axis=-1, keepdims=True))
        p = e / jnp.sum(e, axis=-1, keepdims=True)
        p_o[j] = p
        outs.append(nn(p.astype(BF16), val[:, sl]).astype(BF16))
    o = jnp.concatenate(outs, 1)
    o_o[...] = o
    tick()
    bring(3)
    x1 = x + (nn(o, mat(2)) + e_gains[6:7])
    x1_o[...] = x1
    hat2, _ = norm_parts(x1)
    h2 = (hat2 * (1.0 + e_gains[2:3]) + e_gains[3:4]).astype(BF16)
    u, dg = gelu_parts(nn(h2, mat(3)) + e_bias[...])
    u = u.astype(BF16)
    u_o[...] = u
    dg_o[...] = dg
    masked_keys(groups - 1, lambda k: tick())
    bring(4)
    tick()
    bring(5)
    encoded = (x1 + (nn(u, mat(4)) + e_gains[7:8])).astype(BF16)
    enc_o[...] = encoded
    here_pos = nn(mat(6), pick_s[...]).T
    Xv = nn(encoded, mat(5)) + d_gains[8:9] + here_pos
    hat, _ = norm_parts(Xv)
    h = (hat * (1.0 + d_gains[0:1]) + d_gains[1:2]).astype(BF16)
    qv, kv, vv = three(nn(h, mat(7)))
    qkv_s[...] = jnp.concatenate([qv, kv, vv], 1)
    seen = jnp.sum(pick_s[...].astype(F32), axis=1, keepdims=True) > 0.5
    X_o[...] = jnp.where(seen, place_rows(pick_s[...], Xv), X_o[...])
    for i, ref in enumerate((q_o, k_o, v_o)):
        placed = nn(pick_s[...], qkv_s[:, dW * i : dW * (i + 1)]).astype(BF16)
        ref[...] = jnp.where(seen, placed, ref[...])
    tick()
    rest = list(steps)
    seen_row = nt(jnp.ones((8, ROWS_E), BF16), pick_s[...])[0:1] > 0.5
    slot = lax.broadcasted_iota(jnp.int32, (ROWS_E, 1), 0)
    slot_bias = jnp.where(slot < visible, 0.0, FAR_BELOW)
    bias = dead_bias(count, slots)

    @pl.loop(0, groups)
    def _(g):
        for at, t in enumerate(rest):

            @pl.when(g == at)
            def _():
                advance(t)

        cols = pl.ds(pl.multiple_of(g * GROUP, GROUP), GROUP)
        vcols = pl.ds(pl.multiple_of(g * GROUP + 2 * dW, GROUP), GROUP)
        kcols = pl.ds(pl.multiple_of(g * GROUP + dW, GROUP), GROUP)
        qT = q_o[:, cols].T
        kvg = qkv_s[:, kcols]
        vvT = qkv_s[:, vcols].T
        qvT = qkv_s[:, cols].T
        s = nn(k_o[:, cols], jnp.concatenate([head_rows(qvT, j) for j in range(4)], 1))
        s = jnp.concatenate([s[:SHORT], s[SHORT:] + bias], 0)
        high = jnp.max(s, axis=0, keepdims=True)
        p = jnp.exp2(s - high)
        total = jnp.sum(p, axis=0, keepdims=True)
        o = nn(v_o[:, cols].T, p.astype(BF16)) * (1.0 / total)
        L = high + jnp.log2(total)
        per_head = [slice(ROWS_E * j, ROWS_E * (j + 1)) for j in range(4)]
        ov = jnp.concatenate([o[HD * j : HD * (j + 1), per_head[j]] for j in range(4)], 0)
        oT_seen = nt(ov.astype(BF16), pick_s[...])
        terms, left = [], jnp.concatenate([L[:, sl] for sl in per_head], 0)
        for _ in range(3):
            terms.append(left.astype(BF16))
            left = left - terms[-1].astype(F32)
        L_seen = nt(jnp.concatenate(terms, 1), jnp.concatenate([pick_s[...]] * 3, 1))
        outs = []
        for j in range(4):
            rows = slice(HD * j, HD * (j + 1))
            s = nn(kvg, head_rows(qT, j)) + slot_bias
            before = high_s[g, j : j + 1, :]
            high = jnp.maximum(jnp.max(s, axis=0, keepdims=True), before)
            p = jnp.exp2(s - high)
            kept = jnp.exp2(before - high)
            total = jnp.sum(p, axis=0, keepdims=True) + sum_s[g, j : j + 1, :] * kept
            o = nn(vvT[rows], p.astype(BF16)) + oT_s[g, rows, :] * kept
            o = jnp.where(seen_row, oT_seen[rows], o * (1.0 / total))
            outs.append(o.astype(BF16))
            L = high + jnp.log2(total)
            L_o[g, j : j + 1, :] = jnp.where(seen_row, L_seen[j : j + 1], L)
        att_o[:, cols] = jnp.concatenate(outs, 0).T

    for i in range(8, n):
        bring(i)
    engine.finish()
    for i in range(1, n):
        keep(i).wait()


def front(lengths, orders, patches, small_shards, arrays, Z):
    shapes = [(SMALL_ROWS, 128)] + [a.shape for a in arrays]
    n, count = len(shapes), 8 * Z
    cuts = (1, 3, 1, 3, 3, 1, 1, 1, 1, 2, 2)
    chunks = []
    for i in (0, 6, 7, 1, 2, 3, 4, 5, 8, 9, 10):
        w = shapes[i][1] // cuts[i]
        chunks += [(i, w * t, w) for t in range(cuts[i])]
    slots, W = patches.shape
    Fw, dW, dF = shapes[3][1], shapes[5][1], shapes[9][1]
    sd = jax.ShapeDtypeStruct
    outs = [sd((2, Z, 2, 2) + s, BF16) for s in shapes[1:]]
    outs += [sd((1,), jnp.int32), sd((1, ROWS_E), jnp.int32)]
    outs += [sd((8, W), F32), sd((16, dW), F32), sd((1, Fw), F32), sd((1, dF), F32)]
    R = ROWS_E
    outs += [sd((R, W), BF16), sd((R, W), F32), sd((R, 3 * W), BF16), sd((R, W), BF16)]
    outs += [sd((R, W), F32), sd((R, Fw), BF16), sd((R, Fw), F32), sd((HEADS_E, R, R), F32)]
    outs += [sd((slots, dW), F32)] + [sd((slots, dW), BF16)] * 4
    outs += [sd((dW // GROUP, 4, slots), F32)]
    m = len(chunks)
    given = (*small_shards, *arrays)
    return pl.pallas_call(
        functools.partial(front_kernel, Z, chunks),
        out_shape=outs,
        in_specs=[S, V, A] + [A] * 14,
        out_specs=[A] * (n - 1) + [S] + [V] * 19,
        scratch_shapes=[pltpu.VMEM(a.shape, F32) for a in given]
        + [pltpu.VMEM(s, BF16) for s in shapes]
        + [pltpu.VMEM((2, Z, 2, 2) + s, BF16) for s in shapes]
        + [pltpu.VMEM((slots, W), BF16), D((15,)), D((n - 1,))]
        + [pltpu.VMEM((slots, R), BF16), pltpu.VMEM((slots, 1), F32)]
        + [pltpu.VMEM((dW // GROUP, 4, slots), F32)] * 2
        + [pltpu.VMEM((dW // GROUP, GROUP, slots), F32), pltpu.VMEM((R, 3 * dW), BF16)]
        + [D((m,)), D((m, Z - 1)), D((m, Z - 1))]
        + [D((m, 4)), D((m, 4)), D((m, 5)), D((m, 5))],
        compiler_params=pltpu.CompilerParams(
            collective_id=0, has_side_effects=True, vmem_limit_bytes=62 * 2**20
        ),
    )(lengths, orders, patches, *given)


def dec_mid_kernel(steps, FC, info, x_r, o_r, cot_r, gains, bias, proj, fc1, fc2,
                   dec_o, gx1_o, go_o, gfc2_o, gfc1_o, gproj_o, gvec_o, gbias_o, *acc):
    i = pl.program_id(0)
    n, W = x_r.shape
    Fw = fc1.shape[1]
    if steps > 1:
        afc2, afc1, aproj = acc
        @pl.when(i == 0)
        def _():
            for ref in (afc2, afc1, aproj): ref[...] = jnp.zeros_like(ref)
    @pl.when(i == 0)
    def _():
        for ref in (gvec_o, gbias_o): ref[...] = jnp.zeros_like(ref)
    live = lax.broadcasted_iota(jnp.int32, (n, 1), 0) + i * n < info[0]
    o = o_r[...]
    x1 = x_r[...] + (nn(o, proj[...]) + gains[6:7])
    hat, r = norm_parts(x1)
    h2 = (hat * (1.0 + gains[2:3]) + gains[3:4]).astype(BF16)
    G = jnp.where(live, cot_r[...].astype(F32), 0.0)
    gy = G.astype(BF16)
    def first(c):
        sl = slice(c*FC, (c+1)*FC)
        return nn(h2, fc1[:, sl]), nt(gy, fc2[sl, :])
    nc = Fw//FC
    y = None; gh2 = None
    nxt = first(0)
    for c in range(nc):
        sl = slice(c*FC, (c+1)*FC)
        z, gu = nxt
        if c+1 < nc: nxt = first(c+1)
        u, dg = gelu_parts(z + bias[:, sl])
        u = u.astype(BF16)
        gz32 = gu * dg
        gz = gz32.astype(BF16)
        yc = nn(u, fc2[sl, :])
        y = yc if y is None else y + yc
        gc = nt(gz, fc1[:, sl])
        gh2 = gc if gh2 is None else gh2 + gc
        gbias_o[:, sl] += col_sum(gz.astype(F32))
        if steps > 1:
            afc2[sl, :] += tn(u, gy)
            afc1[:, sl] += tn(h2, gz)
        else:
            gfc2_o[sl, :] = tn(u, gy).astype(BF16)
            gfc1_o[:, sl] = tn(h2, gz).astype(BF16)
    y = x1 + (y + gains[7:8])
    dec_o[...] = jnp.where(live, y, 0.0).astype(BF16)
    gvec_o[0:1, :] += col_sum(gh2 * hat)
    gvec_o[1:2, :] += col_sum(gh2)
    gx1 = G + norm_back(gh2, hat, r, gains[2:3])
    gx1_o[...] = gx1
    ga = gx1.astype(BF16)
    gvec_o[2:3, :] += col_sum(ga.astype(F32))
    gvec_o[3:4, :] += col_sum(G)
    go_o[...] = nt(ga, proj[...]).astype(BF16)
    if steps > 1:
        aproj[...] += tn(o, ga)
        @pl.when(i == steps - 1)
        def _():
            gfc2_o[...] = afc2[...].astype(BF16)
            gfc1_o[...] = afc1[...].astype(BF16)
            gproj_o[...] = aproj[...].astype(BF16)
    else:
        gproj_o[...] = tn(o, ga).astype(BF16)

def dec_mid(info, x, o, cot, gains, bias, proj, fc1, fc2, tile=1024, FC=1024):
    n, W = x.shape
    sd = jax.ShapeDtypeStruct
    full = lambda a: pl.BlockSpec(a.shape, lambda i: (0,)*a.ndim)
    row = pl.BlockSpec((tile, W), lambda i: (i, 0))
    Fw = fc1.shape[1]
    outs = (sd((n, W), BF16), sd((n, W), F32), sd((n, W), BF16), sd(fc2.shape, BF16), sd(fc1.shape, BF16), sd(proj.shape, BF16), sd((8, W), F32), sd((1, Fw), F32))
    return pl.pallas_call(functools.partial(dec_mid_kernel, n//tile, FC), grid=(n//tile,), out_shape=outs,
        in_specs=[S, row, row, row, full(gains), full(bias), full(proj), full(fc1), full(fc2)],
        out_specs=(row, row, row) + tuple(full(a) for a in outs[3:]),
        scratch_shapes=[pltpu.VMEM(w.shape, F32) for w in (fc2, fc1, proj)] if n > tile else [],
        compiler_params=params(60))(info, x, o, cot, gains, bias, proj, fc1, fc2)

def dec_post_kernel(steps, info, places, x_r, gx1_r, gq_r, gk_r, gv_r, gains, qkv, gqkv_o, gposT_o, gemb_o, gvec_o, aqkv, aemb):
    i = pl.program_id(0)
    @pl.when(i == 0)
    def _():
        for ref in (aqkv, aemb, gvec_o): ref[...] = jnp.zeros_like(ref)
    n = x_r.shape[0]
    x = x_r[...]
    hat, r = norm_parts(x)
    h = (hat * (1.0 + gains[0:1]) + gains[1:2]).astype(BF16)
    gm = jnp.concatenate([gq_r[...], gk_r[...], gv_r[...]], 1)
    W = x.shape[1]
    aqkv[...] += tn(h, gm)
    gh = nt(gm, qkv[...])
    gvec_o[0:1, :] += col_sum(gh * hat)
    gvec_o[1:2, :] += col_sum(gh)
    gvec_o[4:5, :] += col_sum(gq_r[...].astype(F32))
    gvec_o[5:6, :] += col_sum(gv_r[...].astype(F32))
    gx = gx1_r[...] + norm_back(gh, hat, r, gains[0:1])
    gxb = gx.astype(BF16)
    gposT_o[...] = gxb.T
    pos_i = lax.broadcasted_iota(jnp.int32, (n, ROWS_E), 0) + i * n
    rr = lax.broadcasted_iota(jnp.int32, (n, ROWS_E), 1)
    pick = ((pos_i == places[...]) & (rr < info[0] // 10)).astype(BF16)
    seen = jnp.sum(pick.astype(F32), axis=1, keepdims=True)
    aemb[...] += tn(pick, gxb)
    gvec_o[9:10, :] += col_sum(gx * (1.0 - seen))
    @pl.when(i == steps - 1)
    def _():
        gqkv_o[...] = aqkv[...].astype(BF16)
        gemb_o[...] = aemb[...].astype(BF16)
        gvec_o[8:9, :] = col_sum(aemb[...])

def dec_post(info, places, x, gx1, gq, gk, gv, gains, qkv, tile=1024):
    n, W = x.shape
    sd = jax.ShapeDtypeStruct
    full = lambda a: pl.BlockSpec(a.shape, lambda i: (0,)*a.ndim)
    row = pl.BlockSpec((tile, W), lambda i: (i, 0))
    outs = (sd(qkv.shape, BF16), sd((W, n), BF16), sd((ROWS_E, W), BF16), sd((16, W), F32))
    return pl.pallas_call(functools.partial(dec_post_kernel, n//tile), grid=(n//tile,), out_shape=outs,
        in_specs=[S, full(places), row, row, row, row, row, full(gains), full(qkv)],
        out_specs=(full(outs[0]), pl.BlockSpec((W, tile), lambda i: (0, i)), full(outs[2]), full(outs[3])),
        scratch_shapes=[pltpu.VMEM(qkv.shape, F32), pltpu.VMEM((ROWS_E, W), F32)],
        compiler_params=params())(info, places, x, gx1, gq, gk, gv, gains, qkv)

SPOTS = (0, 2, 4, 6, 8, 10, 12, 14, 16)


def attend_back_kernel(Z, chunks, info, q_ref, k_ref, v_ref, go_ref, o_ref, L_ref, *refs):
    blocks, (gq_ref, gk_ref, gv_ref), outs, rest = refs[:3], refs[3:6], refs[6:9], refs[9:]
    lands, rest = rest[:3], rest[3:]
    engine = Scatter(Z, take_buffers(rest[:-7], blocks, (True,) * 3, lands), chunks, rest[-7:])
    g = pl.program_id(0)

    @pl.when(g == 0)
    def _():
        engine.greet()

    q = q_ref[...]
    k = k_ref[...]
    v = v_ref[...]
    go = go_ref[...]
    bias = dead_bias(info[0], k.shape[0])
    qT, kT, goT, oT = q.T, k.T, go.T, o_ref[...].T
    inner_all = goT.astype(F32) * oT.astype(F32)
    ak = av = None
    gqs = []
    for j in range(4):
        for step in range(4):
            if 4 * step + j in SPOTS:

                @pl.when(g == step)
                def _():
                    engine.tick(SPOTS.index(4 * step + j))

        rows = slice(HD * j, HD * (j + 1))
        s = nn(k, head_rows(qT, j))
        s = jnp.concatenate([s[:SHORT], s[SHORT:] + bias], 0)
        p = jnp.exp2(s - L_ref[0, j : j + 1, :])
        gp = nn(v, head_rows(goT, j))
        inner = jnp.sum(inner_all[rows], axis=0, keepdims=True)
        gs = (p * (gp - inner)).astype(BF16)
        a = nn(p.astype(BF16), head_lanes(go, j))
        b = nn(gs, head_lanes(q, j))
        av = a if av is None else av + a
        ak = b if ak is None else ak + b
        gqs.append((nn(kT[rows], gs) * math.log(2.0)).astype(BF16))
    gq_ref[...] = jnp.concatenate(gqs, 0).T
    gk_ref[...] = (ak * HD**-0.5).astype(BF16)
    gv_ref[...] = av.astype(BF16)

    @pl.when(g == 3)
    def _():
        engine.tick(SPOTS.index(16))
        engine.finish()
        for out, land in zip(outs, lands):
            out[...] = land[...]


def attend_back(info, q, k, v, go, o, L, grads, Z):
    n, W = k.shape
    blk = pl.BlockSpec((n, GROUP), lambda g: (0, g))
    shapes = [a.shape[4:] for a in grads]
    chunks = []
    for i, (r, c) in enumerate(shapes[:2]):
        chunks += [(i, 0, c // 2), (i, c // 2, c // 2)]
    chunks.append((2, 0, shapes[2][1]))
    buffers, sems = scatter_buffers(shapes, (True,) * 3, Z, chunks)
    outs = [jax.ShapeDtypeStruct((Z, *s), BF16) for s in shapes]
    return pl.pallas_call(
        functools.partial(attend_back_kernel, Z, chunks),
        grid=(W // GROUP,),
        out_shape=[jax.ShapeDtypeStruct((n, W), BF16)] * 3 + outs,
        in_specs=[S, blk, blk, blk, blk, blk, pl.BlockSpec((1, 4, n), lambda g: (g, 0, 0))]
        + [A] * 3,
        out_specs=[blk] * 3 + [V] * 3,
        scratch_shapes=[pltpu.VMEM(a.shape, BF16) for a in outs] + buffers + sems,
        compiler_params=pltpu.CompilerParams(
            collective_id=1, has_side_effects=True, vmem_limit_bytes=60 * 2**20
        ),
    )(info, q, k, v, go, o, L, *grads)


def enc_bwd_kernel(Z, chunks, *refs):
    given, small_in, blocks_in = refs[:14], refs[14:18], refs[18:20]
    gx_o, outs, rest = refs[20], refs[21:29], refs[29:]
    local, made, rest = rest[:13], rest[13:19], rest[19:]
    e_vec, e_bias, whole, sem = rest[-11:-7]
    loaded = (True, True) + (False,) * 6
    engine = Scatter(
        Z, take_buffers(rest[:-11], (*blocks_in, *made), loaded, outs), chunks, rest[-7:]
    )
    g_embed, g_fc2, g_fc1, g_proj, g_qkv, g_small = made
    gains, mid_vec, post_vec, d_bias = small_in
    places = (*local, local[8].at[:, pl.ds(0, given[13].shape[1])])
    loads = [pltpu.make_async_copy(given[i], places[i], sem.at[i]) for i in range(14)]
    for load in loads[:13]:
        load.start()

    def got(i):
        loads[i].wait()
        return places[i][...]

    engine.greet()
    steps = iter(range(engine.ticks))

    def tick():
        engine.tick(next(steps))

    def store(ref, value):
        ref[...] = value.astype(BF16).reshape(ref.shape)

    tick()
    ge = got(0)
    store(g_embed, tn(got(1), ge))
    gy = nt(ge, got(2)).astype(BF16)
    G = gy.astype(F32)
    tick()
    u = got(3)
    store(g_fc2, tn(u, gy))
    tick()
    gz = (nt(gy, got(4)) * got(5)).astype(BF16)
    e_bias[...] = col_sum(gz.astype(F32))
    tick()
    hat2, r2 = norm_parts(got(6))
    h2 = (hat2 * (1.0 + gains[2:3]) + gains[3:4]).astype(BF16)
    store(g_fc1, tn(h2, gz))
    tick()
    gh2 = nt(gz, got(8))
    loads[13].start()
    e_vec[2:3, :] = col_sum(gh2 * hat2)
    e_vec[3:4, :] = col_sum(gh2)
    gx1 = G + norm_back(gh2, hat2, r2, gains[2:3])
    ga = gx1.astype(BF16)
    e_vec[6:7, :] = col_sum(ga.astype(F32))
    e_vec[7:8, :] = col_sum(G)
    store(g_proj, tn(got(7), ga))
    tick()
    go = nt(ga, got(9)).astype(BF16)
    for i in (10, 11, 12):
        loads[i].wait()
    m_r, p_r, x_r = places[10:13]
    W = gx1.shape[1]
    hs = W // HEADS_E
    gq, gk, gv = [], [], []
    for j in range(HEADS_E):
        q = m_r[:, hs * j : hs * (j + 1)]
        k = m_r[:, W + hs * j : W + hs * (j + 1)]
        val = m_r[:, 2 * W + hs * j : 2 * W + hs * (j + 1)]
        g = go[:, hs * j : hs * (j + 1)]
        p = p_r[j]
        gv.append(tn(p.astype(BF16), g).astype(BF16))
        gp = nt(g, val)
        gs = (p * (gp - jnp.sum(gp * p, axis=-1, keepdims=True))).astype(BF16)
        gq.append((nn(gs, k) * hs**-0.5).astype(BF16))
        gk.append((tn(gs, q) * hs**-0.5).astype(BF16))
        if j == HEADS_E // 2:
            tick()
    gm = jnp.concatenate(gq + gk + gv, 1)
    tick()
    e_vec[4:5, :] = col_sum(gm[:, :W].astype(F32))
    e_vec[5:6, :] = col_sum(gm[:, 2 * W :].astype(F32))
    hat, r = norm_parts(x_r[...])
    h = (hat * (1.0 + gains[0:1]) + gains[1:2]).astype(BF16)
    store(g_qkv, tn(h, gm))
    tick()
    gh = nt(gm, got(13))
    e_vec[0:1, :] = col_sum(gh * hat)
    e_vec[1:2, :] = col_sum(gh)
    gx_o[...] = gx1 + norm_back(gh, hat, r, gains[0:1])
    pack(g_small, e_vec, e_bias, mid_vec, post_vec, d_bias, whole)
    for t in steps:
        engine.tick(t)
    engine.finish()


def pack(out, e_vec, e_bias, mid_vec, post_vec, d_bias, whole):
    Z = out.shape[1]
    count = 8 * Z
    whole[...] = jnp.zeros_like(whole)
    whole[0:2] = post_vec[0:2]
    whole[2:4] = mid_vec[0:2]
    whole[4:6] = post_vec[4:6]
    whole[6:8] = mid_vec[2:4]
    whole[8:10] = post_vec[8:10]
    out[...] = jnp.zeros_like(out)
    for ref, row, rows in ((e_vec, 0, 8), (whole, 8, 16), (e_bias, 24, 1), (d_bias, 25, 1)):
        w = ref.shape[1] // count
        values = ref[...].astype(BF16)
        for i in range(count):
            at = (i // (4 * Z), i // 4 % Z, i // 2 % 2, i % 2)
            out[(*at, slice(row, row + rows), slice(0, w))] = values[:, w * i : w * i + w]


def enc_bwd(encoded, gemb, embed, kept, mats, small_in, blocks_in, Z):
    x, m, o, x1, u, dg, p = kept
    qkv, proj, fc1, fc2 = mats
    given = (gemb, encoded, embed, u, fc2, dg, x1, o, fc1, proj, m, p, x, qkv)
    count = 8 * Z

    def block_shape(a):
        return (a.shape[0] // count, a.shape[1])

    shapes = [a.shape[4:] for a in blocks_in]
    shapes += [block_shape(a) for a in (embed, fc2, fc1, proj, qkv)] + [(SMALL_ROWS, 128)]
    W, Fw = fc1.shape
    chunks = [(1, 0, shapes[1][1]), (0, 0, shapes[0][1]), (2, 0, shapes[2][1])]
    chunks += [(3, t * W // 3, W // 3) for t in range(3)]
    chunks += [(4, t * Fw // 4, Fw // 4) for t in range(4)]
    chunks += [(5, 0, W)] + [(6, t * W, W) for t in range(3)] + [(7, 0, 128)]
    loaded = (True, True) + (False,) * 6
    buffers, sems = scatter_buffers(shapes, loaded, Z, chunks)
    sd = jax.ShapeDtypeStruct
    return pl.pallas_call(
        functools.partial(enc_bwd_kernel, Z, chunks),
        out_shape=[sd(x.shape, F32)] + [sd((Z, *s), BF16) for s in shapes],
        in_specs=[A] * 14 + [V] * 4 + [A] * 2,
        out_specs=[V] * 9,
        scratch_shapes=[pltpu.VMEM(a.shape, a.dtype) for a in given[:13]]
        + [pltpu.VMEM((2, Z, 2, 2, *s), BF16) for s in shapes[2:]]
        + buffers
        + [pltpu.VMEM((8, W), F32), pltpu.VMEM((1, Fw), F32), pltpu.VMEM((16, embed.shape[1]), F32)]
        + [D((14,))]
        + sems,
        compiler_params=pltpu.CompilerParams(
            collective_id=2, has_side_effects=True, vmem_limit_bytes=62 * 2**20
        ),
    )(*given, *small_in, *blocks_in)


def last_kernel(n, info, places, gx, *refs):
    ins, g_patch, outs = refs[:n], refs[n], refs[n + 1 :]
    pick = pick_matrix(places[...], info[0] // 10, g_patch.shape[0])
    g_patch[...] = place_rows(pick, gx[...])

    def total(ref):
        acc = ref[0].astype(F32)
        for d in range(1, ref.shape[0]):
            acc = acc + ref[d].astype(F32)
        return acc

    small = total(ins[0])
    for out, row in zip(outs[:4], (0, 8, 24, 25)):
        out[...] = small[row : row + out.shape[0], : out.shape[1]]
    for i, ref in enumerate(ins[1:]):
        outs[4 + i][...] = total(ref)


def last_sums(info, places, gx, arrays, shapes):
    return pl.pallas_call(
        functools.partial(last_kernel, len(arrays)),
        out_shape=[jax.ShapeDtypeStruct(s, F32) for s in shapes],
        in_specs=[S] + [V] * (2 + len(arrays)),
        compiler_params=params(),
    )(info, places, gx, *arrays)


def body(
    patches,
    lengths,
    keep_order,
    e_vectors,
    e_qkv,
    e_proj,
    e_fc1,
    e_fc1_bias,
    e_fc2,
    embed,
    d_vectors,
    dec_pos,
    d_qkv,
    d_proj,
    d_fc1,
    d_fc1_bias,
    d_fc2,
    cotangent,
):
    Z = lax.axis_size("dp") // 4
    slots = patches.shape[1]
    smalls = (e_vectors, d_vectors, e_fc1_bias.reshape(1, -1), d_fc1_bias.reshape(1, -1))
    shards = (e_qkv, e_proj, e_fc1, e_fc2, embed, dec_pos.T, d_qkv, d_proj, d_fc1, d_fc2)
    made = front(lengths, keep_order, patches[0], smalls, shards, Z)
    mats = [m.reshape(-1, m.shape[-1]) for m in made[:10]]
    w_qkv, w_proj, w_fc1, w_fc2, w_embed, posT, dw_qkv, dw_proj, dw_fc1, dw_fc2 = mats
    info, places, e_gains, d_gains, e_bias, d_bias, encoded, *kept = made[10:24]
    x, q, k, v, o, L = made[24:]
    decoded, gx1, go, gd_fc2, gd_fc1, gd_proj, mid_vec, gd_bias = dec_mid(
        info, x, o, cotangent[0], d_gains, d_bias, dw_proj, dw_fc1, dw_fc2
    )

    def blocks(m):
        return m.reshape((2, Z, 2, 2, -1, m.shape[-1]))

    gq, gk, gv, *early = attend_back(
        info, q, k, v, go, o, L, [blocks(m) for m in (gd_fc2, gd_fc1, gd_proj)], Z
    )
    gd_qkv, g_posT, gemb, post_vec = dec_post(
        info, places, x, gx1, gq, gk, gv, d_gains, dw_qkv
    )
    gx, *late = enc_bwd(
        encoded,
        gemb,
        w_embed,
        kept,
        (w_qkv, w_proj, w_fc1, w_fc2),
        (e_gains, mid_vec, post_vec, gd_bias),
        (blocks(gd_qkv), blocks(g_posT)),
        Z,
    )
    pd_qkv, p_pos, p_embed, p_fc2, p_fc1, p_proj, p_qkv, p_small = late
    parts = (p_small, p_qkv, p_proj, p_fc1, p_fc2, p_embed, p_pos, pd_qkv, *early[::-1])
    shapes = [(slots, patches.shape[2])] + [m.shape for m in smalls + shards]
    g_patch, *out = last_sums(info, places, gx, parts, shapes)
    re_vec, rd_vec, re_bias, rd_bias = out[:4]
    re_qkv, re_proj, re_fc1, re_fc2, r_embed, r_pos, rd_qkv, rd_proj, rd_fc1, rd_fc2 = out[4:]
    return (
        decoded[None],
        g_patch[None],
        re_vec,
        re_qkv,
        re_proj,
        re_fc1,
        re_bias.reshape(-1),
        re_fc2,
        r_embed,
        rd_vec,
        r_pos.T,
        rd_qkv,
        rd_proj,
        rd_fc1,
        rd_bias.reshape(-1),
        rd_fc2,
    )


def solution(mesh):
    rows, columns, cubes = P(AXES, None), P(None, AXES), P(AXES, None, None)
    weights = (columns, rows, rows, rows, P(AXES), rows, rows, columns, columns)
    weights = weights + (rows, rows, rows, P(AXES), rows)
    return jax.shard_map(
        body,
        mesh=mesh,
        in_specs=(cubes, P(), P()) + weights + (cubes,),
        out_specs=(cubes, cubes) + weights,
        check_vma=False,
    )
```
